32 devices in a mesh: wide: 8 (over y, x, core), narrow: 4 (over z).
Axes of the slice: x: 2, y: 2, z: 4, core: 2. Of those that a mesh axis runs over, the one named last changes fastest.
Arguments:
- embeddings: bfloat16 [8192, 32, 192], P(('wide', 'narrow')), may hold values from -6 to 6
- upstream: bfloat16 [8192, 16, 192], P(('wide', 'narrow')), may hold values from -6 to 6
- factor_machine_projection: bfloat16 [32, 16], replicated, may hold values from -0.078125 to 0.078125
- w_first: bfloat16 [512, 2048], replicated, may hold values from -0.25 to 0.25
- w_second: bfloat16 [2048, 1536], replicated, may hold values from -0.125 to 0.125
- compress: bfloat16 [8, 32], replicated, may hold values from -1 to 1
- norm_gain: float32 [192], replicated, may hold values from 0.5 to 2
- hot_index: int32 [8192, 16], P(('wide', 'narrow')), may hold values from 0 to 127
- cold_row: int32 [8192, 16], P(('wide', 'narrow')), may hold values from 0 to 255
- cold_owner: int32 [8192, 16, 1], P(('wide', 'narrow')), may hold values from 0 to 7; in each aligned block of 4096 rows (0 to 4095, 4096 to 8191, ..., all dimensions but the last counted through in order) at most 1024 rows name the same one
Outputs:
- grad_first: float32 [512, 2048], P(('wide', 'narrow'))
- grad_second: float32 [2048, 1536], P(('wide', 'narrow'))
- grad_proj: float32 [32, 16], replicated
- compress_gradient: float32 [8, 32], replicated
- grad_gain: float32 [192], replicated
- hot_grad: float32 [16, 128, 192], replicated
- cold_grad: float32 [16, 2048, 192], P(None, 'wide')
The draws below stay inside these ranges and needn't reach their ends.
Inputs may be any that keep to these rules, and one draw needn't show every extreme that they name: `cold_owner`: within the 256 samples of one device (aligned blocks), no owner is named by more than 1024 cold lookups, a bound that some block reaches.
All inputs are finite; a program needn't handle non-finite values.
Results may differ from the reference program's by a relative error of at most 0.0066.
Values sent between devices are 32-bit elements; how exact they have to be, the bound alone decides.
No kernel may reach another device: no remote copies, remote signals or barrier semaphores. Data moves between devices by JAX's collectives and lax.ppermute only.
A program may use at most 128 MiB of HBM per device.

```python
import math
import jax
import jax.numpy as jnp
import numpy as np
from jax import lax

D = 192
HIDDEN_SIZE = 2048
RANK = 16
HOT_TABLES = 16
COLD_TABLES = 16
FM_OUT = 8
LC_OUT = 8
HOT_ROWS = 128
COLD_ROWS_DEV = 256
SAMPLES_DEV = 256
TABLES = 32
OUT_EMB = 16
OWNERS = 8
CAPACITY = 1024
COLD_ROWS = 2048
SAMPLES = 8192


def place_ends(entries, rng, low, largest):
    shape = entries.shape
    index_at = [jax.random.randint(jax.random.fold_in(rng, axis), (), 0, shape[axis]) for axis in range(len(shape))]
    entries = entries.at[tuple(index_at)].set(low)
    longest = shape.index(max(shape))
    index_at[longest] = (index_at[longest] + 1) % shape[longest]
    return entries.at[tuple(index_at)].set(largest)


def shard_levels(own_key, dims, split, smallest, largest):
    loudness, own = 1.0, jax.random.fold_in(own_key, 6)
    for dim, shards_of in split:
        heights = jnp.exp(jax.random.uniform(jax.random.fold_in(own, dim), (shards_of,), jnp.float32, smallest / len(split), largest / len(split)))
        loudness = loudness * jnp.repeat(heights, dims[dim] // shards_of).reshape([-1 if axis == dim else 1 for axis in range(len(dims))])
    return loudness


def cumulative_ranks(count, lean):
    weights = [(1 << 20) // math.isqrt(standing ** lean) + 1 for standing in range(1, count + 1)]
    scale = 1 + sum(weights) // (1 << 30)
    return np.cumsum(np.array([max(1, weight // scale) for weight in weights]))


def ranked(stream_key, extent, number_of, slope):
    table = cumulative_ranks(number_of, slope)
    lot = jax.random.randint(jax.random.fold_in(stream_key, 1), extent, 0, int(table[number_of - 1]))
    rank = jnp.searchsorted(jnp.asarray(table, jnp.int32), lot, side="right")
    return jax.random.permutation(jax.random.fold_in(stream_key, 2), number_of)[rank].astype(jnp.int32)


def deal_out(own_key, own, number, rows, amount, top, most, slope):
    order = jax.random.permutation(own_key, amount)
    heavy_load, usual = load_shares(amount, rows * top, most, slope, True), load_shares(amount, rows * top, most, slope, False)
    places = jnp.arange(amount)

    def named(lengths, rotation):
        used = int((lengths > 0).sum())
        fixed = max(1, used // 4)
        passed = fixed + (places - fixed + rotation * (used - fixed)) % max(1, amount - fixed)
        return jnp.zeros((amount,), jnp.int32).at[order[jnp.where(places < fixed, places, passed)]].set(jnp.asarray(lengths, jnp.int32))

    lengths = jnp.where(number % 4 == 0, named(heavy_load, number // 4), named(usual, number - number // 4 - 1))
    mixed = jax.random.permutation(jax.random.fold_in(own, 3), amount)
    source_of, taker = mixed[0:amount // 2 * 2:2], mixed[1:amount // 2 * 2:2]
    room = jnp.minimum(lengths[source_of] - 1, most - lengths[taker]) // 2
    room = jnp.where((source_of == order[0]) | (taker == order[0]) | (lengths[taker] == 0), 0, jnp.maximum(room, 0))
    passed = jax.random.randint(jax.random.fold_in(own, 4), (amount // 2,), 0, 1 << 20) % (room + 1)
    lengths = lengths.at[source_of].add(-passed).at[taker].add(passed)
    items = jnp.searchsorted(jnp.cumsum(lengths), jnp.arange(rows * top), side="right").astype(jnp.int32)
    listing = items.reshape(top, rows).T
    listing = listing[jax.random.permutation(jax.random.fold_in(own, 1), rows)]
    rotation = jax.random.randint(jax.random.fold_in(own, 2), (rows, 1), 0, top)
    return jnp.take_along_axis(listing, (jnp.arange(top)[None, :] + rotation) % top, axis=1)


def load_shares(count, total, bound, slope, full):
    weights = [(1 << 20) // math.isqrt(rank ** slope) + 1 for rank in range(1, count + 1)]
    largest = bound if full else min(bound, max(-(-total // count), total * weights[0] // sum(weights)))
    least = 1 if total - largest >= count - 1 else 0
    counts, rest = [largest] + [least] * (count - 1), total - largest - least * (count - 1)
    while rest > 0:
        free = [i for i in range(1, count) if counts[i] < largest] or [i for i in range(1, count) if counts[i] < bound]
        whole, budget = sum([weights[i] for i in free]), rest
        for i in free:
            addition = min(bound - counts[i], max(1, budget * weights[i] // whole), rest)
            counts[i] = counts[i] + addition
            rest = rest - addition
    return np.array(counts)


def gaussian(stream_key, dims, scale, bound, split=(), kind=jnp.bfloat16):
    drawn = scale * jax.random.normal(stream_key, dims, jnp.float32)
    if split:
        drawn = drawn * shard_levels(stream_key, dims, split, -0.22, 0.18)
    return jnp.clip(drawn, -bound, bound).astype(kind)


def setup_inputs(seed: int = 0) -> dict:
    keys = jax.random.split(jax.random.key(seed), 11)
    embeddings = gaussian(keys[0], (SAMPLES, TABLES, D), 1.0, 6.0, ((0, 32),))
    upstream = gaussian(keys[1], (SAMPLES, OUT_EMB, D), 1.0, 6.0, ((0, 32),))
    factor_machine_projection = gaussian(keys[2], (TABLES, RANK), (TABLES * D) ** -0.5, 0.078125)
    w_first = gaussian(keys[3], (TABLES * RANK, HIDDEN_SIZE), (TABLES * RANK) ** -0.5, 0.25)
    w_second = gaussian(keys[4], (HIDDEN_SIZE, FM_OUT * D), HIDDEN_SIZE ** -0.5, 0.125)
    compress = gaussian(keys[5], (LC_OUT, TABLES), TABLES ** -0.5, 1.0)
    norm_gain = jnp.clip(jnp.exp(jax.random.uniform(keys[6], (D,), jnp.float32, math.log(0.5), math.log(2.0))), 0.5, 2.0)
    hot_index = place_ends(ranked(keys[7], (SAMPLES, HOT_TABLES), HOT_ROWS, 2), jax.random.fold_in(keys[7], 3), 0, HOT_ROWS - 1).astype(jnp.int32)
    cold_row = place_ends(jax.random.randint(keys[8], (SAMPLES, COLD_TABLES), 0, COLD_ROWS_DEV), jax.random.fold_in(keys[8], 1), 0, COLD_ROWS_DEV - 1).astype(jnp.int32)
    cold_owner_keys = jax.random.split(jax.random.fold_in(keys[9], 1), SAMPLES * COLD_TABLES // (SAMPLES_DEV * COLD_TABLES))
    cold_owner_turns = jax.random.permutation(jax.random.fold_in(keys[9], 3), SAMPLES * COLD_TABLES // (SAMPLES_DEV * COLD_TABLES))
    cold_owner = jax.vmap(lambda own, number: deal_out(jax.random.fold_in(keys[9], 2), own, number, SAMPLES_DEV * COLD_TABLES, OWNERS, 1, CAPACITY, 2))(cold_owner_keys, cold_owner_turns).reshape((SAMPLES, COLD_TABLES, 1))
    return {"embeddings": embeddings, "upstream": upstream, "factor_machine_projection": factor_machine_projection, "w_first": w_first, "w_second": w_second, "compress": compress, "norm_gain": norm_gain, "hot_index": hot_index, "cold_row": cold_row, "cold_owner": cold_owner}


def silu_slope(pre_act):
    sigmoid_v = jax.nn.sigmoid(pre_act)
    return sigmoid_v * (1.0 + pre_act * (1.0 - sigmoid_v))

def block_grads(embeddings, upstream, factor_machine_projection, w_first, w_second, compress, norm_gain):
    sample_count = embeddings.shape[0]
    wide_embedding = embeddings.astype(jnp.float32)
    inner_projection = jnp.einsum('snd,nk->sdk', wide_embedding, factor_machine_projection.astype(jnp.float32)).astype(jnp.bfloat16)
    pair_terms = jnp.einsum('snd,sdk->snk', wide_embedding, inner_projection.astype(jnp.float32)).astype(jnp.bfloat16)
    flat_pairs = pair_terms.reshape(sample_count, TABLES * RANK)
    pre_act = jnp.dot(flat_pairs, w_first, preferred_element_type=jnp.float32)
    hidden = jax.nn.silu(pre_act).astype(jnp.bfloat16)
    fm_out = jnp.dot(hidden, w_second, preferred_element_type=jnp.float32).reshape(sample_count, FM_OUT, D)
    linear_compress_output = jnp.einsum('oh,jhm->jom', compress.astype(jnp.float32), wide_embedding)
    joined = jnp.concatenate([fm_out, linear_compress_output], axis=1)
    row_mean = lax.optimization_barrier(jnp.mean(joined, axis=2, keepdims=True))
    centered = joined - row_mean
    inv_std = lax.rsqrt(lax.optimization_barrier(jnp.mean(centered * centered, axis=2, keepdims=True)) + 1e-05)
    normed = centered * inv_std
    cotangent = upstream.astype(jnp.float32)
    grad_gain = lax.optimization_barrier(jnp.sum(cotangent * normed, axis=(0, 1)))
    d_norm = cotangent * norm_gain
    d_joined = (inv_std * (d_norm - lax.optimization_barrier(jnp.mean(d_norm, axis=2, keepdims=True)) - normed * lax.optimization_barrier(jnp.mean(d_norm * normed, axis=2, keepdims=True)))).astype(jnp.bfloat16)
    d_fm = d_joined[:, :FM_OUT].reshape(sample_count, FM_OUT * D)
    linear_compress_gradient = d_joined[:, FM_OUT:]
    grad_second = jnp.dot(hidden.T, d_fm, preferred_element_type=jnp.float32)
    d_pre = (jnp.dot(d_fm, w_second.T, preferred_element_type=jnp.float32) * silu_slope(pre_act)).astype(jnp.bfloat16)
    grad_first = jnp.dot(flat_pairs.T, d_pre, preferred_element_type=jnp.float32)
    pairwise_gradient = jnp.dot(d_pre, w_first.T, preferred_element_type=jnp.float32).astype(jnp.bfloat16)
    pairwise_gradient = pairwise_gradient.reshape(sample_count, TABLES, RANK).astype(jnp.float32)
    wide_compress_gradient = linear_compress_gradient.astype(jnp.float32)
    compress_gradient = jnp.einsum('ocw,ogw->cg', wide_compress_gradient, wide_embedding)
    inner_gradient = jnp.einsum('snd,snk->sdk', wide_embedding, pairwise_gradient).astype(jnp.bfloat16).astype(jnp.float32)
    grad_proj = jnp.einsum('snd,sdk->nk', wide_embedding, inner_gradient)
    embedding_gradient = jnp.einsum('ku,tkj->tuj', compress.astype(jnp.float32), wide_compress_gradient) + jnp.einsum('pcg,pog->pco', pairwise_gradient, inner_projection.astype(jnp.float32)) + jnp.einsum('jp,tzp->tjz', factor_machine_projection.astype(jnp.float32), inner_gradient)
    return (grad_first, grad_second, grad_proj, compress_gradient, grad_gain, embedding_gradient)

def reference(embeddings, upstream, factor_machine_projection, w_first, w_second, compress, norm_gain, hot_index, cold_row, cold_owner):
    blocks = SAMPLES // SAMPLES_DEV

    def scan_step(totals, block_data):
        embed_block, up_block, hot_block, row_block, owner_block = block_data
        parts = block_grads(embed_block, up_block, factor_machine_projection, w_first, w_second, compress, norm_gain)
        embedding_gradient = parts[5]
        onehot = (hot_block[:, :, None] == jnp.arange(HOT_ROWS, dtype=jnp.int32)[None, None, :]).astype(jnp.float32)
        hot_add = jnp.einsum('str,std->trd', onehot, embedding_gradient[:, :HOT_TABLES], precision=lax.Precision.HIGHEST)
        targets = (jnp.arange(COLD_TABLES, dtype=jnp.int32)[None, :] * COLD_ROWS + owner_block[:, :, 0] * COLD_ROWS_DEV + row_block).astype(jnp.int32).reshape(-1)
        cold_add = jax.ops.segment_sum(embedding_gradient[:, HOT_TABLES:].reshape(-1, D), targets, num_segments=COLD_TABLES * COLD_ROWS)
        updated = (totals[0] + parts[0], totals[1] + parts[1], totals[2] + parts[2], totals[3] + parts[3], totals[4] + parts[4], totals[5] + hot_add, totals[6] + cold_add)
        return (updated, None)
    start = (jnp.zeros((TABLES * RANK, HIDDEN_SIZE), jnp.float32), jnp.zeros((HIDDEN_SIZE, FM_OUT * D), jnp.float32), jnp.zeros((TABLES, RANK), jnp.float32), jnp.zeros((LC_OUT, TABLES), jnp.float32), jnp.zeros((D,), jnp.float32), jnp.zeros((HOT_TABLES, HOT_ROWS, D), jnp.float32), jnp.zeros((COLD_TABLES * COLD_ROWS, D), jnp.float32))
    inputs = (embeddings.reshape(blocks, SAMPLES_DEV, TABLES, D), upstream.reshape(blocks, SAMPLES_DEV, OUT_EMB, D), hot_index.reshape(blocks, SAMPLES_DEV, HOT_TABLES), cold_row.reshape(blocks, SAMPLES_DEV, COLD_TABLES), cold_owner.reshape(blocks, SAMPLES_DEV, COLD_TABLES, 1))
    totals, _ = lax.scan(scan_step, start, inputs)
    return (totals[0], totals[1], totals[2], totals[3], totals[4], totals[5], totals[6].reshape(COLD_TABLES, COLD_ROWS, D))
```

```python
import functools

import jax
import jax.numpy as jnp
from jax import lax
from jax.experimental import pallas as pl
from jax.experimental.pallas import tpu as pltpu
from jax.sharding import PartitionSpec as P

D = 192
RANK = 16
HOT_TABLES = 16
COLD_TABLES = 16
FM_OUT = 8
LC_OUT = 8
HOT_ROWS = 128
COLD_ROWS_DEV = 256
TABLES = 32
LANES = 128


def silu_slope(pre_act):
    sigmoid_v = jax.nn.sigmoid(pre_act)
    return sigmoid_v * (1.0 + pre_act * (1.0 - sigmoid_v))


def bits_of(axis):
    return (lax.axis_size(axis) - 1).bit_length()


def flip(value, axis, bit):
    return lax.ppermute(value, axis, [(i, i ^ (1 << bit)) for i in range(lax.axis_size(axis))])


def my_bit(axis, bit):
    return (lax.axis_index(axis) >> bit) & 1


def halve(value, dims, axis, bit):
    dim = dims.index((axis, bit))
    me = my_bit(axis, bit)
    send = lax.dynamic_index_in_dim(value, 1 - me, dim, keepdims=False)
    keep = lax.dynamic_index_in_dim(value, me, dim, keepdims=False)
    return keep + flip(send, axis, bit), dims[:dim] + dims[dim + 1 :]


def scatter_sum(value, dims, order):
    for axis, bit in order:
        value, dims = halve(value, dims, axis, bit)
    return value


def gather_back(value, order):
    for axis, bit in reversed(order):
        got = flip(value, axis, bit)
        me = my_bit(axis, bit)
        value = jnp.stack(
            [jnp.where(me == 0, value, got), jnp.where(me == 0, got, value)], axis=0
        )
    return value


def add_rows_kernel(blocks, rows, parts, *refs):
    ids, values, out = refs[:parts], refs[parts : 2 * parts], refs[2 * parts]
    table_ids = jnp.concatenate([r[0] for r in ids], axis=1)
    table_values = jnp.concatenate([r[0].astype(jnp.bfloat16) for r in values], axis=1)
    for b in range(blocks):
        at = lax.broadcasted_iota(jnp.int32, (rows, table_ids.shape[1]), 0) + b * rows
        onehot = (at == table_ids).astype(jnp.float32).astype(jnp.bfloat16)
        out[b, 0] = lax.dot_general(
            table_values, onehot, (((1,), (1,)), ((), ())), preferred_element_type=jnp.float32
        )


def add_rows(values, ids, blocks, rows):
    tables, depth, samples = values[0].shape
    parts = len(values)
    return pl.pallas_call(
        functools.partial(add_rows_kernel, blocks, rows, parts),
        grid=(tables,),
        in_specs=[pl.BlockSpec((1, 1, samples), lambda t: (t, 0, 0))] * parts
        + [pl.BlockSpec((1, depth, samples), lambda t: (t, 0, 0))] * parts,
        out_specs=pl.BlockSpec((blocks, 1, depth, rows), lambda t: (0, t, 0, 0)),
        out_shape=jax.ShapeDtypeStruct((blocks, tables, depth, rows), jnp.float32),
        compiler_params=pltpu.CompilerParams(vmem_limit_bytes=48 * 1024 * 1024),
        cost_estimate=pl.CostEstimate(
            flops=2 * tables * depth * samples * parts * blocks * rows,
            bytes_accessed=4 * tables * depth * (samples * parts + blocks * rows),
            transcendentals=0,
        ),
    )(*ids, *values)


def local(
    embeddings,
    upstream,
    factor_machine_projection,
    w_first,
    w_second,
    compress,
    norm_gain,
    hot_index,
    cold_row,
    cold_owner,
):
    wide, narrow = lax.axis_size("wide"), lax.axis_size("narrow")
    wide_bits = [("wide", b) for b in range(bits_of("wide"))]
    narrow_bits = [("narrow", b) for b in range(bits_of("narrow"))]
    w_dims, n_dims = wide_bits[::-1], narrow_bits[::-1]
    links = wide_bits[1:]
    order_a = wide_bits[:1] + links + narrow_bits
    order_b = wide_bits[:1] + links[::-1] + narrow_bits

    sample_count = embeddings.shape[0]
    inner_projection = jnp.einsum(
        "snd,nk->sdk", embeddings, factor_machine_projection, preferred_element_type=jnp.float32
    ).astype(jnp.bfloat16)
    pair_terms = jnp.einsum(
        "snd,sdk->snk", embeddings, inner_projection, preferred_element_type=jnp.float32
    ).astype(jnp.bfloat16)
    flat_pairs = pair_terms.reshape(sample_count, TABLES * RANK)
    pre_act = jnp.dot(flat_pairs, w_first, preferred_element_type=jnp.float32)
    hidden = jax.nn.silu(pre_act).astype(jnp.bfloat16)
    fm_out = jnp.dot(hidden, w_second, preferred_element_type=jnp.float32).reshape(
        sample_count, FM_OUT, D
    )
    linear_compress_output = jnp.einsum(
        "oh,jhm->jom", compress, embeddings, preferred_element_type=jnp.float32
    )
    joined = jnp.concatenate([fm_out, linear_compress_output], axis=1)
    row_mean = jnp.mean(joined, axis=2, keepdims=True)
    centered = joined - row_mean
    inv_std = lax.rsqrt(jnp.mean(centered * centered, axis=2, keepdims=True) + 1e-05)
    normed = centered * inv_std
    cotangent = upstream.astype(jnp.float32)
    grad_gain = jnp.sum(cotangent * normed, axis=(0, 1))
    d_norm = cotangent * norm_gain
    d_joined = (
        inv_std
        * (
            d_norm
            - jnp.mean(d_norm, axis=2, keepdims=True)
            - normed * jnp.mean(d_norm * normed, axis=2, keepdims=True)
        )
    ).astype(jnp.bfloat16)
    d_fm = d_joined[:, :FM_OUT].reshape(sample_count, FM_OUT * D)
    linear_compress_gradient = d_joined[:, FM_OUT:]
    grad_second = jnp.einsum("sh,sf->hf", hidden, d_fm, preferred_element_type=jnp.float32)
    d_pre = (
        jnp.einsum("sf,hf->sh", d_fm, w_second, preferred_element_type=jnp.float32)
        * silu_slope(pre_act)
    ).astype(jnp.bfloat16)
    grad_first = jnp.einsum("sp,sh->ph", flat_pairs, d_pre, preferred_element_type=jnp.float32)
    pairwise_gradient = jnp.einsum(
        "sh,ph->sp", d_pre, w_first, preferred_element_type=jnp.float32
    ).astype(jnp.bfloat16)
    pairwise_gradient = pairwise_gradient.reshape(sample_count, TABLES, RANK)
    inner_gradient = jnp.einsum(
        "snd,snk->sdk", embeddings, pairwise_gradient, preferred_element_type=jnp.float32
    ).astype(jnp.bfloat16)
    embedding_gradient = (
        jnp.einsum(
            "ku,tkj->tuj", compress, linear_compress_gradient, preferred_element_type=jnp.float32
        )
        + jnp.einsum(
            "pcg,pog->pco", pairwise_gradient, inner_projection, preferred_element_type=jnp.float32
        )
        + jnp.einsum(
            "jp,tzp->tjz",
            factor_machine_projection,
            inner_gradient,
            preferred_element_type=jnp.float32,
        )
    )
    by_table = jnp.transpose(embedding_gradient, (1, 2, 0))
    compress_gradient = jnp.einsum(
        "ocw,ogw->cg", linear_compress_gradient, embeddings, preferred_element_type=jnp.float32
    )
    grad_proj = jnp.einsum(
        "snd,sdk->nk", embeddings, inner_gradient, preferred_element_type=jnp.float32
    )

    share = COLD_TABLES // narrow
    cold_ids = (cold_owner[:, :, 0] * COLD_ROWS_DEV + cold_row).T.reshape(
        narrow, share, 1, sample_count
    )
    cold_values = by_table[HOT_TABLES:].reshape(narrow, share, D, sample_count)
    here = lax.axis_index("narrow")
    got_ids, got_values = [], []
    for step in range(narrow):
        target = (here + step) % narrow
        ids = lax.dynamic_index_in_dim(cold_ids, target, 0, keepdims=False)
        values = lax.dynamic_index_in_dim(cold_values, target, 0, keepdims=False)
        if step:
            ring = [(i, (i + step) % narrow) for i in range(narrow)]
            ids, values = lax.ppermute(ids, "narrow", ring), lax.ppermute(values, "narrow", ring)
        got_ids.append(ids)
        got_values.append(values)
    cold_dense = add_rows(got_values, got_ids, wide, COLD_ROWS_DEV)
    half = share // 2
    cold_dense = cold_dense.reshape([2] * len(w_dims) + [2, half, D, COLD_ROWS_DEV])
    lead = (slice(None),) * len(w_dims)
    cold_pieces = []
    for piece, order in ((0, order_a), (1, order_b)):
        value = scatter_sum(cold_dense[lead + (piece,)], w_dims, order[: len(w_dims)])
        cold_pieces.append(value)
    cold_mine = jnp.concatenate(cold_pieces, axis=0)
    cold_grad = jnp.zeros((narrow, share, D, COLD_ROWS_DEV), jnp.float32)
    ring = [(i, (i + 1) % narrow) for i in range(narrow)]
    value = cold_mine
    for step in range(narrow):
        if step:
            value = lax.ppermute(value, "narrow", ring)
        cold_grad = lax.dynamic_update_index_in_dim(
            cold_grad, value, (here - step) % narrow, 0
        )
    cold_grad = jnp.transpose(
        cold_grad.reshape(COLD_TABLES, D, COLD_ROWS_DEV), (0, 2, 1)
    )

    dims = w_dims + n_dims
    devices = wide * narrow

    def reduce_matrix(matrix):
        rows, columns = matrix.shape
        own = rows // devices
        if own % 16:
            whole = matrix.reshape([2] * len(dims) + [own, columns])
            return scatter_sum(whole, dims, order_a)
        pieces = matrix.reshape([2] * len(dims) + [2, own // 2, columns])
        lead = (slice(None),) * len(dims)
        done = [
            scatter_sum(pieces[lead + (piece,)], dims, order)
            for piece, order in ((0, order_a), (1, order_b))
        ]
        return jnp.concatenate(done, axis=0)

    grad_second = reduce_matrix(grad_second)
    grad_first = reduce_matrix(grad_first)

    hot_local = add_rows(
        [by_table[:HOT_TABLES]], [hot_index.T.reshape(HOT_TABLES, 1, sample_count)], 1, HOT_ROWS
    )
    hot_rows = hot_local.size // LANES
    small = jnp.concatenate([grad_proj.reshape(-1), compress_gradient.reshape(-1), grad_gain])
    small = jnp.pad(small, (0, -small.size % LANES)).reshape(-1, LANES)
    shared = jnp.concatenate([hot_local.reshape(hot_rows, LANES), small], axis=0)
    shared = jnp.pad(shared, ((0, -shared.shape[0] % (8 * devices)), (0, 0)))
    order = order_a
    shared = shared.reshape([2] * len(dims) + [-1, LANES])
    mine = scatter_sum(shared, order, order)
    shared = gather_back(mine, order).reshape(-1, LANES)
    hot_grad = jnp.transpose(shared[:hot_rows].reshape(HOT_TABLES, D, HOT_ROWS), (0, 2, 1))
    small = shared[hot_rows:].reshape(-1)
    n_proj, n_compress = TABLES * RANK, LC_OUT * TABLES
    grad_proj = small[:n_proj].reshape(TABLES, RANK)
    compress_gradient = small[n_proj : n_proj + n_compress].reshape(LC_OUT, TABLES)
    grad_gain = small[n_proj + n_compress : n_proj + n_compress + D]
    return (grad_first, grad_second, grad_proj, compress_gradient, grad_gain, hot_grad, cold_grad)


def solution(mesh):
    placed = (
        P(("wide", "narrow"), None, None),
        P(("wide", "narrow"), None, None),
        P(),
        P(),
        P(),
        P(),
        P(),
        P(("wide", "narrow"), None),
        P(("wide", "narrow"), None),
        P(("wide", "narrow"), None, None),
    )
    return jax.shard_map(
        local,
        mesh=mesh,
        in_specs=placed,
        out_specs=(
            P(("wide", "narrow"), None),
            P(("wide", "narrow"), None),
            P(),
            P(),
            P(),
            P(),
            P(None, "wide", None),
        ),
        check_vma=False,
    )
```

```python
import functools

import jax
import jax.numpy as jnp
from jax import lax
from jax.experimental import pallas as pl
from jax.experimental.pallas import tpu as pltpu
from jax.sharding import PartitionSpec as P

D = 192
RANK = 16
HOT_TABLES = 16
COLD_TABLES = 16
FM_OUT = 8
LC_OUT = 8
HOT_ROWS = 128
COLD_ROWS_DEV = 256
TABLES = 32
LANES = 128


NT = (((1,), (1,)), ((), ()))
NN = (((1,), (0,)), ((), ()))
GROUP = 16
OCTET = 8
VMEM = 60 * 1024 * 1024


def mm(a, b, dims=NN):
    return lax.dot_general(a, b, dims, preferred_element_type=jnp.float32)


def iota(shape, dim):
    return lax.broadcasted_iota(jnp.int32, shape, dim)


def ones_where(mask):
    return mask.astype(jnp.float32).astype(jnp.bfloat16)


def eye(size):
    return ones_where(iota((size, size), 0) == iota((size, size), 1))


def same_sample(rows, columns):
    return ones_where(
        lax.rem(iota((rows, columns), 0), GROUP) == lax.rem(iota((rows, columns), 1), GROUP)
    )


def spread_rows(count):
    return ones_where(
        lax.div(iota((count * GROUP, count), 0), GROUP) == iota((count * GROUP, count), 1)
    )


def spread_columns(count):
    return ones_where(
        lax.div(iota((count, count * GROUP), 1), GROUP) == iota((count, count * GROUP), 0)
    )


def expand(matrix):
    rows, columns = matrix.shape
    tall = mm(spread_rows(rows), matrix).astype(jnp.bfloat16)
    full = mm(tall, spread_columns(columns)).astype(jnp.bfloat16)
    return full * same_sample(rows * GROUP, columns * GROUP)


def expand_t(matrix):
    rows, columns = matrix.shape
    tall = mm(spread_rows(columns), matrix, NT).astype(jnp.bfloat16)
    full = mm(tall, spread_columns(rows)).astype(jnp.bfloat16)
    return full * same_sample(columns * GROUP, rows * GROUP)


def pick_rank():
    shape = (RANK * GROUP, OCTET * RANK)
    return ones_where(lax.div(iota(shape, 0), GROUP) == lax.rem(iota(shape, 1), RANK))


def same_table():
    shape = (OCTET * GROUP, OCTET * RANK)
    return ones_where(lax.div(iota(shape, 0), GROUP) == lax.div(iota(shape, 1), RANK))


def mlp_kernel(
    core,
    x,
    up,
    proj,
    w_first,
    w_second,
    comp,
    gain,
    second_keep,
    second_send,
    first_keep,
    first_send,
    xs,
    inner,
    d_pair,
    d_lc,
    grad_gain,
    flat,
    flat_t,
    hidden,
    hidden_t,
    slope,
    lc_out,
    d_fm,
    d_pre,
):
    step = pl.program_id(0)
    samples = x.shape[2]
    hidden_size = w_first.shape[1]
    groups = samples // GROUP

    @pl.when(step == 0)
    def _():
        unit = eye(samples)
        for n in range(TABLES):
            xs[n] = mm(unit, x[n], NT).astype(jnp.bfloat16)
        comp_rows = expand(comp[...])
        for b in range(D // GROUP):
            block = x[:, GROUP * b : GROUP * (b + 1), :].reshape(TABLES * GROUP, samples)
            lc_out[:, GROUP * b : GROUP * (b + 1), :] = mm(comp_rows, block).reshape(
                LC_OUT, GROUP, samples
            )
        proj_t = expand_t(proj[...])
        samples_match = same_sample(TABLES * GROUP, RANK * GROUP).astype(jnp.float32)
        rank_of = pick_rank()
        table_match = same_table().astype(jnp.float32)

        def group(g, carry):
            rows = pl.ds(pl.multiple_of(g * GROUP, GROUP), GROUP)
            xg = xs[:, rows, :].reshape(TABLES * GROUP, D)
            inner_g = mm(proj_t, xg).astype(jnp.bfloat16)
            inner[:, rows, :] = inner_g.reshape(RANK, GROUP, D)
            pair = (mm(xg, inner_g, NT) * samples_match).astype(jnp.bfloat16)
            for j in range(TABLES // OCTET):
                part = pair[OCTET * GROUP * j : OCTET * GROUP * (j + 1)]
                wide_part = mm(part, rank_of) * table_match
                flat[rows, OCTET * RANK * j : OCTET * RANK * (j + 1)] = jnp.sum(
                    wide_part.reshape(OCTET, GROUP, OCTET * RANK), axis=0
                ).astype(jnp.bfloat16)
            return carry

        lax.fori_loop(0, groups, group, 0)
        pairs = flat.shape[1]
        block = 256
        unit_b = eye(block)
        for b in range(pairs // block):
            at = slice(block * b, block * (b + 1))
            flat_t[at] = mm(unit_b, flat[:, at], NT).astype(jnp.bfloat16)
        for b in range(hidden_size // block):
            at = slice(block * b, block * (b + 1))
            pre = mm(flat[...], w_first[:, at])
            sigmoid_v = 1.0 / (1.0 + jnp.exp(-pre))
            slope[:, at] = sigmoid_v * (1.0 + pre * (1.0 - sigmoid_v))
            hidden_b = (pre * sigmoid_v).astype(jnp.bfloat16)
            hidden[:, at] = hidden_b
            hidden_t[at] = mm(unit_b, hidden_b, NT).astype(jnp.bfloat16)
        gain_column = jnp.sum(
            jnp.where(iota((D, D), 0) == iota((D, D), 1), gain[...], 0.0), axis=1, keepdims=True
        )
        scale = 1.0 / D
        gain_sum = jnp.zeros((D, samples), jnp.float32)

        def norm(joined, o, gain_sum):
            mean = jnp.sum(joined, axis=0, keepdims=True) * scale
            centered = joined - mean
            variance = jnp.sum(centered * centered, axis=0, keepdims=True) * scale
            inv_std = lax.rsqrt(variance + 1e-05)
            normed = centered * inv_std
            cotangent = up[o].astype(jnp.float32)
            gain_sum = gain_sum + cotangent * normed
            d_norm = cotangent * gain_column
            mean_d = jnp.sum(d_norm, axis=0, keepdims=True) * scale
            mean_n = jnp.sum(d_norm * normed, axis=0, keepdims=True) * scale
            return (inv_std * (d_norm - mean_d - normed * mean_n)).astype(jnp.bfloat16), gain_sum

        for c in range(FM_OUT // 2):
            at = slice(2 * D * c, 2 * D * (c + 1))
            fm_t = mm(hidden[...], w_second[:, at]).T
            low, gain_sum = norm(fm_t[:D], 2 * c, gain_sum)
            high, gain_sum = norm(fm_t[D:], 2 * c + 1, gain_sum)
            both = jnp.concatenate([low, high], axis=0)
            d_fm[:, at] = mm(unit, both, NT).astype(jnp.bfloat16)
        for o in range(LC_OUT):
            d_joined, gain_sum = norm(lc_out[o], FM_OUT + o, gain_sum)
            d_lc[o] = mm(unit, d_joined, NT).astype(jnp.bfloat16)
        gain_row = jnp.sum(gain_sum, axis=1, keepdims=True)
        grad_gain[...] = jnp.broadcast_to(gain_row, grad_gain.shape)
        for b in range(hidden_size // block):
            at = slice(block * b, block * (b + 1))
            d_pre[:, at] = (mm(d_fm[...], w_second[at], NT) * slope[:, at]).astype(jnp.bfloat16)
        d_pair[...] = mm(d_pre[...], w_first[...], NT).astype(jnp.bfloat16)

    mine = core[0]
    second_rows, first_rows = second_keep.shape[1], first_keep.shape[1]
    for which, second, first in ((mine, second_keep, first_keep), (1 - mine, second_send, first_send)):
        w = 2 * step + which
        rows = pl.ds(pl.multiple_of(w * second_rows, second_rows), second_rows)
        second[0] = mm(hidden_t[rows], d_fm[...])
        rows = pl.ds(pl.multiple_of(w * first_rows, first_rows), first_rows)
        first[0] = mm(flat_t[rows], d_pre[...])


def whole(shape):
    zeros = (0,) * len(shape)
    return pl.BlockSpec(shape, lambda j, c: zeros, pipeline_mode=pl.Buffered(1))


def mlp(core, x, up, proj, w_first, w_second, comp, gain, wide):
    samples = x.shape[2]
    pairs, hidden_size = w_first.shape
    outs = w_second.shape[1]
    half, second_rows, first_rows = wide // 2, hidden_size // wide, pairs // wide
    second = jax.ShapeDtypeStruct((half, second_rows, outs), jnp.float32)
    first = jax.ShapeDtypeStruct((half, first_rows, hidden_size), jnp.float32)
    rest = [
        jax.ShapeDtypeStruct((TABLES, samples, D), jnp.bfloat16),
        jax.ShapeDtypeStruct((RANK, samples, D), jnp.bfloat16),
        jax.ShapeDtypeStruct((samples, pairs), jnp.bfloat16),
        jax.ShapeDtypeStruct((LC_OUT, samples, D), jnp.bfloat16),
        jax.ShapeDtypeStruct((D, LANES), jnp.float32),
    ]

    def by_step(shape):
        return pl.BlockSpec((1,) + shape.shape[1:], lambda j, c: (j, 0, 0))

    bf16, f32 = jnp.bfloat16, jnp.float32
    return pl.pallas_call(
        mlp_kernel,
        grid_spec=pltpu.PrefetchScalarGridSpec(
            num_scalar_prefetch=1,
            grid=(half,),
            in_specs=[whole(a.shape) for a in (x, up, proj, w_first, w_second, comp, gain)],
            out_specs=[by_step(second)] * 2 + [by_step(first)] * 2 + [whole(r.shape) for r in rest],
            scratch_shapes=[
                pltpu.VMEM((samples, pairs), bf16),
                pltpu.VMEM((pairs, samples), bf16),
                pltpu.VMEM((samples, hidden_size), bf16),
                pltpu.VMEM((hidden_size, samples), bf16),
                pltpu.VMEM((samples, hidden_size), f32),
                pltpu.VMEM((LC_OUT, D, samples), f32),
                pltpu.VMEM((samples, outs), bf16),
                pltpu.VMEM((samples, hidden_size), bf16),
            ],
        ),
        out_shape=[second, second, first, first] + rest,
        compiler_params=pltpu.CompilerParams(vmem_limit_bytes=VMEM),
        cost_estimate=pl.CostEstimate(
            flops=16_000_000_000, bytes_accessed=32_000_000, transcendentals=600_000
        ),
    )(core, x, up, proj, w_first, w_second, comp, gain)


def rows_kernel(
    narrow, here, xs, inner, d_pair, d_lc, proj, comp, hot_ids, *refs
):
    colds, (hot, sums, d_rows, totals) = refs[:narrow], refs[narrow:]
    samples = xs.shape[1]
    share = COLD_TABLES // narrow
    proj_rows, comp_rows = expand(proj[...]), expand_t(comp[...])
    match = same_sample(OCTET * GROUP, RANK * GROUP)
    match_t = same_sample(RANK * GROUP, OCTET * GROUP)
    rank_of, table_match = pick_rank(), same_table()
    totals[...] = jnp.zeros_like(totals)

    def group(g, carry):
        rows = pl.ds(pl.multiple_of(g * GROUP, GROUP), GROUP)
        xg = xs[:, rows, :].reshape(TABLES * GROUP, D)
        inner_g = inner[:, rows, :].reshape(RANK * GROUP, D)
        d_lc_g = d_lc[:, rows, :].reshape(LC_OUT * GROUP, D)
        parts, parts_t = [], []
        for j in range(TABLES // OCTET):
            own = d_pair[rows, OCTET * RANK * j : OCTET * RANK * (j + 1)]
            spread = jnp.concatenate([own] * OCTET, axis=0) * table_match
            parts.append(mm(spread, rank_of, NT).astype(jnp.bfloat16) * match)
            parts_t.append(mm(rank_of, spread, NT).astype(jnp.bfloat16) * match_t)
        d_pairs = jnp.concatenate(parts, axis=0)
        d_pairs_t = jnp.concatenate(parts_t, axis=1)
        d_inner = mm(d_pairs_t, xg).astype(jnp.bfloat16)
        d_embed = mm(d_pairs, inner_g) + mm(proj_rows, d_inner) + mm(comp_rows, d_lc_g)
        d_rows[:, rows, :] = d_embed.astype(jnp.bfloat16).reshape(TABLES, GROUP, D)
        totals[...] += mm(jnp.concatenate([d_inner, d_lc_g], axis=0), xg, NT)
        return carry

    lax.fori_loop(0, samples // GROUP, group, 0)
    unit = eye(D)
    for step in range(narrow):
        target = lax.rem(here[0] + step, narrow)
        for i in range(share):
            colds[step][i] = mm(unit, d_rows[HOT_TABLES + target * share + i], NT)
    for t in range(HOT_TABLES):
        values = mm(unit, d_rows[t], NT).astype(jnp.bfloat16)
        onehot = ones_where(iota((HOT_ROWS, samples), 0) == hot_ids[t : t + 1, :])
        hot[t] = mm(values, onehot, NT)
    sums_shape = totals.shape
    own = lax.rem(iota(sums_shape, 0), GROUP) == lax.rem(iota(sums_shape, 1), GROUP)
    masked = jnp.where(own, totals[...], 0.0)
    folded = jnp.sum(masked.reshape(RANK + LC_OUT, GROUP, sums_shape[1]), axis=1)
    sums[...] = lax.dot_general(
        folded,
        spread_rows(TABLES).astype(jnp.float32),
        NN,
        precision=lax.Precision.HIGHEST,
        preferred_element_type=jnp.float32,
    )


def row_gradients(here, xs, inner, d_pair, d_lc, proj, comp, hot_ids, narrow):
    samples = xs.shape[1]
    share = COLD_TABLES // narrow
    vmem = pl.BlockSpec(memory_space=pltpu.VMEM)
    return pl.pallas_call(
        functools.partial(rows_kernel, narrow),
        in_specs=[pl.BlockSpec(memory_space=pltpu.SMEM)] + [vmem] * 7,
        out_specs=[vmem] * (narrow + 2),
        out_shape=[jax.ShapeDtypeStruct((share, D, samples), jnp.float32)] * narrow
        + [
            jax.ShapeDtypeStruct((HOT_TABLES, D, HOT_ROWS), jnp.float32),
            jax.ShapeDtypeStruct((RANK + LC_OUT, TABLES), jnp.float32),
        ],
        scratch_shapes=[
            pltpu.VMEM((TABLES, samples, D), jnp.bfloat16),
            pltpu.VMEM(((RANK + LC_OUT) * GROUP, TABLES * GROUP), jnp.float32),
        ],
        compiler_params=pltpu.CompilerParams(vmem_limit_bytes=VMEM),
        cost_estimate=pl.CostEstimate(
            flops=8_000_000_000, bytes_accessed=12_000_000, transcendentals=0
        ),
    )(here, xs, inner, d_pair, d_lc, proj, comp, hot_ids)


def bits_of(axis):
    return (lax.axis_size(axis) - 1).bit_length()


def flip(value, axis, bit):
    return lax.ppermute(value, axis, [(i, i ^ (1 << bit)) for i in range(lax.axis_size(axis))])


def my_bit(axis, bit):
    return (lax.axis_index(axis) >> bit) & 1


def halve(value, dims, axis, bit):
    dim = dims.index((axis, bit))
    me = my_bit(axis, bit)
    send = lax.dynamic_index_in_dim(value, 1 - me, dim, keepdims=False)
    keep = lax.dynamic_index_in_dim(value, me, dim, keepdims=False)
    return keep + flip(send, axis, bit), dims[:dim] + dims[dim + 1 :]


def scatter_sum(value, dims, order):
    for axis, bit in order:
        value, dims = halve(value, dims, axis, bit)
    return value


def gather_back(value, order):
    for axis, bit in reversed(order):
        got = flip(value, axis, bit)
        me = my_bit(axis, bit)
        value = jnp.stack(
            [jnp.where(me == 0, value, got), jnp.where(me == 0, got, value)], axis=0
        )
    return value


def add_rows_kernel(blocks, rows, parts, *refs):
    ids, values, out = refs[:parts], refs[parts : 2 * parts], refs[2 * parts]
    table_ids = jnp.concatenate([r[0] for r in ids], axis=1)
    table_values = jnp.concatenate([r[0].astype(jnp.bfloat16) for r in values], axis=1)
    for b in range(blocks):
        at = lax.broadcasted_iota(jnp.int32, (rows, table_ids.shape[1]), 0) + b * rows
        onehot = (at == table_ids).astype(jnp.float32).astype(jnp.bfloat16)
        out[b, 0] = lax.dot_general(
            table_values, onehot, (((1,), (1,)), ((), ())), preferred_element_type=jnp.float32
        )


def add_rows(values, ids, blocks, rows):
    tables, depth, samples = values[0].shape
    parts = len(values)
    return pl.pallas_call(
        functools.partial(add_rows_kernel, blocks, rows, parts),
        grid=(tables,),
        in_specs=[pl.BlockSpec((1, 1, samples), lambda t: (t, 0, 0))] * parts
        + [pl.BlockSpec((1, depth, samples), lambda t: (t, 0, 0))] * parts,
        out_specs=pl.BlockSpec((blocks, 1, depth, rows), lambda t: (0, t, 0, 0)),
        out_shape=jax.ShapeDtypeStruct((blocks, tables, depth, rows), jnp.float32),
        compiler_params=pltpu.CompilerParams(vmem_limit_bytes=48 * 1024 * 1024),
        cost_estimate=pl.CostEstimate(
            flops=2 * tables * depth * samples * parts * blocks * rows,
            bytes_accessed=4 * tables * depth * (samples * parts + blocks * rows),
            transcendentals=0,
        ),
    )(*ids, *values)


def local(
    embeddings,
    upstream,
    factor_machine_projection,
    w_first,
    w_second,
    compress,
    norm_gain,
    hot_index,
    cold_row,
    cold_owner,
):
    wide, narrow = lax.axis_size("wide"), lax.axis_size("narrow")
    wide_bits = [("wide", b) for b in range(bits_of("wide"))]
    narrow_bits = [("narrow", b) for b in range(bits_of("narrow"))]
    w_dims, n_dims = wide_bits[::-1], narrow_bits[::-1]
    links = wide_bits[1:]
    order_a = wide_bits[:1] + links + narrow_bits
    order_b = wide_bits[:1] + links[::-1] + narrow_bits

    sample_count = embeddings.shape[0]
    here = lax.axis_index("narrow")
    x = jnp.transpose(embeddings, (1, 2, 0))
    up = jnp.transpose(upstream, (1, 2, 0))
    core = my_bit("wide", 0).reshape(1)
    second_keep, second_send, first_keep, first_send, xs, inner, d_pair, d_lc, gain_sum = mlp(
        core,
        x,
        up,
        factor_machine_projection,
        w_first,
        w_second,
        compress,
        norm_gain.reshape(1, D),
        wide,
    )
    *cold_values, hot_local, sums = row_gradients(
        here.reshape(1),
        xs,
        inner,
        d_pair,
        d_lc,
        factor_machine_projection,
        compress,
        hot_index.T,
        narrow,
    )
    grad_gain = gain_sum[:, 0]
    grad_proj, compress_gradient = sums[:RANK].T, sums[RANK:]

    share = COLD_TABLES // narrow
    cold_ids = (cold_owner[:, :, 0] * COLD_ROWS_DEV + cold_row).T.reshape(
        narrow, share, 1, sample_count
    )
    got_ids, got_values = [], []
    for step in range(narrow):
        target = (here + step) % narrow
        ids = lax.dynamic_index_in_dim(cold_ids, target, 0, keepdims=False)
        values = cold_values[step]
        if step:
            ring = [(i, (i + step) % narrow) for i in range(narrow)]
            ids, values = lax.ppermute(ids, "narrow", ring), lax.ppermute(values, "narrow", ring)
        got_ids.append(ids)
        got_values.append(values)
    cold_dense = add_rows(got_values, got_ids, wide, COLD_ROWS_DEV)
    half = share // 2
    cold_dense = cold_dense.reshape([2] * len(w_dims) + [2, half, D, COLD_ROWS_DEV])
    lead = (slice(None),) * len(w_dims)
    cold_pieces = []
    for piece, order in ((0, order_a), (1, order_b)):
        value = scatter_sum(cold_dense[lead + (piece,)], w_dims, order[: len(w_dims)])
        cold_pieces.append(value)
    cold_mine = jnp.concatenate(cold_pieces, axis=0)
    cold_grad = jnp.zeros((narrow, share, D, COLD_ROWS_DEV), jnp.float32)
    ring = [(i, (i + 1) % narrow) for i in range(narrow)]
    value = cold_mine
    for step in range(narrow):
        if step:
            value = lax.ppermute(value, "narrow", ring)
        cold_grad = lax.dynamic_update_index_in_dim(
            cold_grad, value, (here - step) % narrow, 0
        )
    cold_grad = jnp.transpose(
        cold_grad.reshape(COLD_TABLES, D, COLD_ROWS_DEV), (0, 2, 1)
    )

    dims = w_dims + n_dims
    devices = wide * narrow

    def reduce_matrix(keep, send):
        got = flip(send, "wide", 0)
        own, columns = keep.shape[1] // narrow, keep.shape[2]
        left = dims[: len(w_dims) - 1] + n_dims
        if own % 16:
            pieces = [(slice(None), order_a)]
        else:
            pieces = [(slice(0, own // 2), order_a), (slice(own // 2, own), order_b)]
        done = []
        for rows, order in pieces:
            lead = (slice(None),) * len(left)
            size = [2] * len(left) + [own, columns]
            value = keep.reshape(size)[lead + (rows,)] + got.reshape(size)[lead + (rows,)]
            done.append(scatter_sum(value, left, order[1:]))
        return jnp.concatenate(done, axis=0)

    grad_second = reduce_matrix(second_keep, second_send)
    grad_first = reduce_matrix(first_keep, first_send)

    hot_rows = hot_local.size // LANES
    small = jnp.concatenate([grad_proj.reshape(-1), compress_gradient.reshape(-1), grad_gain])
    small = jnp.pad(small, (0, -small.size % LANES)).reshape(-1, LANES)
    shared = jnp.concatenate([hot_local.reshape(hot_rows, LANES), small], axis=0)
    shared = jnp.pad(shared, ((0, -shared.shape[0] % (8 * devices)), (0, 0)))
    order = order_a
    shared = shared.reshape([2] * len(dims) + [-1, LANES])
    mine = scatter_sum(shared, order, order)
    shared = gather_back(mine, order).reshape(-1, LANES)
    hot_grad = jnp.transpose(shared[:hot_rows].reshape(HOT_TABLES, D, HOT_ROWS), (0, 2, 1))
    small = shared[hot_rows:].reshape(-1)
    n_proj, n_compress = TABLES * RANK, LC_OUT * TABLES
    grad_proj = small[:n_proj].reshape(TABLES, RANK)
    compress_gradient = small[n_proj : n_proj + n_compress].reshape(LC_OUT, TABLES)
    grad_gain = small[n_proj + n_compress : n_proj + n_compress + D]
    return (grad_first, grad_second, grad_proj, compress_gradient, grad_gain, hot_grad, cold_grad)


def solution(mesh):
    placed = (
        P(("wide", "narrow"), None, None),
        P(("wide", "narrow"), None, None),
        P(),
        P(),
        P(),
        P(),
        P(),
        P(("wide", "narrow"), None),
        P(("wide", "narrow"), None),
        P(("wide", "narrow"), None, None),
    )
    return jax.shard_map(
        local,
        mesh=mesh,
        in_specs=placed,
        out_specs=(
            P(("wide", "narrow"), None),
            P(("wide", "narrow"), None),
            P(),
            P(),
            P(),
            P(),
            P(None, "wide", None),
        ),
        check_vma=False,
    )
```

```python
import functools

import jax
import jax.numpy as jnp
from jax import lax
from jax.experimental import pallas as pl
from jax.experimental.pallas import tpu as pltpu
from jax.sharding import PartitionSpec as P

D = 192
RANK = 16
HOT_TABLES = 16
COLD_TABLES = 16
FM_OUT = 8
LC_OUT = 8
HOT_ROWS = 128
COLD_ROWS_DEV = 256
TABLES = 32
LANES = 128
COLUMNS = 512
ID_ROWS = 8


NT = (((1,), (1,)), ((), ()))
NN = (((1,), (0,)), ((), ()))
GROUP = 16
OCTET = 8
VMEM = 60 * 1024 * 1024


def mm(a, b, dims=NN):
    return lax.dot_general(a, b, dims, preferred_element_type=jnp.float32)


def iota(shape, dim):
    return lax.broadcasted_iota(jnp.int32, shape, dim)


def ones_where(mask):
    return mask.astype(jnp.float32).astype(jnp.bfloat16)


def eye(size):
    return ones_where(iota((size, size), 0) == iota((size, size), 1))


def same_sample(rows, columns):
    return ones_where(
        lax.rem(iota((rows, columns), 0), GROUP) == lax.rem(iota((rows, columns), 1), GROUP)
    )


def spread_rows(count):
    return ones_where(
        lax.div(iota((count * GROUP, count), 0), GROUP) == iota((count * GROUP, count), 1)
    )


def spread_columns(count):
    return ones_where(
        lax.div(iota((count, count * GROUP), 1), GROUP) == iota((count, count * GROUP), 0)
    )


def expand(matrix):
    rows, columns = matrix.shape
    tall = mm(spread_rows(rows), matrix).astype(jnp.bfloat16)
    full = mm(tall, spread_columns(columns)).astype(jnp.bfloat16)
    return full * same_sample(rows * GROUP, columns * GROUP)


def expand_t(matrix):
    rows, columns = matrix.shape
    tall = mm(spread_rows(columns), matrix, NT).astype(jnp.bfloat16)
    full = mm(tall, spread_columns(rows)).astype(jnp.bfloat16)
    return full * same_sample(columns * GROUP, rows * GROUP)


def pick_rank():
    shape = (RANK * GROUP, OCTET * RANK)
    return ones_where(lax.div(iota(shape, 0), GROUP) == lax.rem(iota(shape, 1), RANK))


def same_table():
    shape = (OCTET * GROUP, OCTET * RANK)
    return ones_where(lax.div(iota(shape, 0), GROUP) == lax.div(iota(shape, 1), RANK))


def mlp_kernel(
    wide,
    core,
    x,
    up,
    proj,
    w_first,
    w_second,
    comp,
    gain,
    keep,
    send,
    xs,
    inner,
    d_pair,
    d_lc,
    grad_gain,
    flat,
    flat_t,
    hidden,
    hidden_t,
    slope,
    lc_out,
    d_fm,
    d_pre,
):
    step = pl.program_id(0)
    samples = x.shape[2]
    hidden_size = w_first.shape[1]
    groups = samples // GROUP

    @pl.when(step == 0)
    def _():
        unit = eye(samples)
        for n in range(TABLES):
            xs[n] = mm(unit, x[n], NT).astype(jnp.bfloat16)
        comp_rows = expand(comp[...])
        for b in range(D // GROUP):
            block = x[:, GROUP * b : GROUP * (b + 1), :].reshape(TABLES * GROUP, samples)
            lc_out[:, GROUP * b : GROUP * (b + 1), :] = mm(comp_rows, block).reshape(
                LC_OUT, GROUP, samples
            )
        proj_t = expand_t(proj[...])
        samples_match = same_sample(TABLES * GROUP, RANK * GROUP).astype(jnp.float32)
        rank_of = pick_rank()
        table_match = same_table().astype(jnp.float32)

        def group(g, carry):
            rows = pl.ds(pl.multiple_of(g * GROUP, GROUP), GROUP)
            xg = xs[:, rows, :].reshape(TABLES * GROUP, D)
            inner_g = mm(proj_t, xg).astype(jnp.bfloat16)
            inner[:, rows, :] = inner_g.reshape(RANK, GROUP, D)
            pair = (mm(xg, inner_g, NT) * samples_match).astype(jnp.bfloat16)
            for j in range(TABLES // OCTET):
                part = pair[OCTET * GROUP * j : OCTET * GROUP * (j + 1)]
                wide_part = mm(part, rank_of) * table_match
                flat[rows, OCTET * RANK * j : OCTET * RANK * (j + 1)] = jnp.sum(
                    wide_part.reshape(OCTET, GROUP, OCTET * RANK), axis=0
                ).astype(jnp.bfloat16)
            return carry

        lax.fori_loop(0, groups, group, 0, unroll=2)
        pairs = flat.shape[1]
        block = 256
        unit_b = eye(block)
        for b in range(pairs // block):
            at = slice(block * b, block * (b + 1))
            flat_t[at] = mm(unit_b, flat[:, at], NT).astype(jnp.bfloat16)
        for b in range(hidden_size // block):
            at = slice(block * b, block * (b + 1))
            pre = mm(flat[...], w_first[:, at])
            sigmoid_v = 1.0 / (1.0 + jnp.exp(-pre))
            slope[:, at] = sigmoid_v * (1.0 + pre * (1.0 - sigmoid_v))
            hidden_b = (pre * sigmoid_v).astype(jnp.bfloat16)
            hidden[:, at] = hidden_b
            hidden_t[at] = mm(unit_b, hidden_b, NT).astype(jnp.bfloat16)
        gain_column = jnp.sum(
            jnp.where(iota((D, D), 0) == iota((D, D), 1), gain[...], 0.0), axis=1, keepdims=True
        )
        scale = 1.0 / D
        gain_sum = jnp.zeros((D, samples), jnp.float32)

        def norm(joined, o, gain_sum):
            mean = jnp.sum(joined, axis=0, keepdims=True) * scale
            centered = joined - mean
            variance = jnp.sum(centered * centered, axis=0, keepdims=True) * scale
            inv_std = lax.rsqrt(variance + 1e-05)
            normed = centered * inv_std
            cotangent = up[o].astype(jnp.float32)
            gain_sum = gain_sum + cotangent * normed
            d_norm = cotangent * gain_column
            mean_d = jnp.sum(d_norm, axis=0, keepdims=True) * scale
            mean_n = jnp.sum(d_norm * normed, axis=0, keepdims=True) * scale
            return (inv_std * (d_norm - mean_d - normed * mean_n)).astype(jnp.bfloat16), gain_sum

        for c in range(FM_OUT // 2):
            at = slice(2 * D * c, 2 * D * (c + 1))
            fm_t = mm(hidden[...], w_second[:, at]).T
            low, gain_sum = norm(fm_t[:D], 2 * c, gain_sum)
            high, gain_sum = norm(fm_t[D:], 2 * c + 1, gain_sum)
            both = jnp.concatenate([low, high], axis=0)
            d_fm[:, at] = mm(unit, both, NT).astype(jnp.bfloat16)
        for o in range(LC_OUT):
            d_joined, gain_sum = norm(lc_out[o], FM_OUT + o, gain_sum)
            d_lc[o] = mm(unit, d_joined, NT).astype(jnp.bfloat16)
        gain_row = jnp.sum(gain_sum, axis=1, keepdims=True)
        grad_gain[...] = jnp.broadcast_to(gain_row, grad_gain.shape)
        for b in range(hidden_size // block):
            at = slice(block * b, block * (b + 1))
            d_pre[:, at] = (mm(d_fm[...], w_second[at], NT) * slope[:, at]).astype(jnp.bfloat16)
        d_pair[...] = mm(d_pre[...], w_first[...], NT).astype(jnp.bfloat16)

    mine = core[0]
    narrow = keep.shape[1]
    second_rows = hidden_t.shape[0] // wide
    first_rows = flat_t.shape[0] // wide
    own_second, own_first = second_rows // narrow, first_rows // narrow
    second_cuts, first_cuts = d_fm.shape[1] // COLUMNS, hidden_size // COLUMNS
    for which, out in ((1 - mine, send), (mine, keep)):
        w = 2 * step + which
        rows = pl.ds(pl.multiple_of(w * second_rows, second_rows), second_rows)
        for c in range(second_cuts):
            part = mm(hidden_t[rows], d_fm[:, COLUMNS * c : COLUMNS * (c + 1)])
            out[0, :, own_second * c : own_second * (c + 1), :] = part.reshape(
                narrow, own_second, COLUMNS
            )
        rows = pl.ds(pl.multiple_of(w * first_rows, first_rows), first_rows)
        for c in range(first_cuts):
            part = mm(flat_t[rows], d_pre[:, COLUMNS * c : COLUMNS * (c + 1)])
            at = own_second * second_cuts + own_first * c
            out[0, :, at : at + own_first, :] = part.reshape(narrow, own_first, COLUMNS)


def whole(shape):
    zeros = (0,) * len(shape)
    return pl.BlockSpec(shape, lambda j, c: zeros, pipeline_mode=pl.Buffered(1))


def mlp(core, x, up, proj, w_first, w_second, comp, gain, wide, narrow):
    samples = x.shape[2]
    pairs, hidden_size = w_first.shape
    outs = w_second.shape[1]
    half = wide // 2
    chunk = (w_first.size + w_second.size) // (wide * narrow * COLUMNS)
    sums = jax.ShapeDtypeStruct((half, narrow, chunk, COLUMNS), jnp.float32)
    rest = [
        jax.ShapeDtypeStruct((TABLES, samples, D), jnp.bfloat16),
        jax.ShapeDtypeStruct((RANK, samples, D), jnp.bfloat16),
        jax.ShapeDtypeStruct((samples, pairs), jnp.bfloat16),
        jax.ShapeDtypeStruct((LC_OUT, samples, D), jnp.bfloat16),
        jax.ShapeDtypeStruct((D, LANES), jnp.float32),
    ]

    def by_step(shape):
        return pl.BlockSpec((1,) + shape.shape[1:], lambda j, c: (j, 0, 0, 0))

    bf16, f32 = jnp.bfloat16, jnp.float32
    return pl.pallas_call(
        functools.partial(mlp_kernel, wide),
        grid_spec=pltpu.PrefetchScalarGridSpec(
            num_scalar_prefetch=1,
            grid=(half,),
            in_specs=[whole(a.shape) for a in (x, up, proj, w_first, w_second, comp, gain)],
            out_specs=[by_step(sums)] * 2 + [whole(r.shape) for r in rest],
            scratch_shapes=[
                pltpu.VMEM((samples, pairs), bf16),
                pltpu.VMEM((pairs, samples), bf16),
                pltpu.VMEM((samples, hidden_size), bf16),
                pltpu.VMEM((hidden_size, samples), bf16),
                pltpu.VMEM((samples, hidden_size), f32),
                pltpu.VMEM((LC_OUT, D, samples), f32),
                pltpu.VMEM((samples, outs), bf16),
                pltpu.VMEM((samples, hidden_size), bf16),
            ],
        ),
        out_shape=[sums, sums] + rest,
        compiler_params=pltpu.CompilerParams(vmem_limit_bytes=VMEM),
        cost_estimate=pl.CostEstimate(
            flops=16_000_000_000, bytes_accessed=32_000_000, transcendentals=600_000
        ),
    )(core, x, up, proj, w_first, w_second, comp, gain)


def rows_kernel(
    narrow, here, xs, inner, d_pair, d_lc, proj, comp, hot_ids, cold_ids, *refs
):
    colds, (hot, sums, d_rows, totals) = refs[:narrow], refs[narrow:]
    samples = xs.shape[1]
    share = COLD_TABLES // narrow
    proj_rows, comp_rows = expand(proj[...]), expand_t(comp[...])
    match = same_sample(OCTET * GROUP, RANK * GROUP)
    match_t = same_sample(RANK * GROUP, OCTET * GROUP)
    rank_of, table_match = pick_rank(), same_table()
    totals[...] = jnp.zeros_like(totals)

    def group(g, carry):
        rows = pl.ds(pl.multiple_of(g * GROUP, GROUP), GROUP)
        xg = xs[:, rows, :].reshape(TABLES * GROUP, D)
        inner_g = inner[:, rows, :].reshape(RANK * GROUP, D)
        d_lc_g = d_lc[:, rows, :].reshape(LC_OUT * GROUP, D)
        parts, parts_t = [], []
        for j in range(TABLES // OCTET):
            own = d_pair[rows, OCTET * RANK * j : OCTET * RANK * (j + 1)]
            spread = jnp.concatenate([own] * OCTET, axis=0) * table_match
            parts.append(mm(spread, rank_of, NT).astype(jnp.bfloat16) * match)
            parts_t.append(mm(rank_of, spread, NT).astype(jnp.bfloat16) * match_t)
        d_pairs = jnp.concatenate(parts, axis=0)
        d_pairs_t = jnp.concatenate(parts_t, axis=1)
        d_inner = mm(d_pairs_t, xg).astype(jnp.bfloat16)
        d_embed = mm(d_pairs, inner_g) + mm(proj_rows, d_inner) + mm(comp_rows, d_lc_g)
        d_rows[:, rows, :] = d_embed.astype(jnp.bfloat16).reshape(TABLES, GROUP, D)
        totals[...] += mm(jnp.concatenate([d_inner, d_lc_g], axis=0), xg, NT)
        return carry

    lax.fori_loop(0, samples // GROUP, group, 0, unroll=2)
    unit = eye(D)
    for step in range(narrow):
        target = lax.rem(here[0] + step, narrow)
        for i in range(share):
            colds[step][D * i : D * (i + 1)] = mm(
                unit, d_rows[HOT_TABLES + target * share + i], NT
            )
        for i in range(ID_ROWS):
            colds[step][D * share + i : D * share + i + 1] = cold_ids[
                pl.ds(target * share + min(i, share - 1), 1)
            ]
    for t in range(HOT_TABLES):
        values = mm(unit, d_rows[t], NT).astype(jnp.bfloat16)
        onehot = ones_where(iota((HOT_ROWS, samples), 0) == hot_ids[t : t + 1, :])
        hot[t] = mm(values, onehot, NT)
    sums_shape = totals.shape
    own = lax.rem(iota(sums_shape, 0), GROUP) == lax.rem(iota(sums_shape, 1), GROUP)
    masked = jnp.where(own, totals[...], 0.0)
    folded = jnp.sum(masked.reshape(RANK + LC_OUT, GROUP, sums_shape[1]), axis=1)
    sums[...] = lax.dot_general(
        folded,
        spread_rows(TABLES).astype(jnp.float32),
        NN,
        precision=lax.Precision.HIGHEST,
        preferred_element_type=jnp.float32,
    )


def row_gradients(here, xs, inner, d_pair, d_lc, proj, comp, hot_ids, cold_ids, narrow):
    samples = xs.shape[1]
    share = COLD_TABLES // narrow
    vmem = pl.BlockSpec(memory_space=pltpu.VMEM)
    return pl.pallas_call(
        functools.partial(rows_kernel, narrow),
        in_specs=[pl.BlockSpec(memory_space=pltpu.SMEM)] + [vmem] * 8,
        out_specs=[vmem] * (narrow + 2),
        out_shape=[jax.ShapeDtypeStruct((share * D + ID_ROWS, samples), jnp.float32)] * narrow
        + [
            jax.ShapeDtypeStruct((HOT_TABLES, D, HOT_ROWS), jnp.float32),
            jax.ShapeDtypeStruct((RANK + LC_OUT, TABLES), jnp.float32),
        ],
        scratch_shapes=[
            pltpu.VMEM((TABLES, samples, D), jnp.bfloat16),
            pltpu.VMEM(((RANK + LC_OUT) * GROUP, TABLES * GROUP), jnp.float32),
        ],
        compiler_params=pltpu.CompilerParams(vmem_limit_bytes=VMEM),
        cost_estimate=pl.CostEstimate(
            flops=8_000_000_000, bytes_accessed=12_000_000, transcendentals=0
        ),
    )(here, xs, inner, d_pair, d_lc, proj, comp, hot_ids, cold_ids)


def bits_of(axis):
    return (lax.axis_size(axis) - 1).bit_length()


def flip(value, axis, bit):
    return lax.ppermute(value, axis, [(i, i ^ (1 << bit)) for i in range(lax.axis_size(axis))])


def my_bit(axis, bit):
    return (lax.axis_index(axis) >> bit) & 1


def split(value, dims, label):
    dim = dims.index(label)
    me = my_bit(*label)
    send = lax.dynamic_index_in_dim(value, 1 - me, dim, keepdims=False)
    keep = lax.dynamic_index_in_dim(value, me, dim, keepdims=False)
    return send, keep, dims[:dim] + dims[dim + 1 :]


def join(value, label):
    got = flip(value, *label)
    me = my_bit(*label)
    return jnp.stack([jnp.where(me == 0, value, got), jnp.where(me == 0, got, value)], axis=0)


def nothing(*refs):
    pass


def gate(values, after=()):
    values, after = list(values), list(after)
    return pl.pallas_call(
        nothing,
        in_specs=[pl.BlockSpec(memory_space=pl.ANY)] * (len(values) + len(after)),
        out_specs=[pl.BlockSpec(memory_space=pl.ANY)] * len(values),
        out_shape=[jax.ShapeDtypeStruct(v.shape, v.dtype) for v in values],
        input_output_aliases={i: i for i in range(len(values))},
    )(*values, *after)


def start(parts, labels):
    return [split(value, dims, label) for (value, dims), label in zip(parts, labels)]


def finish(cuts, labels):
    return [(keep + flip(send, *label), dims) for (send, keep, dims), label in zip(cuts, labels)]


def ordered(cuts, after=()):
    sends = gate([cut[0] for cut in cuts], after)
    return [(send, cut[1], cut[2]) for send, cut in zip(sends, cuts)]


def combine_kernel(bits, *refs):
    sums = [refs[2 * i][...] + refs[2 * i + 1][...] for i in range(4)]
    for value, out in zip(sums, refs[8:]):
        out[...] = value


def combine(bits, keep, got):
    blocks, n, rows, columns = keep.shape
    half = blocks // 2
    shape = (1, n, rows // 2, columns)

    def spec(piece, other):
        if piece == 0:
            return pl.BlockSpec(shape, lambda i, b: (2 * i + (b[0] ^ other), 0, 0, 0))
        return pl.BlockSpec(shape, lambda i, b: (half * (b[1] ^ other) + i, 0, 1, 0))

    specs = [spec(piece, other) for piece in (0, 1) for other in (1, 0)]
    out = jax.ShapeDtypeStruct((half, n, rows // 2, columns), keep.dtype)
    return pl.pallas_call(
        combine_kernel,
        grid_spec=pltpu.PrefetchScalarGridSpec(
            num_scalar_prefetch=1,
            grid=(half,),
            in_specs=[s for s in specs for _ in range(2)],
            out_specs=[pl.BlockSpec(shape, lambda i, b: (i, 0, 0, 0))] * 4,
        ),
        out_shape=[out] * 4,
        compiler_params=pltpu.CompilerParams(vmem_limit_bytes=VMEM),
        cost_estimate=pl.CostEstimate(
            flops=keep.size, bytes_accessed=12 * keep.size, transcendentals=0
        ),
    )(bits, *[keep, got] * 4)


def add_rows_kernel(rows, parts, core, *refs):
    ids, values, (keep, send) = refs[:parts], refs[parts : 2 * parts], refs[-2:]
    table = pl.program_id(0)
    numbers = jnp.concatenate([r[pl.ds(table, 1)] for r in ids], axis=1).astype(jnp.int32)
    owners, at = lax.div(numbers, rows), lax.rem(numbers, rows)
    values = jnp.concatenate([r[...].astype(jnp.bfloat16) for r in values], axis=1)
    onehot = ones_where(iota((rows, numbers.shape[1]), 0) == at)
    for which, out in ((1 - core[0], send), (core[0], keep)):
        for b in range(out.shape[0]):
            out[b, 0] = mm(values * ones_where(owners == 2 * b + which), onehot, NT)


def add_rows(core, values, tables, blocks, rows):
    samples = values[0].shape[1]
    parts = len(values)
    out = jax.ShapeDtypeStruct((blocks // 2, tables, D, rows), jnp.float32)
    return pl.pallas_call(
        functools.partial(add_rows_kernel, rows, parts),
        grid_spec=pltpu.PrefetchScalarGridSpec(
            num_scalar_prefetch=1,
            grid=(tables,),
            in_specs=[
                pl.BlockSpec((ID_ROWS, samples), lambda t, c: (tables * D // ID_ROWS, 0))
            ]
            * parts
            + [pl.BlockSpec((D, samples), lambda t, c: (t, 0))] * parts,
            out_specs=[pl.BlockSpec((blocks // 2, 1, D, rows), lambda t, c: (0, t, 0, 0))] * 2,
        ),
        out_shape=[out] * 2,
        compiler_params=pltpu.CompilerParams(vmem_limit_bytes=VMEM),
        cost_estimate=pl.CostEstimate(
            flops=1, bytes_accessed=1, transcendentals=0
        ),
    )(core, *values, *values)


def local(
    embeddings,
    upstream,
    factor_machine_projection,
    w_first,
    w_second,
    compress,
    norm_gain,
    hot_index,
    cold_row,
    cold_owner,
):
    wide, narrow = lax.axis_size("wide"), lax.axis_size("narrow")
    devices = wide * narrow
    wide_bits = [("wide", b) for b in range(bits_of("wide"))]
    narrow_bits = [("narrow", b) for b in range(bits_of("narrow"))]
    core_bit, links = wide_bits[0], wide_bits[1:]
    left_dims = links[::-1] + narrow_bits[::-1]

    sample_count = embeddings.shape[0]
    here = lax.axis_index("narrow")
    x = jnp.transpose(embeddings, (1, 2, 0))
    up = jnp.transpose(upstream, (1, 2, 0))
    core = my_bit("wide", 0).reshape(1)
    mlp_keep, mlp_send, xs, inner, d_pair, d_lc, gain_sum = mlp(
        core,
        x,
        up,
        factor_machine_projection,
        w_first,
        w_second,
        compress,
        norm_gain.reshape(1, D),
        wide,
        narrow,
    )
    *cold_values, hot_local, sums = row_gradients(
        here.reshape(1),
        xs,
        inner,
        d_pair,
        d_lc,
        factor_machine_projection,
        compress,
        hot_index.T,
        (cold_owner[:, :, 0] * COLD_ROWS_DEV + cold_row).T.astype(jnp.float32),
        narrow,
    )
    grad_gain = gain_sum[:, 0]
    grad_proj, compress_gradient = sums[:RANK].T, sums[RANK:]

    share = COLD_TABLES // narrow

    def go_round(value, step):
        return lax.ppermute(value, "narrow", [(i, (i + step) % narrow) for i in range(narrow)])

    got_values = [cold_values[0], go_round(cold_values[1], 1)]

    hot_rows = hot_local.size // LANES
    small = jnp.concatenate([grad_proj.reshape(-1), compress_gradient.reshape(-1), grad_gain])
    small = jnp.pad(small, (0, -small.size % LANES)).reshape(-1, LANES)
    shared = jnp.concatenate([hot_local.reshape(hot_rows, LANES), small], axis=0)
    shared = jnp.pad(shared, ((0, -shared.shape[0] % (8 * devices)), (0, 0)))
    hot_order = [core_bit] + links + narrow_bits
    shared = shared.reshape([2] * len(hot_order) + [-1, LANES])
    hot = (shared, hot_order)

    def halve(part, label):
        (part,) = finish(start([part], [label]), [label])
        return part

    hot = halve(halve(hot, core_bit), links[0])

    (mlp_got,) = gate([flip(mlp_send, *core_bit)], [cold_values[0]])
    link_bits = jnp.stack([my_bit(*links[0]), my_bit(*links[-1])])

    def first_cuts(keep, got):
        a_send, a_keep, b_send, b_keep = combine(link_bits, keep, got)
        dims = links[::-1]
        return [
            (a_send, a_keep, dims[:-1]),
            (b_send, b_keep, dims[1:]),
        ]

    def unfold(parts, tail):
        return [(value.reshape([2] * len(dims) + tail), dims) for value, dims in parts]

    chunk = mlp_keep.shape[2]
    cuts = first_cuts(mlp_keep, mlp_got)
    later = list(cold_values[2:])
    sends = gate([cut[0] for cut in cuts] + later, [hot[0], got_values[1]])
    cuts = [(send, cut[1], cut[2]) for send, cut in zip(sends, cuts)]
    got_values += [go_round(value, step + 2) for step, value in enumerate(sends[2:])]
    mlp_parts = unfold(
        finish(cuts, [links[0], links[-1]]), [2] * len(narrow_bits) + [chunk // 2, COLUMNS]
    )
    mlp_parts = [(value, dims + narrow_bits[::-1]) for value, dims in mlp_parts]
    for turn in range(1, len(links)):
        labels = [links[turn], links[-1 - turn]]
        cuts = start(mlp_parts, labels)
        if turn == len(links) - 1:
            (hot_cut,) = start([hot], narrow_bits[:1])
            sends = gate([cut[0] for cut in cuts] + [hot_cut[0]] + got_values)
            cuts = [(send, cut[1], cut[2]) for send, cut in zip(sends, cuts)]
            (hot,) = finish([(sends[2], hot_cut[1], hot_cut[2])], narrow_bits[:1])
            got_values = sends[3:]
        mlp_parts = finish(cuts, labels)

    cold_keep, cold_send = add_rows(core, got_values, share, wide, COLD_ROWS_DEV)
    low, high = narrow_bits
    ready = start([hot, mlp_parts[0]], [high, low])
    cold_send, *sends = gate([cold_send] + [cut[0] for cut in ready], [mlp_parts[1][0]])
    ready = [(send, cut[1], cut[2]) for send, cut in zip(sends, ready)]
    hot, mlp_first = finish(ready, [high, low])
    mlp_second = mlp_parts[1]
    cuts = first_cuts(cold_keep, flip(cold_send, *core_bit))
    half = D // 2
    parts = []
    for turn in range(len(links)):
        labels = [links[turn], links[-1 - turn]]
        moving = list(parts)
        if turn == 0:
            moving, labels = [mlp_second, mlp_first, hot], labels + [low, high, links[1]]
        elif turn == len(links) - 1:
            moving, labels = moving + [mlp_second], labels + [high]
        first = cuts if turn == 0 else []
        ready = first + start(moving, labels[len(first) :])
        if turn == len(links) - 1:
            *sends, hot_value = gate([cut[0] for cut in ready] + [hot[0]])
            ready = [(send, cut[1], cut[2]) for send, cut in zip(sends, ready)]
            hot_value = join(hot_value, high)
        else:
            ready = ordered(ready)
        moved = finish(ready, labels)
        parts = moved[:2]
        if turn == 0:
            parts = unfold(parts, [share, half, COLD_ROWS_DEV])
            mlp_second, mlp_first, hot = moved[2:]
            for label in links[2:]:
                hot = halve(hot, label)
        elif turn == len(links) - 1:
            mlp_second = moved[2]
    mlp_parts = [mlp_first, mlp_second]

    cold_grad = jnp.zeros((narrow, share, D, COLD_ROWS_DEV), jnp.float32)
    moving = jnp.concatenate([parts[0][0], parts[1][0]], axis=1)
    joins = [narrow_bits[:1], links[:0:-1]] + [[]] * (narrow - 4) + [links[:1]]
    for step in range(narrow):
        cold_grad = lax.dynamic_update_index_in_dim(cold_grad, moving, (here - step) % narrow, 0)
        if step == narrow - 1:
            break
        after = [] if step else [value for value, _ in mlp_parts]
        moving, hot_value = gate([moving, hot_value], after)
        moving = go_round(moving, 1)
        for label in joins[step]:
            hot_value = join(hot_value, label)
    (hot_value,) = gate([hot_value], [moving])
    shared = join(hot_value, core_bit).reshape(-1, LANES)
    cold_grad = jnp.transpose(
        cold_grad.reshape(COLD_TABLES, D, COLD_ROWS_DEV), (0, 2, 1)
    )
    hot_grad = jnp.transpose(shared[:hot_rows].reshape(HOT_TABLES, D, HOT_ROWS), (0, 2, 1))
    small = shared[hot_rows:].reshape(-1)
    n_proj, n_compress = TABLES * RANK, LC_OUT * TABLES
    grad_proj = small[:n_proj].reshape(TABLES, RANK)
    compress_gradient = small[n_proj : n_proj + n_compress].reshape(LC_OUT, TABLES)
    grad_gain = small[n_proj + n_compress : n_proj + n_compress + D]

    done = jnp.concatenate([value for value, _ in mlp_parts], axis=0)
    own_second, own_first = w_first.shape[1] // devices, TABLES * RANK // devices
    cut = own_second * FM_OUT * D // COLUMNS

    def side_by_side(blocks, rows):
        return jnp.transpose(blocks.reshape(-1, rows, COLUMNS), (1, 0, 2)).reshape(rows, -1)

    grad_second = side_by_side(done[:cut], own_second)
    grad_first = side_by_side(done[cut:], own_first)
    return (grad_first, grad_second, grad_proj, compress_gradient, grad_gain, hot_grad, cold_grad)


def solution(mesh):
    placed = (
        P(("wide", "narrow"), None, None),
        P(("wide", "narrow"), None, None),
        P(),
        P(),
        P(),
        P(),
        P(),
        P(("wide", "narrow"), None),
        P(("wide", "narrow"), None),
        P(("wide", "narrow"), None, None),
    )
    return jax.shard_map(
        local,
        mesh=mesh,
        in_specs=placed,
        out_specs=(
            P(("wide", "narrow"), None),
            P(("wide", "narrow"), None),
            P(),
            P(),
            P(),
            P(),
            P(None, "wide", None),
        ),
        check_vma=False,
    )
```

```python
import functools

import jax
import jax.numpy as jnp
from jax import lax
from jax.experimental import pallas as pl
from jax.experimental.pallas import tpu as pltpu
from jax.sharding import PartitionSpec as P

D = 192
RANK = 16
HOT_TABLES = 16
COLD_TABLES = 16
FM_OUT = 8
LC_OUT = 8
HOT_ROWS = 128
COLD_ROWS_DEV = 256
TABLES = 32
LANES = 128
COLUMNS = 512
ID_ROWS = 8
DENSE_COST = 12000000000


NT = (((1,), (1,)), ((), ()))
NN = (((1,), (0,)), ((), ()))
GROUP = 16
OCTET = 8
VMEM = 60 * 1024 * 1024


def mm(a, b, dims=NN):
    return lax.dot_general(a, b, dims, preferred_element_type=jnp.float32)


def iota(shape, dim):
    return lax.broadcasted_iota(jnp.int32, shape, dim)


def ones_where(mask):
    return mask.astype(jnp.float32).astype(jnp.bfloat16)


def eye(size):
    return ones_where(iota((size, size), 0) == iota((size, size), 1))


def same_sample(rows, columns):
    return ones_where(
        lax.rem(iota((rows, columns), 0), GROUP) == lax.rem(iota((rows, columns), 1), GROUP)
    )


def spread_rows(count):
    return ones_where(
        lax.div(iota((count * GROUP, count), 0), GROUP) == iota((count * GROUP, count), 1)
    )


def spread_columns(count):
    return ones_where(
        lax.div(iota((count, count * GROUP), 1), GROUP) == iota((count, count * GROUP), 0)
    )


def expand(matrix):
    rows, columns = matrix.shape
    tall = mm(spread_rows(rows), matrix).astype(jnp.bfloat16)
    full = mm(tall, spread_columns(columns)).astype(jnp.bfloat16)
    return full * same_sample(rows * GROUP, columns * GROUP)


def expand_t(matrix):
    rows, columns = matrix.shape
    tall = mm(spread_rows(columns), matrix, NT).astype(jnp.bfloat16)
    full = mm(tall, spread_columns(rows)).astype(jnp.bfloat16)
    return full * same_sample(columns * GROUP, rows * GROUP)


def pick_rank():
    shape = (RANK * GROUP, OCTET * RANK)
    return ones_where(lax.div(iota(shape, 0), GROUP) == lax.rem(iota(shape, 1), RANK))


def same_table():
    shape = (OCTET * GROUP, OCTET * RANK)
    return ones_where(lax.div(iota(shape, 0), GROUP) == lax.div(iota(shape, 1), RANK))


def mlp_kernel(
    wide,
    core,
    x,
    up,
    proj,
    w_first,
    w_second,
    comp,
    gain,
    keep,
    send,
    xs,
    inner,
    d_pair,
    d_lc,
    grad_gain,
    flat,
    flat_t,
    hidden,
    hidden_t,
    slope,
    lc_out,
    d_fm,
    d_pre,
):
    step = pl.program_id(0)
    samples = x.shape[2]
    hidden_size = w_first.shape[1]
    groups = samples // GROUP

    @pl.when(step == 0)
    def _():
        unit = eye(samples)
        for n in range(TABLES):
            xs[n] = mm(unit, x[n], NT).astype(jnp.bfloat16)
        comp_rows = expand(comp[...])
        for b in range(D // GROUP):
            block = x[:, GROUP * b : GROUP * (b + 1), :].reshape(TABLES * GROUP, samples)
            lc_out[:, GROUP * b : GROUP * (b + 1), :] = mm(comp_rows, block).reshape(
                LC_OUT, GROUP, samples
            )
        proj_t = expand_t(proj[...])
        samples_match = same_sample(TABLES * GROUP, RANK * GROUP).astype(jnp.float32)
        rank_of = pick_rank()
        table_match = same_table().astype(jnp.float32)

        def group(g, carry):
            rows = pl.ds(pl.multiple_of(g * GROUP, GROUP), GROUP)
            xg = xs[:, rows, :].reshape(TABLES * GROUP, D)
            inner_g = mm(proj_t, xg).astype(jnp.bfloat16)
            inner[:, rows, :] = inner_g.reshape(RANK, GROUP, D)
            pair = (mm(xg, inner_g, NT) * samples_match).astype(jnp.bfloat16)
            for j in range(TABLES // OCTET):
                part = pair[OCTET * GROUP * j : OCTET * GROUP * (j + 1)]
                wide_part = mm(part, rank_of) * table_match
                flat[rows, OCTET * RANK * j : OCTET * RANK * (j + 1)] = jnp.sum(
                    wide_part.reshape(OCTET, GROUP, OCTET * RANK), axis=0
                ).astype(jnp.bfloat16)
            return carry

        lax.fori_loop(0, groups, group, 0, unroll=2)
        pairs = flat.shape[1]
        block = 256
        unit_b = eye(block)
        for b in range(pairs // block):
            at = slice(block * b, block * (b + 1))
            flat_t[at] = mm(unit_b, flat[:, at], NT).astype(jnp.bfloat16)
        for b in range(hidden_size // block):
            at = slice(block * b, block * (b + 1))
            pre = mm(flat[...], w_first[:, at])
            sigmoid_v = 1.0 / (1.0 + jnp.exp(-pre))
            slope[:, at] = sigmoid_v * (1.0 + pre * (1.0 - sigmoid_v))
            hidden_b = (pre * sigmoid_v).astype(jnp.bfloat16)
            hidden[:, at] = hidden_b
            hidden_t[at] = mm(unit_b, hidden_b, NT).astype(jnp.bfloat16)
        gain_column = jnp.sum(
            jnp.where(iota((D, D), 0) == iota((D, D), 1), gain[...], 0.0), axis=1, keepdims=True
        )
        scale = 1.0 / D
        gain_sum = jnp.zeros((D, samples), jnp.float32)

        def norm(joined, o, gain_sum):
            mean = jnp.sum(joined, axis=0, keepdims=True) * scale
            centered = joined - mean
            variance = jnp.sum(centered * centered, axis=0, keepdims=True) * scale
            inv_std = lax.rsqrt(variance + 1e-05)
            normed = centered * inv_std
            cotangent = up[o].astype(jnp.float32)
            gain_sum = gain_sum + cotangent * normed
            d_norm = cotangent * gain_column
            mean_d = jnp.sum(d_norm, axis=0, keepdims=True) * scale
            mean_n = jnp.sum(d_norm * normed, axis=0, keepdims=True) * scale
            return (inv_std * (d_norm - mean_d - normed * mean_n)).astype(jnp.bfloat16), gain_sum

        for c in range(FM_OUT // 2):
            at = slice(2 * D * c, 2 * D * (c + 1))
            fm_t = mm(hidden[...], w_second[:, at]).T
            low, gain_sum = norm(fm_t[:D], 2 * c, gain_sum)
            high, gain_sum = norm(fm_t[D:], 2 * c + 1, gain_sum)
            both = jnp.concatenate([low, high], axis=0)
            d_fm[:, at] = mm(unit, both, NT).astype(jnp.bfloat16)
        for o in range(LC_OUT):
            d_joined, gain_sum = norm(lc_out[o], FM_OUT + o, gain_sum)
            d_lc[o] = mm(unit, d_joined, NT).astype(jnp.bfloat16)
        gain_row = jnp.sum(gain_sum, axis=1, keepdims=True)
        grad_gain[...] = jnp.broadcast_to(gain_row, grad_gain.shape)
        for b in range(hidden_size // block):
            at = slice(block * b, block * (b + 1))
            d_pre[:, at] = (mm(d_fm[...], w_second[at], NT) * slope[:, at]).astype(jnp.bfloat16)
        d_pair[...] = mm(d_pre[...], w_first[...], NT).astype(jnp.bfloat16)

    mine = core[0]
    narrow = keep.shape[1]
    second_rows = hidden_t.shape[0] // wide
    first_rows = flat_t.shape[0] // wide
    own_second, own_first = second_rows // narrow, first_rows // narrow
    second_cuts, first_cuts = d_fm.shape[1] // COLUMNS, hidden_size // COLUMNS
    for which, out in ((1 - mine, send), (mine, keep)):
        w = 2 * step + which
        rows = pl.ds(pl.multiple_of(w * second_rows, second_rows), second_rows)
        for c in range(second_cuts):
            part = mm(hidden_t[rows], d_fm[:, COLUMNS * c : COLUMNS * (c + 1)])
            out[0, :, own_second * c : own_second * (c + 1), :] = part.reshape(
                narrow, own_second, COLUMNS
            )
        rows = pl.ds(pl.multiple_of(w * first_rows, first_rows), first_rows)
        for c in range(first_cuts):
            part = mm(flat_t[rows], d_pre[:, COLUMNS * c : COLUMNS * (c + 1)])
            at = own_second * second_cuts + own_first * c
            out[0, :, at : at + own_first, :] = part.reshape(narrow, own_first, COLUMNS)


def whole(shape):
    zeros = (0,) * len(shape)
    return pl.BlockSpec(shape, lambda j, c: zeros, pipeline_mode=pl.Buffered(1))


def mlp(core, x, up, proj, w_first, w_second, comp, gain, wide, narrow):
    samples = x.shape[2]
    pairs, hidden_size = w_first.shape
    outs = w_second.shape[1]
    half = wide // 2
    chunk = (w_first.size + w_second.size) // (wide * narrow * COLUMNS)
    sums = jax.ShapeDtypeStruct((half, narrow, chunk, COLUMNS), jnp.float32)
    rest = [
        jax.ShapeDtypeStruct((TABLES, samples, D), jnp.bfloat16),
        jax.ShapeDtypeStruct((RANK, samples, D), jnp.bfloat16),
        jax.ShapeDtypeStruct((samples, pairs), jnp.bfloat16),
        jax.ShapeDtypeStruct((LC_OUT, samples, D), jnp.bfloat16),
        jax.ShapeDtypeStruct((D, LANES), jnp.float32),
    ]

    def by_step(shape):
        return pl.BlockSpec((1,) + shape.shape[1:], lambda j, c: (j, 0, 0, 0))

    bf16, f32 = jnp.bfloat16, jnp.float32
    return pl.pallas_call(
        functools.partial(mlp_kernel, wide),
        grid_spec=pltpu.PrefetchScalarGridSpec(
            num_scalar_prefetch=1,
            grid=(half,),
            in_specs=[whole(a.shape) for a in (x, up, proj, w_first, w_second, comp, gain)],
            out_specs=[by_step(sums)] * 2 + [whole(r.shape) for r in rest],
            scratch_shapes=[
                pltpu.VMEM((samples, pairs), bf16),
                pltpu.VMEM((pairs, samples), bf16),
                pltpu.VMEM((samples, hidden_size), bf16),
                pltpu.VMEM((hidden_size, samples), bf16),
                pltpu.VMEM((samples, hidden_size), f32),
                pltpu.VMEM((LC_OUT, D, samples), f32),
                pltpu.VMEM((samples, outs), bf16),
                pltpu.VMEM((samples, hidden_size), bf16),
            ],
        ),
        out_shape=[sums, sums] + rest,
        compiler_params=pltpu.CompilerParams(vmem_limit_bytes=VMEM),
        cost_estimate=pl.CostEstimate(
            flops=16_000_000_000, bytes_accessed=32_000_000, transcendentals=600_000
        ),
    )(core, x, up, proj, w_first, w_second, comp, gain)


def rows_kernel(
    narrow, here, xs, inner, d_pair, d_lc, proj, comp, hot_ids, cold_ids, *refs
):
    colds, (hot, sums, d_rows, totals) = refs[:narrow], refs[narrow:]
    samples = xs.shape[1]
    share = COLD_TABLES // narrow
    proj_rows, comp_rows = expand(proj[...]), expand_t(comp[...])
    match = same_sample(OCTET * GROUP, RANK * GROUP)
    match_t = same_sample(RANK * GROUP, OCTET * GROUP)
    rank_of, table_match = pick_rank(), same_table()
    totals[...] = jnp.zeros_like(totals)

    def group(g, carry):
        rows = pl.ds(pl.multiple_of(g * GROUP, GROUP), GROUP)
        xg = xs[:, rows, :].reshape(TABLES * GROUP, D)
        inner_g = inner[:, rows, :].reshape(RANK * GROUP, D)
        d_lc_g = d_lc[:, rows, :].reshape(LC_OUT * GROUP, D)
        parts, parts_t = [], []
        for j in range(TABLES // OCTET):
            own = d_pair[rows, OCTET * RANK * j : OCTET * RANK * (j + 1)]
            spread = jnp.concatenate([own] * OCTET, axis=0) * table_match
            parts.append(mm(spread, rank_of, NT).astype(jnp.bfloat16) * match)
            parts_t.append(mm(rank_of, spread, NT).astype(jnp.bfloat16) * match_t)
        d_pairs = jnp.concatenate(parts, axis=0)
        d_pairs_t = jnp.concatenate(parts_t, axis=1)
        d_inner = mm(d_pairs_t, xg).astype(jnp.bfloat16)
        d_embed = mm(d_pairs, inner_g) + mm(proj_rows, d_inner) + mm(comp_rows, d_lc_g)
        d_rows[:, rows, :] = d_embed.astype(jnp.bfloat16).reshape(TABLES, GROUP, D)
        totals[...] += mm(jnp.concatenate([d_inner, d_lc_g], axis=0), xg, NT)
        return carry

    lax.fori_loop(0, samples // GROUP, group, 0, unroll=2)
    unit = eye(D)
    for step in range(narrow):
        target = lax.rem(here[0] + step, narrow)
        for i in range(share):
            colds[step][D * i : D * (i + 1)] = mm(
                unit, d_rows[HOT_TABLES + target * share + i], NT
            )
        for i in range(ID_ROWS):
            colds[step][D * share + i : D * share + i + 1] = cold_ids[
                pl.ds(target * share + min(i, share - 1), 1)
            ]
    for t in range(HOT_TABLES):
        values = mm(unit, d_rows[t], NT).astype(jnp.bfloat16)
        onehot = ones_where(iota((HOT_ROWS, samples), 0) == hot_ids[t : t + 1, :])
        hot[t] = mm(values, onehot, NT)
    sums_shape = totals.shape
    own = lax.rem(iota(sums_shape, 0), GROUP) == lax.rem(iota(sums_shape, 1), GROUP)
    masked = jnp.where(own, totals[...], 0.0)
    folded = jnp.sum(masked.reshape(RANK + LC_OUT, GROUP, sums_shape[1]), axis=1)
    sums[...] = lax.dot_general(
        folded,
        spread_rows(TABLES).astype(jnp.float32),
        NN,
        precision=lax.Precision.HIGHEST,
        preferred_element_type=jnp.float32,
    )


def row_gradients(here, xs, inner, d_pair, d_lc, proj, comp, hot_ids, cold_ids, narrow, part, parts):
    samples = xs.shape[1] // parts
    share = COLD_TABLES // narrow

    def middle(count):
        return pl.BlockSpec((count, samples, D), lambda i: (0, part, 0))

    def last(count):
        return pl.BlockSpec((count, samples), lambda i: (0, part))

    def full(*shape):
        zeros = (0,) * len(shape)
        return pl.BlockSpec(shape, lambda i: zeros)

    shapes = [(share * D + ID_ROWS, samples)] * narrow
    shapes += [(HOT_TABLES, D, HOT_ROWS), (RANK + LC_OUT, TABLES)]
    return pl.pallas_call(
        functools.partial(rows_kernel, narrow),
        grid=(1,),
        in_specs=[
            pl.BlockSpec(memory_space=pltpu.SMEM),
            middle(TABLES),
            middle(RANK),
            pl.BlockSpec((samples, TABLES * RANK), lambda i: (part, 0)),
            middle(LC_OUT),
            full(*proj.shape),
            full(*comp.shape),
            last(HOT_TABLES),
            last(COLD_TABLES),
        ],
        out_specs=[full(*shape) for shape in shapes],
        out_shape=[jax.ShapeDtypeStruct(shape, jnp.float32) for shape in shapes],
        scratch_shapes=[
            pltpu.VMEM((TABLES, samples, D), jnp.bfloat16),
            pltpu.VMEM(((RANK + LC_OUT) * GROUP, TABLES * GROUP), jnp.float32),
        ],
        compiler_params=pltpu.CompilerParams(vmem_limit_bytes=VMEM),
        cost_estimate=pl.CostEstimate(
            flops=1, bytes_accessed=1, transcendentals=0
        ),
    )(here, xs, inner, d_pair, d_lc, proj, comp, hot_ids, cold_ids)


def bits_of(axis):
    return (lax.axis_size(axis) - 1).bit_length()


def flip(value, axis, bit):
    return lax.ppermute(value, axis, [(i, i ^ (1 << bit)) for i in range(lax.axis_size(axis))])


def my_bit(axis, bit):
    return (lax.axis_index(axis) >> bit) & 1


def split(value, dims, label):
    dim = dims.index(label)
    me = my_bit(*label)
    send = lax.dynamic_index_in_dim(value, 1 - me, dim, keepdims=False)
    keep = lax.dynamic_index_in_dim(value, me, dim, keepdims=False)
    return send, keep, dims[:dim] + dims[dim + 1 :]


def join(value, label):
    got = flip(value, *label)
    me = my_bit(*label)
    return jnp.stack([jnp.where(me == 0, value, got), jnp.where(me == 0, got, value)], axis=0)


def nothing(*refs):
    pass


def gate(values, after=()):
    values, after = list(values), list(after)
    return list(
        pl.pallas_call(
        nothing,
        in_specs=[pl.BlockSpec(memory_space=pl.ANY)] * (len(values) + len(after)),
        out_specs=[pl.BlockSpec(memory_space=pl.ANY)] * len(values),
        out_shape=[jax.ShapeDtypeStruct(v.shape, v.dtype) for v in values],
        input_output_aliases={i: i for i in range(len(values))},
    )(*values, *after)
    )


def start(parts, labels):
    return [split(value, dims, label) for (value, dims), label in zip(parts, labels)]


def finish(cuts, labels):
    return [(keep + flip(send, *label), dims) for (send, keep, dims), label in zip(cuts, labels)]


def ordered(cuts, after=()):
    sends = gate([cut[0] for cut in cuts], after)
    return [(send, cut[1], cut[2]) for send, cut in zip(sends, cuts)]


def combine_kernel(bits, *refs):
    sums = [refs[2 * i][...] + refs[2 * i + 1][...] for i in range(4)]
    for value, out in zip(sums, refs[8:]):
        out[...] = value


def combine(bits, keep, got):
    blocks, n, rows, columns = keep.shape
    half = blocks // 2
    shape = (1, n, rows // 2, columns)

    def spec(piece, other):
        if piece == 0:
            return pl.BlockSpec(shape, lambda i, b: (2 * i + (b[0] ^ other), 0, 0, 0))
        return pl.BlockSpec(shape, lambda i, b: (half * (b[1] ^ other) + i, 0, 1, 0))

    specs = [spec(piece, other) for piece in (0, 1) for other in (1, 0)]
    out = jax.ShapeDtypeStruct((half, n, rows // 2, columns), keep.dtype)
    return pl.pallas_call(
        combine_kernel,
        grid_spec=pltpu.PrefetchScalarGridSpec(
            num_scalar_prefetch=1,
            grid=(half,),
            in_specs=[s for s in specs for _ in range(2)],
            out_specs=[pl.BlockSpec(shape, lambda i, b: (i, 0, 0, 0))] * 4,
        ),
        out_shape=[out] * 4,
        compiler_params=pltpu.CompilerParams(vmem_limit_bytes=VMEM),
        cost_estimate=pl.CostEstimate(
            flops=keep.size, bytes_accessed=12 * keep.size, transcendentals=0
        ),
    )(bits, *[keep, got] * 4)


def add_rows_kernel(rows, parts, core, *refs):
    ids, values, (keep, send) = refs[:parts], refs[parts : 2 * parts], refs[-2:]
    table = pl.program_id(0)
    numbers = jnp.concatenate([r[pl.ds(table, 1)] for r in ids], axis=1).astype(jnp.int32)
    owners, at = lax.div(numbers, rows), lax.rem(numbers, rows)
    values = jnp.concatenate([r[...].astype(jnp.bfloat16) for r in values], axis=1)
    onehot = ones_where(iota((rows, numbers.shape[1]), 0) == at)
    for which, out in ((1 - core[0], send), (core[0], keep)):
        for b in range(out.shape[0]):
            out[b, 0] = mm(values * ones_where(owners == 2 * b + which), onehot, NT)


def add_rows(core, values, tables, blocks, rows):
    samples = values[0].shape[1]
    parts = len(values)
    out = jax.ShapeDtypeStruct((blocks // 2, tables, D, rows), jnp.float32)
    return pl.pallas_call(
        functools.partial(add_rows_kernel, rows, parts),
        grid_spec=pltpu.PrefetchScalarGridSpec(
            num_scalar_prefetch=1,
            grid=(tables,),
            in_specs=[
                pl.BlockSpec((ID_ROWS, samples), lambda t, c: (tables * D // ID_ROWS, 0))
            ]
            * parts
            + [pl.BlockSpec((D, samples), lambda t, c: (t, 0))] * parts,
            out_specs=[pl.BlockSpec((blocks // 2, 1, D, rows), lambda t, c: (0, t, 0, 0))] * 2,
        ),
        out_shape=[out] * 2,
        compiler_params=pltpu.CompilerParams(vmem_limit_bytes=VMEM),
        cost_estimate=pl.CostEstimate(
            flops=DENSE_COST, bytes_accessed=1, transcendentals=0
        ),
    )(core, *values, *values)


def local(
    embeddings,
    upstream,
    factor_machine_projection,
    w_first,
    w_second,
    compress,
    norm_gain,
    hot_index,
    cold_row,
    cold_owner,
):
    wide, narrow = lax.axis_size("wide"), lax.axis_size("narrow")
    devices = wide * narrow
    wide_bits = [("wide", b) for b in range(bits_of("wide"))]
    narrow_bits = [("narrow", b) for b in range(bits_of("narrow"))]
    core_bit, links = wide_bits[0], wide_bits[1:]
    left_dims = links[::-1] + narrow_bits[::-1]

    sample_count = embeddings.shape[0]
    here = lax.axis_index("narrow")
    x = jnp.transpose(embeddings, (1, 2, 0))
    up = jnp.transpose(upstream, (1, 2, 0))
    core = my_bit("wide", 0).reshape(1)
    mlp_keep, mlp_send, xs, inner, d_pair, d_lc, gain_sum = mlp(
        core,
        x,
        up,
        factor_machine_projection,
        w_first,
        w_second,
        compress,
        norm_gain.reshape(1, D),
        wide,
        narrow,
    )
    cold_ids = (cold_owner[:, :, 0] * COLD_ROWS_DEV + cold_row).T.astype(jnp.float32)

    def rows_of(part, d_pair):
        *values, hot_sums, sums = row_gradients(
            here.reshape(1),
            xs,
            inner,
            d_pair,
            d_lc,
            factor_machine_projection,
            compress,
            hot_index.T,
            cold_ids,
            narrow,
            part,
            2,
        )
        return values, hot_sums, sums

    share = COLD_TABLES // narrow
    low, high = narrow_bits
    link_bits = jnp.stack([my_bit(*links[0]), my_bit(*links[-1])])

    def go_round(value, step):
        return lax.ppermute(value, "narrow", [(i, (i + step) % narrow) for i in range(narrow)])

    def halve(part, label):
        (part,) = finish(start([part], [label]), [label])
        return part

    def first_cuts(keep, got):
        a_send, a_keep, b_send, b_keep = combine(link_bits, keep, got)
        dims = links[::-1]
        return [
            (a_send, a_keep, dims[:-1]),
            (b_send, b_keep, dims[1:]),
        ]

    def unfold(parts, tail):
        return [(value.reshape([2] * len(dims) + tail), dims) for value, dims in parts]

    early, hot_early, sums_early = rows_of(0, d_pair)
    got_early = [go_round(value, step) for step, value in enumerate(early) if step]
    (mlp_got,) = gate([flip(mlp_send, *core_bit)], early[:1])
    chunk = mlp_keep.shape[2]
    cuts = first_cuts(mlp_keep, mlp_got)
    (d_pair_late,) = gate([d_pair], [cuts[0][0]])
    late, hot_late, sums_late = rows_of(1, d_pair_late)

    sums = sums_early + sums_late
    grad_proj, compress_gradient = sums[:RANK].T, sums[RANK:]
    hot_local = hot_early + hot_late
    hot_rows = hot_local.size // LANES
    small = jnp.concatenate([grad_proj.reshape(-1), compress_gradient.reshape(-1), gain_sum[:, 0]])
    small = jnp.pad(small, (0, -small.size % LANES)).reshape(-1, LANES)
    shared = jnp.concatenate([hot_local.reshape(hot_rows, LANES), small], axis=0)
    shared = jnp.pad(shared, ((0, -shared.shape[0] % (8 * devices)), (0, 0)))
    hot_order = [core_bit] + links + [low]
    hot = (shared.reshape([2] * len(hot_order) + [-1, LANES]), hot_order)

    late_sends = gate(late[1:], got_early)
    got_late = [go_round(value, step + 1) for step, value in enumerate(late_sends)]
    got_values = early[:1] + got_early + late[:1] + got_late
    mlp_parts = unfold(
        finish(cuts, [links[0], links[-1]]), [2] * len(narrow_bits) + [chunk // 2, COLUMNS]
    )
    mlp_parts = [(value, dims + narrow_bits[::-1]) for value, dims in mlp_parts]
    for turn in range(1, len(links)):
        labels = [links[turn], links[-1 - turn]]
        cuts = start(mlp_parts, labels)
        if turn == len(links) - 1:
            (hot_cut,) = start([hot], [core_bit])
            sends = gate([cut[0] for cut in cuts] + [hot_cut[0]], late_sends)
            cuts = [(send, cut[1], cut[2]) for send, cut in zip(sends, cuts)]
            (hot,) = finish([(sends[2], hot_cut[1], hot_cut[2])], [core_bit])
        mlp_parts = finish(cuts, labels)

    cold_keep, cold_send = add_rows(core, got_values, share, wide, COLD_ROWS_DEV)
    labels = [low, low, links[0]]
    ready = start(mlp_parts + [hot], labels)
    cold_send, *sends = gate([cold_send] + [cut[0] for cut in ready])
    ready = [(send, cut[1], cut[2]) for send, cut in zip(sends, ready)]
    mlp_first, mlp_second, hot = finish(ready, labels)
    for label in links[1:]:
        hot = halve(hot, label)
    cuts = first_cuts(cold_keep, flip(cold_send, *core_bit))
    half = D // 2
    parts = []
    for turn in range(len(links)):
        labels = [links[turn], links[-1 - turn]]
        last = turn == len(links) - 1
        if turn == 0:
            labels = labels + [high, high, low]
            *parts, mlp_first, mlp_second, hot = finish(
                ordered(cuts + start([mlp_first, mlp_second, hot], labels[2:])), labels
            )
            parts = unfold(parts, [share, half, COLD_ROWS_DEV])
        elif last:
            ready = start(parts, labels)
            *sends, hot_value = gate([cut[0] for cut in ready] + [hot[0]])
            ready = [(send, cut[1], cut[2]) for send, cut in zip(sends, ready)]
            hot_value = hot_value + flip(hot_value, *high)
            parts = finish(ready, labels)
        else:
            parts = finish(ordered(start(parts, labels)), labels)
    mlp_parts = [mlp_first, mlp_second]

    cold_grad = jnp.zeros((narrow, share, D, COLD_ROWS_DEV), jnp.float32)
    moving = jnp.concatenate([parts[0][0], parts[1][0]], axis=1)
    joins = [[low], links[-1:]] + [[]] * (narrow - 4) + [links[-2::-1]]
    for step in range(narrow):
        cold_grad = lax.dynamic_update_index_in_dim(cold_grad, moving, (here - step) % narrow, 0)
        if step == narrow - 1:
            break
        after = [] if step else [value for value, _ in mlp_parts]
        moving, hot_value = gate([moving, hot_value], after)
        moving = go_round(moving, 1)
        for label in joins[step]:
            hot_value = join(hot_value, label)
    (hot_value,) = gate([hot_value], [moving])
    shared = join(hot_value, core_bit).reshape(-1, LANES)
    cold_grad = jnp.transpose(
        cold_grad.reshape(COLD_TABLES, D, COLD_ROWS_DEV), (0, 2, 1)
    )
    hot_grad = jnp.transpose(shared[:hot_rows].reshape(HOT_TABLES, D, HOT_ROWS), (0, 2, 1))
    small = shared[hot_rows:].reshape(-1)
    n_proj, n_compress = TABLES * RANK, LC_OUT * TABLES
    grad_proj = small[:n_proj].reshape(TABLES, RANK)
    compress_gradient = small[n_proj : n_proj + n_compress].reshape(LC_OUT, TABLES)
    grad_gain = small[n_proj + n_compress : n_proj + n_compress + D]

    done = jnp.concatenate([value for value, _ in mlp_parts], axis=0)
    own_second, own_first = w_first.shape[1] // devices, TABLES * RANK // devices
    cut = own_second * FM_OUT * D // COLUMNS

    def side_by_side(blocks, rows):
        return jnp.transpose(blocks.reshape(-1, rows, COLUMNS), (1, 0, 2)).reshape(rows, -1)

    grad_second = side_by_side(done[:cut], own_second)
    grad_first = side_by_side(done[cut:], own_first)
    return (grad_first, grad_second, grad_proj, compress_gradient, grad_gain, hot_grad, cold_grad)


def solution(mesh):
    placed = (
        P(("wide", "narrow"), None, None),
        P(("wide", "narrow"), None, None),
        P(),
        P(),
        P(),
        P(),
        P(),
        P(("wide", "narrow"), None),
        P(("wide", "narrow"), None),
        P(("wide", "narrow"), None, None),
    )
    return jax.shard_map(
        local,
        mesh=mesh,
        in_specs=placed,
        out_specs=(
            P(("wide", "narrow"), None),
            P(("wide", "narrow"), None),
            P(),
            P(),
            P(),
            P(),
            P(None, "wide", None),
        ),
        check_vma=False,
    )
```

```python
import functools

import jax
import jax.numpy as jnp
from jax import lax
from jax.experimental import pallas as pl
from jax.experimental.pallas import tpu as pltpu
from jax.sharding import PartitionSpec as P

D = 192
RANK = 16
HOT_TABLES = 16
COLD_TABLES = 16
FM_OUT = 8
LC_OUT = 8
HOT_ROWS = 128
COLD_ROWS_DEV = 256
TABLES = 32
LANES = 128
COLUMNS = 512
ID_ROWS = 8
SENDS = 2
DENSE_COST = 12000000000


NT = (((1,), (1,)), ((), ()))
NN = (((1,), (0,)), ((), ()))
GROUP = 16
OCTET = 8
VMEM = 60 * 1024 * 1024


def mm(a, b, dims=NN):
    return lax.dot_general(a, b, dims, preferred_element_type=jnp.float32)


def iota(shape, dim):
    return lax.broadcasted_iota(jnp.int32, shape, dim)


def ones_where(mask):
    return mask.astype(jnp.float32).astype(jnp.bfloat16)


def eye(size):
    return ones_where(iota((size, size), 0) == iota((size, size), 1))


def same_sample(rows, columns):
    return ones_where(
        lax.rem(iota((rows, columns), 0), GROUP) == lax.rem(iota((rows, columns), 1), GROUP)
    )


def spread_rows(count):
    return ones_where(
        lax.div(iota((count * GROUP, count), 0), GROUP) == iota((count * GROUP, count), 1)
    )


def spread_columns(count):
    return ones_where(
        lax.div(iota((count, count * GROUP), 1), GROUP) == iota((count, count * GROUP), 0)
    )


def expand(matrix):
    rows, columns = matrix.shape
    tall = mm(spread_rows(rows), matrix).astype(jnp.bfloat16)
    full = mm(tall, spread_columns(columns)).astype(jnp.bfloat16)
    return full * same_sample(rows * GROUP, columns * GROUP)


def expand_t(matrix):
    rows, columns = matrix.shape
    tall = mm(spread_rows(columns), matrix, NT).astype(jnp.bfloat16)
    full = mm(tall, spread_columns(rows)).astype(jnp.bfloat16)
    return full * same_sample(columns * GROUP, rows * GROUP)


def pick_rank():
    shape = (RANK * GROUP, OCTET * RANK)
    return ones_where(lax.div(iota(shape, 0), GROUP) == lax.rem(iota(shape, 1), RANK))


def same_table():
    shape = (OCTET * GROUP, OCTET * RANK)
    return ones_where(lax.div(iota(shape, 0), GROUP) == lax.div(iota(shape, 1), RANK))


def mlp_kernel(
    wide,
    core,
    x,
    up,
    proj,
    w_first,
    w_second,
    comp,
    gain,
    keep,
    send,
    xs,
    inner,
    d_pair,
    d_lc,
    grad_gain,
    flat,
    flat_t,
    hidden,
    hidden_t,
    slope,
    lc_out,
    d_fm,
    d_pre,
):
    step = pl.program_id(0)
    samples = x.shape[2]
    hidden_size = w_first.shape[1]
    groups = samples // GROUP

    @pl.when(step == 0)
    def _():
        unit = eye(samples)
        for n in range(TABLES):
            xs[n] = mm(unit, x[n], NT).astype(jnp.bfloat16)
        comp_rows = expand(comp[...])
        for b in range(D // GROUP):
            block = x[:, GROUP * b : GROUP * (b + 1), :].reshape(TABLES * GROUP, samples)
            lc_out[:, GROUP * b : GROUP * (b + 1), :] = mm(comp_rows, block).reshape(
                LC_OUT, GROUP, samples
            )
        proj_t = expand_t(proj[...])
        samples_match = same_sample(TABLES * GROUP, RANK * GROUP).astype(jnp.float32)
        rank_of = pick_rank()
        table_match = same_table().astype(jnp.float32)

        def group(g, carry):
            rows = pl.ds(pl.multiple_of(g * GROUP, GROUP), GROUP)
            xg = xs[:, rows, :].reshape(TABLES * GROUP, D)
            inner_g = mm(proj_t, xg).astype(jnp.bfloat16)
            inner[:, rows, :] = inner_g.reshape(RANK, GROUP, D)
            pair = (mm(xg, inner_g, NT) * samples_match).astype(jnp.bfloat16)
            for j in range(TABLES // OCTET):
                part = pair[OCTET * GROUP * j : OCTET * GROUP * (j + 1)]
                wide_part = mm(part, rank_of) * table_match
                flat[rows, OCTET * RANK * j : OCTET * RANK * (j + 1)] = jnp.sum(
                    wide_part.reshape(OCTET, GROUP, OCTET * RANK), axis=0
                ).astype(jnp.bfloat16)
            return carry

        lax.fori_loop(0, groups, group, 0, unroll=2)
        pairs = flat.shape[1]
        block = 256
        unit_b = eye(block)
        for b in range(pairs // block):
            at = slice(block * b, block * (b + 1))
            flat_t[at] = mm(unit_b, flat[:, at], NT).astype(jnp.bfloat16)
        for b in range(hidden_size // block):
            at = slice(block * b, block * (b + 1))
            pre = mm(flat[...], w_first[:, at])
            sigmoid_v = 1.0 / (1.0 + jnp.exp(-pre))
            slope[:, at] = sigmoid_v * (1.0 + pre * (1.0 - sigmoid_v))
            hidden_b = (pre * sigmoid_v).astype(jnp.bfloat16)
            hidden[:, at] = hidden_b
            hidden_t[at] = mm(unit_b, hidden_b, NT).astype(jnp.bfloat16)
        gain_column = jnp.sum(
            jnp.where(iota((D, D), 0) == iota((D, D), 1), gain[...], 0.0), axis=1, keepdims=True
        )
        scale = 1.0 / D
        gain_sum = jnp.zeros((D, samples), jnp.float32)

        def norm(joined, o, gain_sum):
            mean = jnp.sum(joined, axis=0, keepdims=True) * scale
            centered = joined - mean
            variance = jnp.sum(centered * centered, axis=0, keepdims=True) * scale
            inv_std = lax.rsqrt(variance + 1e-05)
            normed = centered * inv_std
            cotangent = up[o].astype(jnp.float32)
            gain_sum = gain_sum + cotangent * normed
            d_norm = cotangent * gain_column
            mean_d = jnp.sum(d_norm, axis=0, keepdims=True) * scale
            mean_n = jnp.sum(d_norm * normed, axis=0, keepdims=True) * scale
            return (inv_std * (d_norm - mean_d - normed * mean_n)).astype(jnp.bfloat16), gain_sum

        for c in range(FM_OUT // 2):
            at = slice(2 * D * c, 2 * D * (c + 1))
            fm_t = mm(hidden[...], w_second[:, at]).T
            low, gain_sum = norm(fm_t[:D], 2 * c, gain_sum)
            high, gain_sum = norm(fm_t[D:], 2 * c + 1, gain_sum)
            both = jnp.concatenate([low, high], axis=0)
            d_fm[:, at] = mm(unit, both, NT).astype(jnp.bfloat16)
        for o in range(LC_OUT):
            d_joined, gain_sum = norm(lc_out[o], FM_OUT + o, gain_sum)
            d_lc[o] = mm(unit, d_joined, NT).astype(jnp.bfloat16)
        gain_row = jnp.sum(gain_sum, axis=1, keepdims=True)
        grad_gain[...] = jnp.broadcast_to(gain_row, grad_gain.shape)
        for b in range(hidden_size // block):
            at = slice(block * b, block * (b + 1))
            d_pre[:, at] = (mm(d_fm[...], w_second[at], NT) * slope[:, at]).astype(jnp.bfloat16)
        d_pair[...] = mm(d_pre[...], w_first[...], NT).astype(jnp.bfloat16)

    mine = core[0]
    narrow = keep.shape[1]
    second_rows = hidden_t.shape[0] // wide
    first_rows = flat_t.shape[0] // wide
    own_second, own_first = second_rows // narrow, first_rows // narrow
    second_cuts, first_cuts = d_fm.shape[1] // COLUMNS, hidden_size // COLUMNS
    for which, out in ((1 - mine, send), (mine, keep)):
        w = 2 * step + which
        rows = pl.ds(pl.multiple_of(w * second_rows, second_rows), second_rows)
        for c in range(second_cuts):
            part = mm(hidden_t[rows], d_fm[:, COLUMNS * c : COLUMNS * (c + 1)])
            out[0, :, own_second * c : own_second * (c + 1), :] = part.reshape(
                narrow, own_second, COLUMNS
            )
        rows = pl.ds(pl.multiple_of(w * first_rows, first_rows), first_rows)
        for c in range(first_cuts):
            part = mm(flat_t[rows], d_pre[:, COLUMNS * c : COLUMNS * (c + 1)])
            at = own_second * second_cuts + own_first * c
            out[0, :, at : at + own_first, :] = part.reshape(narrow, own_first, COLUMNS)


def whole(shape):
    zeros = (0,) * len(shape)
    return pl.BlockSpec(shape, lambda j, c: zeros, pipeline_mode=pl.Buffered(1))


def mlp(core, x, up, proj, w_first, w_second, comp, gain, wide, narrow):
    samples = x.shape[2]
    pairs, hidden_size = w_first.shape
    outs = w_second.shape[1]
    half = wide // 2
    chunk = (w_first.size + w_second.size) // (wide * narrow * COLUMNS)
    sums = jax.ShapeDtypeStruct((half, narrow, chunk, COLUMNS), jnp.float32)
    rest = [
        jax.ShapeDtypeStruct((TABLES, samples, D), jnp.bfloat16),
        jax.ShapeDtypeStruct((RANK, samples, D), jnp.bfloat16),
        jax.ShapeDtypeStruct((samples, pairs), jnp.bfloat16),
        jax.ShapeDtypeStruct((LC_OUT, samples, D), jnp.bfloat16),
        jax.ShapeDtypeStruct((D, LANES), jnp.float32),
    ]

    def by_step(shape):
        return pl.BlockSpec((1,) + shape.shape[1:], lambda j, c: (j, 0, 0, 0))

    bf16, f32 = jnp.bfloat16, jnp.float32
    return pl.pallas_call(
        functools.partial(mlp_kernel, wide),
        grid_spec=pltpu.PrefetchScalarGridSpec(
            num_scalar_prefetch=1,
            grid=(half,),
            in_specs=[whole(a.shape) for a in (x, up, proj, w_first, w_second, comp, gain)],
            out_specs=[by_step(sums)] * 2 + [whole(r.shape) for r in rest],
            scratch_shapes=[
                pltpu.VMEM((samples, pairs), bf16),
                pltpu.VMEM((pairs, samples), bf16),
                pltpu.VMEM((samples, hidden_size), bf16),
                pltpu.VMEM((hidden_size, samples), bf16),
                pltpu.VMEM((samples, hidden_size), f32),
                pltpu.VMEM((LC_OUT, D, samples), f32),
                pltpu.VMEM((samples, outs), bf16),
                pltpu.VMEM((samples, hidden_size), bf16),
            ],
        ),
        out_shape=[sums, sums] + rest,
        compiler_params=pltpu.CompilerParams(vmem_limit_bytes=VMEM),
        cost_estimate=pl.CostEstimate(
            flops=16_000_000_000, bytes_accessed=32_000_000, transcendentals=600_000
        ),
    )(core, x, up, proj, w_first, w_second, comp, gain)


def rows_kernel(
    narrow, here, xs, inner, d_pair, d_lc, proj, comp, hot_ids, cold_ids, *refs
):
    colds, (hot, sums, d_rows, totals) = refs[:narrow], refs[narrow:]
    samples = xs.shape[1]
    share = COLD_TABLES // narrow
    proj_rows, comp_rows = expand(proj[...]), expand_t(comp[...])
    match = same_sample(OCTET * GROUP, RANK * GROUP)
    match_t = same_sample(RANK * GROUP, OCTET * GROUP)
    rank_of, table_match = pick_rank(), same_table()
    totals[...] = jnp.zeros_like(totals)

    def group(g, carry):
        rows = pl.ds(pl.multiple_of(g * GROUP, GROUP), GROUP)
        xg = xs[:, rows, :].reshape(TABLES * GROUP, D)
        inner_g = inner[:, rows, :].reshape(RANK * GROUP, D)
        d_lc_g = d_lc[:, rows, :].reshape(LC_OUT * GROUP, D)
        parts, parts_t = [], []
        for j in range(TABLES // OCTET):
            own = d_pair[rows, OCTET * RANK * j : OCTET * RANK * (j + 1)]
            spread = jnp.concatenate([own] * OCTET, axis=0) * table_match
            parts.append(mm(spread, rank_of, NT).astype(jnp.bfloat16) * match)
            parts_t.append(mm(rank_of, spread, NT).astype(jnp.bfloat16) * match_t)
        d_pairs = jnp.concatenate(parts, axis=0)
        d_pairs_t = jnp.concatenate(parts_t, axis=1)
        d_inner = mm(d_pairs_t, xg).astype(jnp.bfloat16)
        d_embed = mm(d_pairs, inner_g) + mm(proj_rows, d_inner) + mm(comp_rows, d_lc_g)
        d_rows[:, rows, :] = d_embed.astype(jnp.bfloat16).reshape(TABLES, GROUP, D)
        totals[...] += mm(jnp.concatenate([d_inner, d_lc_g], axis=0), xg, NT)
        return carry

    lax.fori_loop(0, samples // GROUP, group, 0, unroll=2)
    unit = eye(D)
    for step in range(narrow):
        target = lax.rem(here[0] + step, narrow)
        for i in range(share):
            colds[step][D * i : D * (i + 1)] = mm(
                unit, d_rows[HOT_TABLES + target * share + i], NT
            )
        for i in range(ID_ROWS):
            colds[step][D * share + i : D * share + i + 1] = cold_ids[
                pl.ds(target * share + min(i, share - 1), 1)
            ]
    for t in range(HOT_TABLES):
        values = mm(unit, d_rows[t], NT).astype(jnp.bfloat16)
        onehot = ones_where(iota((HOT_ROWS, samples), 0) == hot_ids[t : t + 1, :])
        hot[t] = mm(values, onehot, NT)
    sums_shape = totals.shape
    own = lax.rem(iota(sums_shape, 0), GROUP) == lax.rem(iota(sums_shape, 1), GROUP)
    masked = jnp.where(own, totals[...], 0.0)
    folded = jnp.sum(masked.reshape(RANK + LC_OUT, GROUP, sums_shape[1]), axis=1)
    sums[...] = lax.dot_general(
        folded,
        spread_rows(TABLES).astype(jnp.float32),
        NN,
        precision=lax.Precision.HIGHEST,
        preferred_element_type=jnp.float32,
    )


def row_gradients(here, xs, inner, d_pair, d_lc, proj, comp, hot_ids, cold_ids, narrow, part, parts):
    samples = xs.shape[1] // parts
    share = COLD_TABLES // narrow

    def middle(count):
        return pl.BlockSpec((count, samples, D), lambda i: (0, part, 0))

    def last(count):
        return pl.BlockSpec((count, samples), lambda i: (0, part))

    def full(*shape):
        zeros = (0,) * len(shape)
        return pl.BlockSpec(shape, lambda i: zeros)

    shapes = [(share * D + ID_ROWS, samples)] * narrow
    shapes += [(HOT_TABLES, D, HOT_ROWS), (RANK + LC_OUT, TABLES)]
    return pl.pallas_call(
        functools.partial(rows_kernel, narrow),
        grid=(1,),
        in_specs=[
            pl.BlockSpec(memory_space=pltpu.SMEM),
            middle(TABLES),
            middle(RANK),
            pl.BlockSpec((samples, TABLES * RANK), lambda i: (part, 0)),
            middle(LC_OUT),
            full(*proj.shape),
            full(*comp.shape),
            last(HOT_TABLES),
            last(COLD_TABLES),
        ],
        out_specs=[full(*shape) for shape in shapes],
        out_shape=[jax.ShapeDtypeStruct(shape, jnp.float32) for shape in shapes],
        scratch_shapes=[
            pltpu.VMEM((TABLES, samples, D), jnp.bfloat16),
            pltpu.VMEM(((RANK + LC_OUT) * GROUP, TABLES * GROUP), jnp.float32),
        ],
        compiler_params=pltpu.CompilerParams(vmem_limit_bytes=VMEM),
        cost_estimate=pl.CostEstimate(
            flops=1, bytes_accessed=1, transcendentals=0
        ),
    )(here, xs, inner, d_pair, d_lc, proj, comp, hot_ids, cold_ids)


def bits_of(axis):
    return (lax.axis_size(axis) - 1).bit_length()


def flip(value, axis, bit):
    return lax.ppermute(value, axis, [(i, i ^ (1 << bit)) for i in range(lax.axis_size(axis))])


def my_bit(axis, bit):
    return (lax.axis_index(axis) >> bit) & 1


def split(value, dims, label):
    dim = dims.index(label)
    me = my_bit(*label)
    send = lax.dynamic_index_in_dim(value, 1 - me, dim, keepdims=False)
    keep = lax.dynamic_index_in_dim(value, me, dim, keepdims=False)
    return send, keep, dims[:dim] + dims[dim + 1 :]


def join(value, label):
    got = flip(value, *label)
    me = my_bit(*label)
    return jnp.stack([jnp.where(me == 0, value, got), jnp.where(me == 0, got, value)], axis=0)


def nothing(*refs):
    pass


def gate(values, after=()):
    values, after = list(values), list(after)
    return list(
        pl.pallas_call(
        nothing,
        in_specs=[pl.BlockSpec(memory_space=pl.ANY)] * (len(values) + len(after)),
        out_specs=[pl.BlockSpec(memory_space=pl.ANY)] * len(values),
        out_shape=[jax.ShapeDtypeStruct(v.shape, v.dtype) for v in values],
        input_output_aliases={i: i for i in range(len(values))},
    )(*values, *after)
    )


def start(parts, labels):
    return [split(value, dims, label) for (value, dims), label in zip(parts, labels)]


def finish(cuts, labels):
    return [(keep + flip(send, *label), dims) for (send, keep, dims), label in zip(cuts, labels)]


def ordered(cuts, after=()):
    sends = gate([cut[0] for cut in cuts], after)
    return [(send, cut[1], cut[2]) for send, cut in zip(sends, cuts)]


def combine_kernel(cuts, bits, *refs):
    ins, outs = refs[: 8 * cuts], refs[8 * cuts :]
    for i, out in enumerate(outs):
        rows = out.shape[2] // cuts
        for u in range(cuts):
            keep, got = ins[2 * (cuts * i + u)], ins[2 * (cuts * i + u) + 1]
            out[:, :, rows * u : rows * (u + 1), :] = keep[...] + got[...]


def combine(bits, keep, got):
    blocks, n, rows, columns = keep.shape
    half = blocks // 2
    cuts = max(1, len(got) // 2)
    shape = (1, n, rows // (2 * cuts), columns)

    def spec(piece, other, at):
        if piece == 0:
            return pl.BlockSpec(shape, lambda i, b: (2 * i + (b[0] ^ other), 0, at, 0))
        return pl.BlockSpec(shape, lambda i, b: (half * (b[1] ^ other) + i, 0, at, 0))

    specs, operands = [], []
    for piece in (0, 1):
        for other in (1, 0):
            for at in range(piece * cuts, (piece + 1) * cuts):
                specs += [spec(piece, other, at), spec(piece, other, 0 if len(got) > 1 else at)]
                operands += [keep, got[at] if len(got) > 1 else got[0]]
    out = jax.ShapeDtypeStruct((half, n, rows // 2, columns), keep.dtype)
    return pl.pallas_call(
        functools.partial(combine_kernel, cuts),
        grid_spec=pltpu.PrefetchScalarGridSpec(
            num_scalar_prefetch=1,
            grid=(half,),
            in_specs=specs,
            out_specs=[pl.BlockSpec((1, n, rows // 2, columns), lambda i, b: (i, 0, 0, 0))] * 4,
        ),
        out_shape=[out] * 4,
        compiler_params=pltpu.CompilerParams(vmem_limit_bytes=VMEM),
        cost_estimate=pl.CostEstimate(
            flops=keep.size, bytes_accessed=12 * keep.size, transcendentals=0
        ),
    )(bits, *operands)


def add_rows_kernel(rows, parts, core, *refs):
    ids, values, keep, sends = refs[:parts], refs[parts : 2 * parts], refs[2 * parts], refs[2 * parts + 1 :]
    table = pl.program_id(0)
    numbers = jnp.concatenate([r[pl.ds(table, 1)] for r in ids], axis=1).astype(jnp.int32)
    owners, at = lax.div(numbers, rows), lax.rem(numbers, rows)
    values = jnp.concatenate([r[...].astype(jnp.bfloat16) for r in values], axis=1)
    onehot = ones_where(iota((rows, numbers.shape[1]), 0) == at)
    for which, outs in ((1 - core[0], sends), (core[0], [keep])):
        for b in range(keep.shape[0]):
            sums = mm(values * ones_where(owners == 2 * b + which), onehot, NT)
            size = D // len(outs)
            for i, out in enumerate(outs):
                out[b, 0] = sums[size * i : size * (i + 1)]


def add_rows(core, values, tables, blocks, rows):
    samples = values[0].shape[1]
    parts = len(values)
    out = jax.ShapeDtypeStruct((blocks // 2, tables, D, rows), jnp.float32)
    piece = jax.ShapeDtypeStruct((blocks // 2, tables, D // SENDS, rows), jnp.float32)
    return pl.pallas_call(
        functools.partial(add_rows_kernel, rows, parts),
        grid_spec=pltpu.PrefetchScalarGridSpec(
            num_scalar_prefetch=1,
            grid=(tables,),
            in_specs=[
                pl.BlockSpec((ID_ROWS, samples), lambda t, c: (tables * D // ID_ROWS, 0))
            ]
            * parts
            + [pl.BlockSpec((D, samples), lambda t, c: (t, 0))] * parts,
            out_specs=[pl.BlockSpec((blocks // 2, 1, D, rows), lambda t, c: (0, t, 0, 0))]
            + [pl.BlockSpec((blocks // 2, 1, D // SENDS, rows), lambda t, c: (0, t, 0, 0))] * SENDS,
        ),
        out_shape=[out] + [piece] * SENDS,
        compiler_params=pltpu.CompilerParams(vmem_limit_bytes=VMEM),
        cost_estimate=pl.CostEstimate(
            flops=DENSE_COST, bytes_accessed=1, transcendentals=0
        ),
    )(core, *values, *values)


def local(
    embeddings,
    upstream,
    factor_machine_projection,
    w_first,
    w_second,
    compress,
    norm_gain,
    hot_index,
    cold_row,
    cold_owner,
):
    wide, narrow = lax.axis_size("wide"), lax.axis_size("narrow")
    devices = wide * narrow
    wide_bits = [("wide", b) for b in range(bits_of("wide"))]
    narrow_bits = [("narrow", b) for b in range(bits_of("narrow"))]
    core_bit, links = wide_bits[0], wide_bits[1:]
    left_dims = links[::-1] + narrow_bits[::-1]

    sample_count = embeddings.shape[0]
    here = lax.axis_index("narrow")
    x = jnp.transpose(embeddings, (1, 2, 0))
    up = jnp.transpose(upstream, (1, 2, 0))
    core = my_bit("wide", 0).reshape(1)
    mlp_keep, mlp_send, xs, inner, d_pair, d_lc, gain_sum = mlp(
        core,
        x,
        up,
        factor_machine_projection,
        w_first,
        w_second,
        compress,
        norm_gain.reshape(1, D),
        wide,
        narrow,
    )
    cold_ids = (cold_owner[:, :, 0] * COLD_ROWS_DEV + cold_row).T.astype(jnp.float32)

    def rows_of(part, d_pair):
        *values, hot_sums, sums = row_gradients(
            here.reshape(1),
            xs,
            inner,
            d_pair,
            d_lc,
            factor_machine_projection,
            compress,
            hot_index.T,
            cold_ids,
            narrow,
            part,
            2,
        )
        return values, hot_sums, sums

    share = COLD_TABLES // narrow
    low, high = narrow_bits
    link_bits = jnp.stack([my_bit(*links[0]), my_bit(*links[-1])])

    def go_round(value, step):
        return lax.ppermute(value, "narrow", [(i, (i + step) % narrow) for i in range(narrow)])

    def halve(part, label):
        (part,) = finish(start([part], [label]), [label])
        return part

    def first_cuts(keep, got):
        a_send, a_keep, b_send, b_keep = combine(link_bits, keep, got)
        dims = links[::-1]
        return [
            (a_send, a_keep, dims[:-1]),
            (b_send, b_keep, dims[1:]),
        ]

    def unfold(parts, tail):
        return [(value.reshape([2] * len(dims) + tail), dims) for value, dims in parts]

    early, hot_early, sums_early = rows_of(0, d_pair)
    got_early = [go_round(value, step) for step, value in enumerate(early) if step]
    (mlp_got,) = gate([flip(mlp_send, *core_bit)], early[:1])
    chunk = mlp_keep.shape[2]
    cuts = first_cuts(mlp_keep, [mlp_got])
    (d_pair_late,) = gate([d_pair], [cuts[0][0]])
    late, hot_late, sums_late = rows_of(1, d_pair_late)

    sums = sums_early + sums_late
    grad_proj, compress_gradient = sums[:RANK].T, sums[RANK:]
    hot_local = hot_early + hot_late
    hot_rows = hot_local.size // LANES
    small = jnp.concatenate([grad_proj.reshape(-1), compress_gradient.reshape(-1), gain_sum[:, 0]])
    small = jnp.pad(small, (0, -small.size % LANES)).reshape(-1, LANES)
    shared = jnp.concatenate([hot_local.reshape(hot_rows, LANES), small], axis=0)
    shared = jnp.pad(shared, ((0, -shared.shape[0] % (8 * devices)), (0, 0)))
    hot_order = [core_bit] + links + [low]
    hot = (shared.reshape([2] * len(hot_order) + [-1, LANES]), hot_order)

    late_sends = gate(late[1:], got_early)
    got_late = [go_round(value, step + 1) for step, value in enumerate(late_sends)]
    got_values = early[:1] + got_early + late[:1] + got_late
    mlp_parts = unfold(
        finish(cuts, [links[0], links[-1]]), [2] * len(narrow_bits) + [chunk // 2, COLUMNS]
    )
    mlp_parts = [(value, dims + narrow_bits[::-1]) for value, dims in mlp_parts]
    for turn in range(1, len(links)):
        labels = [links[turn], links[-1 - turn]]
        cuts = start(mlp_parts, labels)
        if turn == len(links) - 1:
            (hot_cut,) = start([hot], [core_bit])
            sends = gate([cut[0] for cut in cuts] + [hot_cut[0]], late_sends)
            cuts = [(send, cut[1], cut[2]) for send, cut in zip(sends, cuts)]
            (hot,) = finish([(sends[2], hot_cut[1], hot_cut[2])], [core_bit])
        mlp_parts = finish(cuts, labels)

    cold_keep, *cold_sends = add_rows(core, got_values, share, wide, COLD_ROWS_DEV)
    labels = [low, links[0]]
    both = start(mlp_parts, [low, low])
    mlp_dims = both[0][2]
    mlp_cut = [jnp.concatenate([cut[i] for cut in both], axis=len(mlp_dims)) for i in range(2)]
    ready = [(*mlp_cut, mlp_dims)] + start([hot], labels[1:])
    sends = gate(cold_sends + [cut[0] for cut in ready])
    cold_sends = sends[:SENDS]
    ready = [(send, cut[1], cut[2]) for send, cut in zip(sends[SENDS:], ready)]
    mlp_part, hot = finish(ready, labels)
    for label in links[1:]:
        hot = halve(hot, label)
    cuts = first_cuts(cold_keep, [flip(send, *core_bit) for send in cold_sends])
    half = D // 2
    parts = []
    for turn in range(len(links)):
        labels = [links[turn], links[-1 - turn]]
        last = turn == len(links) - 1
        if turn == 0:
            labels = labels + [low]
            ready = ordered(cuts + start([hot], labels[2:]))
            *parts, hot = finish(ready, labels)
            parts = unfold(parts, [share, half, COLD_ROWS_DEV])
            ready = ordered(start([mlp_part], [high]), [cut[0] for cut in ready])
            (mlp_part,) = finish(ready, [high])
        elif last:
            ready = start(parts, labels)
            *sends, hot_value = gate([cut[0] for cut in ready] + [hot[0]])
            ready = [(send, cut[1], cut[2]) for send, cut in zip(sends, ready)]
            hot_value = hot_value + flip(hot_value, *high)
            parts = finish(ready, labels)
        else:
            parts = finish(ordered(start(parts, labels)), labels)

    cold_grad = jnp.zeros((narrow, share, D, COLD_ROWS_DEV), jnp.float32)
    moving = jnp.concatenate([parts[0][0], parts[1][0]], axis=1)
    joins = [[low], links[-1:]] + [[]] * (narrow - 4) + [links[-2::-1]]
    for step in range(narrow):
        cold_grad = lax.dynamic_update_index_in_dim(cold_grad, moving, (here - step) % narrow, 0)
        if step == narrow - 1:
            break
        after = [] if step else [mlp_part[0]]
        moving, hot_value = gate([moving, hot_value], after)
        moving = go_round(moving, 1)
        for label in joins[step]:
            hot_value = join(hot_value, label)
    (hot_value,) = gate([hot_value], [moving])
    shared = join(hot_value, core_bit).reshape(-1, LANES)
    cold_grad = jnp.transpose(
        cold_grad.reshape(COLD_TABLES, D, COLD_ROWS_DEV), (0, 2, 1)
    )
    hot_grad = jnp.transpose(shared[:hot_rows].reshape(HOT_TABLES, D, HOT_ROWS), (0, 2, 1))
    small = shared[hot_rows:].reshape(-1)
    n_proj, n_compress = TABLES * RANK, LC_OUT * TABLES
    grad_proj = small[:n_proj].reshape(TABLES, RANK)
    compress_gradient = small[n_proj : n_proj + n_compress].reshape(LC_OUT, TABLES)
    grad_gain = small[n_proj + n_compress : n_proj + n_compress + D]

    done = mlp_part[0]
    own_second, own_first = w_first.shape[1] // devices, TABLES * RANK // devices
    cut = own_second * FM_OUT * D // COLUMNS

    def side_by_side(blocks, rows):
        return jnp.transpose(blocks.reshape(-1, rows, COLUMNS), (1, 0, 2)).reshape(rows, -1)

    grad_second = side_by_side(done[:cut], own_second)
    grad_first = side_by_side(done[cut:], own_first)
    return (grad_first, grad_second, grad_proj, compress_gradient, grad_gain, hot_grad, cold_grad)


def solution(mesh):
    placed = (
        P(("wide", "narrow"), None, None),
        P(("wide", "narrow"), None, None),
        P(),
        P(),
        P(),
        P(),
        P(),
        P(("wide", "narrow"), None),
        P(("wide", "narrow"), None),
        P(("wide", "narrow"), None, None),
    )
    return jax.shard_map(
        local,
        mesh=mesh,
        in_specs=placed,
        out_specs=(
            P(("wide", "narrow"), None),
            P(("wide", "narrow"), None),
            P(),
            P(),
            P(),
            P(),
            P(None, "wide", None),
        ),
        check_vma=False,
    )
```

```python
import functools

import jax
import jax.numpy as jnp
from jax import lax
from jax.experimental import pallas as pl
from jax.experimental.pallas import tpu as pltpu
from jax.sharding import PartitionSpec as P

D = 192
RANK = 16
HOT_TABLES = 16
COLD_TABLES = 16
FM_OUT = 8
LC_OUT = 8
HOT_ROWS = 128
COLD_ROWS_DEV = 256
TABLES = 32
LANES = 128
COLUMNS = 512
ID_ROWS = 8
SENDS = 2
DENSE_COST = 12000000000


NT = (((1,), (1,)), ((), ()))
NN = (((1,), (0,)), ((), ()))
GROUP = 16
OCTET = 8
VMEM = 60 * 1024 * 1024


def mm(a, b, dims=NN):
    return lax.dot_general(a, b, dims, preferred_element_type=jnp.float32)


def iota(shape, dim):
    return lax.broadcasted_iota(jnp.int32, shape, dim)


def ones_where(mask):
    return mask.astype(jnp.float32).astype(jnp.bfloat16)


def eye(size):
    return ones_where(iota((size, size), 0) == iota((size, size), 1))


def same_sample(rows, columns):
    return ones_where(
        lax.rem(iota((rows, columns), 0), GROUP) == lax.rem(iota((rows, columns), 1), GROUP)
    )


def spread_rows(count):
    return ones_where(
        lax.div(iota((count * GROUP, count), 0), GROUP) == iota((count * GROUP, count), 1)
    )


def spread_columns(count):
    return ones_where(
        lax.div(iota((count, count * GROUP), 1), GROUP) == iota((count, count * GROUP), 0)
    )


def expand(matrix):
    rows, columns = matrix.shape
    tall = mm(spread_rows(rows), matrix).astype(jnp.bfloat16)
    full = mm(tall, spread_columns(columns)).astype(jnp.bfloat16)
    return full * same_sample(rows * GROUP, columns * GROUP)


def expand_t(matrix):
    rows, columns = matrix.shape
    tall = mm(spread_rows(columns), matrix, NT).astype(jnp.bfloat16)
    full = mm(tall, spread_columns(rows)).astype(jnp.bfloat16)
    return full * same_sample(columns * GROUP, rows * GROUP)


def pick_rank():
    shape = (RANK * GROUP, OCTET * RANK)
    return ones_where(lax.div(iota(shape, 0), GROUP) == lax.rem(iota(shape, 1), RANK))


def same_table():
    shape = (OCTET * GROUP, OCTET * RANK)
    return ones_where(lax.div(iota(shape, 0), GROUP) == lax.div(iota(shape, 1), RANK))


def mlp_kernel(
    wide,
    core,
    x,
    up,
    proj,
    w_first_in,
    w_second_in,
    comp,
    gain,
    keep,
    send,
    xs,
    inner,
    d_pair,
    d_lc,
    grad_gain,
    flat,
    flat_t,
    hidden,
    hidden_t,
    slope,
    lc_out,
    d_fm,
    d_pre,
    w_first,
    w_second,
    arrived,
):
    step = pl.program_id(0)
    samples = x.shape[2]
    hidden_size = w_first.shape[1]
    groups = samples // GROUP

    @pl.when(step == 0)
    def _():
        first_copy = pltpu.make_async_copy(w_first_in, w_first, arrived.at[0])
        second_copy = pltpu.make_async_copy(w_second_in, w_second, arrived.at[1])
        first_copy.start()
        second_copy.start()
        unit = eye(samples)
        for n in range(TABLES):
            xs[n] = mm(unit, x[n], NT).astype(jnp.bfloat16)
        comp_rows = expand(comp[...])
        for b in range(D // GROUP):
            block = x[:, GROUP * b : GROUP * (b + 1), :].reshape(TABLES * GROUP, samples)
            lc_out[:, GROUP * b : GROUP * (b + 1), :] = mm(comp_rows, block).reshape(
                LC_OUT, GROUP, samples
            )
        proj_t = expand_t(proj[...])
        samples_match = same_sample(TABLES * GROUP, RANK * GROUP).astype(jnp.float32)
        rank_of = pick_rank()
        table_match = same_table().astype(jnp.float32)

        def group(g, carry):
            rows = pl.ds(pl.multiple_of(g * GROUP, GROUP), GROUP)
            xg = xs[:, rows, :].reshape(TABLES * GROUP, D)
            inner_g = mm(proj_t, xg).astype(jnp.bfloat16)
            inner[:, rows, :] = inner_g.reshape(RANK, GROUP, D)
            pair = (mm(xg, inner_g, NT) * samples_match).astype(jnp.bfloat16)
            for j in range(TABLES // OCTET):
                part = pair[OCTET * GROUP * j : OCTET * GROUP * (j + 1)]
                wide_part = mm(part, rank_of) * table_match
                flat[rows, OCTET * RANK * j : OCTET * RANK * (j + 1)] = jnp.sum(
                    wide_part.reshape(OCTET, GROUP, OCTET * RANK), axis=0
                ).astype(jnp.bfloat16)
            return carry

        lax.fori_loop(0, groups, group, 0, unroll=4)
        first_copy.wait()
        second_copy.wait()
        pairs = flat.shape[1]
        block = 256
        unit_b = eye(block)
        for b in range(pairs // block):
            at = slice(block * b, block * (b + 1))
            flat_t[at] = mm(unit_b, flat[:, at], NT).astype(jnp.bfloat16)
        for b in range(hidden_size // block):
            at = slice(block * b, block * (b + 1))
            pre = mm(flat[...], w_first[:, at])
            sigmoid_v = 1.0 / (1.0 + jnp.exp(-pre))
            slope[:, at] = sigmoid_v * (1.0 + pre * (1.0 - sigmoid_v))
            hidden_b = (pre * sigmoid_v).astype(jnp.bfloat16)
            hidden[:, at] = hidden_b
            hidden_t[at] = mm(unit_b, hidden_b, NT).astype(jnp.bfloat16)
        gain_column = jnp.sum(
            jnp.where(iota((D, D), 0) == iota((D, D), 1), gain[...], 0.0), axis=1, keepdims=True
        )
        scale = 1.0 / D
        gain_sum = jnp.zeros((D, samples), jnp.float32)

        def norm(joined, o, gain_sum):
            mean = jnp.sum(joined, axis=0, keepdims=True) * scale
            centered = joined - mean
            variance = jnp.sum(centered * centered, axis=0, keepdims=True) * scale
            inv_std = lax.rsqrt(variance + 1e-05)
            normed = centered * inv_std
            cotangent = up[o].astype(jnp.float32)
            gain_sum = gain_sum + cotangent * normed
            d_norm = cotangent * gain_column
            mean_d = jnp.sum(d_norm, axis=0, keepdims=True) * scale
            mean_n = jnp.sum(d_norm * normed, axis=0, keepdims=True) * scale
            return (inv_std * (d_norm - mean_d - normed * mean_n)).astype(jnp.bfloat16), gain_sum

        for c in range(FM_OUT // 2):
            at = slice(2 * D * c, 2 * D * (c + 1))
            fm_t = mm(hidden[...], w_second[:, at]).T
            low, gain_sum = norm(fm_t[:D], 2 * c, gain_sum)
            high, gain_sum = norm(fm_t[D:], 2 * c + 1, gain_sum)
            both = jnp.concatenate([low, high], axis=0)
            d_fm[:, at] = mm(unit, both, NT).astype(jnp.bfloat16)
        for o in range(LC_OUT):
            d_joined, gain_sum = norm(lc_out[o], FM_OUT + o, gain_sum)
            d_lc[o] = mm(unit, d_joined, NT).astype(jnp.bfloat16)
        gain_row = jnp.sum(gain_sum, axis=1, keepdims=True)
        grad_gain[...] = jnp.broadcast_to(gain_row, grad_gain.shape)
        for b in range(hidden_size // block):
            at = slice(block * b, block * (b + 1))
            d_pre[:, at] = (mm(d_fm[...], w_second[at], NT) * slope[:, at]).astype(jnp.bfloat16)
        d_pair[...] = mm(d_pre[...], w_first[...], NT).astype(jnp.bfloat16)

    mine = core[0]
    narrow = keep.shape[1]
    second_rows = hidden_t.shape[0] // wide
    first_rows = flat_t.shape[0] // wide
    own_second, own_first = second_rows // narrow, first_rows // narrow
    second_cuts, first_cuts = d_fm.shape[1] // COLUMNS, hidden_size // COLUMNS
    for which, out in ((1 - mine, send), (mine, keep)):
        w = 2 * step + which
        rows = pl.ds(pl.multiple_of(w * second_rows, second_rows), second_rows)
        for c in range(second_cuts):
            part = mm(hidden_t[rows], d_fm[:, COLUMNS * c : COLUMNS * (c + 1)])
            out[0, :, own_second * c : own_second * (c + 1), :] = part.reshape(
                narrow, own_second, COLUMNS
            )
        rows = pl.ds(pl.multiple_of(w * first_rows, first_rows), first_rows)
        for c in range(first_cuts):
            part = mm(flat_t[rows], d_pre[:, COLUMNS * c : COLUMNS * (c + 1)])
            at = own_second * second_cuts + own_first * c
            out[0, :, at : at + own_first, :] = part.reshape(narrow, own_first, COLUMNS)


def whole(shape):
    zeros = (0,) * len(shape)
    return pl.BlockSpec(shape, lambda j, c: zeros, pipeline_mode=pl.Buffered(1))


def mlp(core, x, up, proj, w_first, w_second, comp, gain, wide, narrow):
    samples = x.shape[2]
    pairs, hidden_size = w_first.shape
    outs = w_second.shape[1]
    half = wide // 2
    chunk = (w_first.size + w_second.size) // (wide * narrow * COLUMNS)
    sums = jax.ShapeDtypeStruct((half, narrow, chunk, COLUMNS), jnp.float32)
    rest = [
        jax.ShapeDtypeStruct((TABLES, samples, D), jnp.bfloat16),
        jax.ShapeDtypeStruct((RANK, samples, D), jnp.bfloat16),
        jax.ShapeDtypeStruct((samples, pairs), jnp.bfloat16),
        jax.ShapeDtypeStruct((LC_OUT, samples, D), jnp.bfloat16),
        jax.ShapeDtypeStruct((D, LANES), jnp.float32),
    ]

    def by_step(shape):
        return pl.BlockSpec((1,) + shape.shape[1:], lambda j, c: (j, 0, 0, 0))

    bf16, f32 = jnp.bfloat16, jnp.float32
    return pl.pallas_call(
        functools.partial(mlp_kernel, wide),
        grid_spec=pltpu.PrefetchScalarGridSpec(
            num_scalar_prefetch=1,
            grid=(half,),
            in_specs=[whole(a.shape) for a in (x, up, proj)]
            + [pl.BlockSpec(memory_space=pl.ANY)] * 2
            + [whole(a.shape) for a in (comp, gain)],
            out_specs=[by_step(sums)] * 2 + [whole(r.shape) for r in rest],
            scratch_shapes=[
                pltpu.VMEM((samples, pairs), bf16),
                pltpu.VMEM((pairs, samples), bf16),
                pltpu.VMEM((samples, hidden_size), bf16),
                pltpu.VMEM((hidden_size, samples), bf16),
                pltpu.VMEM((samples, hidden_size), f32),
                pltpu.VMEM((LC_OUT, D, samples), f32),
                pltpu.VMEM((samples, outs), bf16),
                pltpu.VMEM((samples, hidden_size), bf16),
                pltpu.VMEM(w_first.shape, bf16),
                pltpu.VMEM(w_second.shape, bf16),
                pltpu.SemaphoreType.DMA((2,)),
            ],
        ),
        out_shape=[sums, sums] + rest,
        compiler_params=pltpu.CompilerParams(vmem_limit_bytes=VMEM),
        cost_estimate=pl.CostEstimate(
            flops=16_000_000_000, bytes_accessed=32_000_000, transcendentals=600_000
        ),
    )(core, x, up, proj, w_first, w_second, comp, gain)


def rows_kernel(
    narrow, here, xs, inner, d_pair, d_lc, proj, comp, hot_ids, cold_ids, *refs
):
    colds, (hot, sums, d_rows, totals) = refs[:narrow], refs[narrow:]
    samples = xs.shape[1]
    share = COLD_TABLES // narrow
    proj_rows, comp_rows = expand(proj[...]), expand_t(comp[...])
    match = same_sample(OCTET * GROUP, RANK * GROUP)
    match_t = same_sample(RANK * GROUP, OCTET * GROUP)
    rank_of, table_match = pick_rank(), same_table()
    totals[...] = jnp.zeros_like(totals)

    def group(g, carry):
        rows = pl.ds(pl.multiple_of(g * GROUP, GROUP), GROUP)
        xg = xs[:, rows, :].reshape(TABLES * GROUP, D)
        inner_g = inner[:, rows, :].reshape(RANK * GROUP, D)
        d_lc_g = d_lc[:, rows, :].reshape(LC_OUT * GROUP, D)
        parts, parts_t = [], []
        for j in range(TABLES // OCTET):
            own = d_pair[rows, OCTET * RANK * j : OCTET * RANK * (j + 1)]
            spread = jnp.concatenate([own] * OCTET, axis=0) * table_match
            parts.append(mm(spread, rank_of, NT).astype(jnp.bfloat16) * match)
            parts_t.append(mm(rank_of, spread, NT).astype(jnp.bfloat16) * match_t)
        d_pairs = jnp.concatenate(parts, axis=0)
        d_pairs_t = jnp.concatenate(parts_t, axis=1)
        d_inner = mm(d_pairs_t, xg).astype(jnp.bfloat16)
        d_embed = mm(d_pairs, inner_g) + mm(proj_rows, d_inner) + mm(comp_rows, d_lc_g)
        d_rows[:, rows, :] = d_embed.astype(jnp.bfloat16).reshape(TABLES, GROUP, D)
        totals[...] += mm(jnp.concatenate([d_inner, d_lc_g], axis=0), xg, NT)
        return carry

    lax.fori_loop(0, samples // GROUP, group, 0, unroll=2)
    unit = eye(D)
    for step in range(narrow):
        target = lax.rem(here[0] + step, narrow)
        for i in range(share):
            colds[step][D * i : D * (i + 1)] = mm(
                unit, d_rows[HOT_TABLES + target * share + i], NT
            )
        for i in range(ID_ROWS):
            colds[step][D * share + i : D * share + i + 1] = cold_ids[
                pl.ds(target * share + min(i, share - 1), 1)
            ]
    for t in range(HOT_TABLES):
        values = mm(unit, d_rows[t], NT).astype(jnp.bfloat16)
        onehot = ones_where(iota((HOT_ROWS, samples), 0) == hot_ids[t : t + 1, :])
        hot[t] = mm(values, onehot, NT)
    sums_shape = totals.shape
    own = lax.rem(iota(sums_shape, 0), GROUP) == lax.rem(iota(sums_shape, 1), GROUP)
    masked = jnp.where(own, totals[...], 0.0)
    folded = jnp.sum(masked.reshape(RANK + LC_OUT, GROUP, sums_shape[1]), axis=1)
    sums[...] = lax.dot_general(
        folded,
        spread_rows(TABLES).astype(jnp.float32),
        NN,
        precision=lax.Precision.HIGHEST,
        preferred_element_type=jnp.float32,
    )


def row_gradients(here, xs, inner, d_pair, d_lc, proj, comp, hot_ids, cold_ids, narrow, part, parts):
    samples = xs.shape[1] // parts
    share = COLD_TABLES // narrow

    def middle(count):
        return pl.BlockSpec((count, samples, D), lambda i: (0, part, 0))

    def last(count):
        return pl.BlockSpec((count, samples), lambda i: (0, part))

    def full(*shape):
        zeros = (0,) * len(shape)
        return pl.BlockSpec(shape, lambda i: zeros)

    shapes = [(share * D + ID_ROWS, samples)] * narrow
    shapes += [(HOT_TABLES, D, HOT_ROWS), (RANK + LC_OUT, TABLES)]
    return pl.pallas_call(
        functools.partial(rows_kernel, narrow),
        grid=(1,),
        in_specs=[
            pl.BlockSpec(memory_space=pltpu.SMEM),
            middle(TABLES),
            middle(RANK),
            pl.BlockSpec((samples, TABLES * RANK), lambda i: (part, 0)),
            middle(LC_OUT),
            full(*proj.shape),
            full(*comp.shape),
            last(HOT_TABLES),
            last(COLD_TABLES),
        ],
        out_specs=[full(*shape) for shape in shapes],
        out_shape=[jax.ShapeDtypeStruct(shape, jnp.float32) for shape in shapes],
        scratch_shapes=[
            pltpu.VMEM((TABLES, samples, D), jnp.bfloat16),
            pltpu.VMEM(((RANK + LC_OUT) * GROUP, TABLES * GROUP), jnp.float32),
        ],
        compiler_params=pltpu.CompilerParams(vmem_limit_bytes=VMEM),
        cost_estimate=pl.CostEstimate(
            flops=1, bytes_accessed=1, transcendentals=0
        ),
    )(here, xs, inner, d_pair, d_lc, proj, comp, hot_ids, cold_ids)


def bits_of(axis):
    return (lax.axis_size(axis) - 1).bit_length()


def flip(value, axis, bit):
    return lax.ppermute(value, axis, [(i, i ^ (1 << bit)) for i in range(lax.axis_size(axis))])


def my_bit(axis, bit):
    return (lax.axis_index(axis) >> bit) & 1


def split(value, dims, label):
    dim = dims.index(label)
    me = my_bit(*label)
    send = lax.dynamic_index_in_dim(value, 1 - me, dim, keepdims=False)
    keep = lax.dynamic_index_in_dim(value, me, dim, keepdims=False)
    return send, keep, dims[:dim] + dims[dim + 1 :]


def join(value, label):
    got = flip(value, *label)
    me = my_bit(*label)
    return jnp.stack([jnp.where(me == 0, value, got), jnp.where(me == 0, got, value)], axis=0)


def nothing(*refs):
    pass


def gate(values, after=()):
    values, after = list(values), list(after)
    return list(
        pl.pallas_call(
        nothing,
        in_specs=[pl.BlockSpec(memory_space=pl.ANY)] * (len(values) + len(after)),
        out_specs=[pl.BlockSpec(memory_space=pl.ANY)] * len(values),
        out_shape=[jax.ShapeDtypeStruct(v.shape, v.dtype) for v in values],
        input_output_aliases={i: i for i in range(len(values))},
    )(*values, *after)
    )


def start(parts, labels):
    return [split(value, dims, label) for (value, dims), label in zip(parts, labels)]


def finish(cuts, labels):
    return [(keep + flip(send, *label), dims) for (send, keep, dims), label in zip(cuts, labels)]


def ordered(cuts, after=()):
    sends = gate([cut[0] for cut in cuts], after)
    return [(send, cut[1], cut[2]) for send, cut in zip(sends, cuts)]


def combine_kernel(cuts, bits, *refs):
    ins, outs = refs[: 8 * cuts], refs[8 * cuts :]
    for i, out in enumerate(outs):
        rows = out.shape[2] // cuts
        for u in range(cuts):
            keep, got = ins[2 * (cuts * i + u)], ins[2 * (cuts * i + u) + 1]
            out[:, :, rows * u : rows * (u + 1), :] = keep[...] + got[...]


def combine(bits, keep, got):
    blocks, n, rows, columns = keep.shape
    half = blocks // 2
    cuts = max(1, len(got) // 2)
    shape = (1, n, rows // (2 * cuts), columns)

    def spec(piece, other, at):
        if piece == 0:
            return pl.BlockSpec(shape, lambda i, b: (2 * i + (b[0] ^ other), 0, at, 0))
        return pl.BlockSpec(shape, lambda i, b: (half * (b[1] ^ other) + i, 0, at, 0))

    specs, operands = [], []
    for piece in (0, 1):
        for other in (1, 0):
            for at in range(piece * cuts, (piece + 1) * cuts):
                specs += [spec(piece, other, at), spec(piece, other, 0 if len(got) > 1 else at)]
                operands += [keep, got[at] if len(got) > 1 else got[0]]
    out = jax.ShapeDtypeStruct((half, n, rows // 2, columns), keep.dtype)
    return pl.pallas_call(
        functools.partial(combine_kernel, cuts),
        grid_spec=pltpu.PrefetchScalarGridSpec(
            num_scalar_prefetch=1,
            grid=(half,),
            in_specs=specs,
            out_specs=[pl.BlockSpec((1, n, rows // 2, columns), lambda i, b: (i, 0, 0, 0))] * 4,
        ),
        out_shape=[out] * 4,
        compiler_params=pltpu.CompilerParams(vmem_limit_bytes=VMEM),
        cost_estimate=pl.CostEstimate(
            flops=keep.size, bytes_accessed=12 * keep.size, transcendentals=0
        ),
    )(bits, *operands)


def add_rows_kernel(rows, parts, core, *refs):
    ids, values, keep, sends = refs[:parts], refs[parts : 2 * parts], refs[2 * parts], refs[2 * parts + 1 :]
    table = pl.program_id(0)
    numbers = jnp.concatenate([r[pl.ds(table, 1)] for r in ids], axis=1).astype(jnp.int32)
    owners, at = lax.div(numbers, rows), lax.rem(numbers, rows)
    values = jnp.concatenate([r[...].astype(jnp.bfloat16) for r in values], axis=1)
    onehot = ones_where(iota((rows, numbers.shape[1]), 0) == at)
    for which, outs in ((1 - core[0], sends), (core[0], [keep])):
        for b in range(keep.shape[0]):
            sums = mm(values * ones_where(owners == 2 * b + which), onehot, NT)
            size = D // len(outs)
            for i, out in enumerate(outs):
                out[b, 0] = sums[size * i : size * (i + 1)]


def add_rows(core, values, tables, blocks, rows):
    samples = values[0].shape[1]
    parts = len(values)
    out = jax.ShapeDtypeStruct((blocks // 2, tables, D, rows), jnp.float32)
    piece = jax.ShapeDtypeStruct((blocks // 2, tables, D // SENDS, rows), jnp.float32)
    return pl.pallas_call(
        functools.partial(add_rows_kernel, rows, parts),
        grid_spec=pltpu.PrefetchScalarGridSpec(
            num_scalar_prefetch=1,
            grid=(tables,),
            in_specs=[
                pl.BlockSpec((ID_ROWS, samples), lambda t, c: (tables * D // ID_ROWS, 0))
            ]
            * parts
            + [pl.BlockSpec((D, samples), lambda t, c: (t, 0))] * parts,
            out_specs=[pl.BlockSpec((blocks // 2, 1, D, rows), lambda t, c: (0, t, 0, 0))]
            + [pl.BlockSpec((blocks // 2, 1, D // SENDS, rows), lambda t, c: (0, t, 0, 0))] * SENDS,
        ),
        out_shape=[out] + [piece] * SENDS,
        compiler_params=pltpu.CompilerParams(vmem_limit_bytes=VMEM),
        cost_estimate=pl.CostEstimate(
            flops=DENSE_COST, bytes_accessed=1, transcendentals=0
        ),
    )(core, *values, *values)


def local(
    embeddings,
    upstream,
    factor_machine_projection,
    w_first,
    w_second,
    compress,
    norm_gain,
    hot_index,
    cold_row,
    cold_owner,
):
    wide, narrow = lax.axis_size("wide"), lax.axis_size("narrow")
    devices = wide * narrow
    wide_bits = [("wide", b) for b in range(bits_of("wide"))]
    narrow_bits = [("narrow", b) for b in range(bits_of("narrow"))]
    core_bit, links = wide_bits[0], wide_bits[1:]
    left_dims = links[::-1] + narrow_bits[::-1]

    sample_count = embeddings.shape[0]
    here = lax.axis_index("narrow")
    x = jnp.transpose(embeddings, (1, 2, 0))
    up = jnp.transpose(upstream, (1, 2, 0))
    core = my_bit("wide", 0).reshape(1)
    mlp_keep, mlp_send, xs, inner, d_pair, d_lc, gain_sum = mlp(
        core,
        x,
        up,
        factor_machine_projection,
        w_first,
        w_second,
        compress,
        norm_gain.reshape(1, D),
        wide,
        narrow,
    )
    cold_ids = (cold_owner[:, :, 0] * COLD_ROWS_DEV + cold_row).T.astype(jnp.float32)

    def rows_of(part, d_pair):
        *values, hot_sums, sums = row_gradients(
            here.reshape(1),
            xs,
            inner,
            d_pair,
            d_lc,
            factor_machine_projection,
            compress,
            hot_index.T,
            cold_ids,
            narrow,
            part,
            2,
        )
        return values, hot_sums, sums

    share = COLD_TABLES // narrow
    low, high = narrow_bits
    link_bits = jnp.stack([my_bit(*links[0]), my_bit(*links[-1])])

    def go_round(value, step):
        return lax.ppermute(value, "narrow", [(i, (i + step) % narrow) for i in range(narrow)])

    def halve(part, label):
        (part,) = finish(start([part], [label]), [label])
        return part

    def first_cuts(keep, got):
        a_send, a_keep, b_send, b_keep = combine(link_bits, keep, got)
        dims = links[::-1]
        return [
            (a_send, a_keep, dims[:-1]),
            (b_send, b_keep, dims[1:]),
        ]

    def unfold(parts, tail):
        return [(value.reshape([2] * len(dims) + tail), dims) for value, dims in parts]

    early, hot_early, sums_early = rows_of(0, d_pair)
    got_early = [go_round(value, step) for step, value in enumerate(early) if step]
    (mlp_got,) = gate([flip(mlp_send, *core_bit)], early[:1])
    chunk = mlp_keep.shape[2]
    cuts = first_cuts(mlp_keep, [mlp_got])
    (d_pair_late,) = gate([d_pair], [cuts[0][0]])
    late, hot_late, sums_late = rows_of(1, d_pair_late)

    sums = sums_early + sums_late
    grad_proj, compress_gradient = sums[:RANK].T, sums[RANK:]
    hot_local = hot_early + hot_late
    hot_rows = hot_local.size // LANES
    small = jnp.concatenate([grad_proj.reshape(-1), compress_gradient.reshape(-1), gain_sum[:, 0]])
    small = jnp.pad(small, (0, -small.size % LANES)).reshape(-1, LANES)
    shared = jnp.concatenate([hot_local.reshape(hot_rows, LANES), small], axis=0)
    shared = jnp.pad(shared, ((0, -shared.shape[0] % (8 * devices)), (0, 0)))
    hot_order = [core_bit] + links + [low]
    hot = (shared.reshape([2] * len(hot_order) + [-1, LANES]), hot_order)

    late_sends = gate(late[1:], got_early)
    got_late = [go_round(value, step + 1) for step, value in enumerate(late_sends)]
    got_values = early[:1] + got_early + late[:1] + got_late
    mlp_parts = unfold(
        finish(cuts, [links[0], links[-1]]), [2] * len(narrow_bits) + [chunk // 2, COLUMNS]
    )
    mlp_parts = [(value, dims + narrow_bits[::-1]) for value, dims in mlp_parts]
    for turn in range(1, len(links)):
        labels = [links[turn], links[-1 - turn]]
        cuts = start(mlp_parts, labels)
        if turn == len(links) - 1:
            (hot_cut,) = start([hot], [core_bit])
            sends = gate([cut[0] for cut in cuts] + [hot_cut[0]], late_sends)
            cuts = [(send, cut[1], cut[2]) for send, cut in zip(sends, cuts)]
            (hot,) = finish([(sends[2], hot_cut[1], hot_cut[2])], [core_bit])
        mlp_parts = finish(cuts, labels)

    cold_keep, *cold_sends = add_rows(core, got_values, share, wide, COLD_ROWS_DEV)
    labels = [low, links[0]]
    both = start(mlp_parts, [low, low])
    mlp_dims = both[0][2]
    mlp_cut = [jnp.concatenate([cut[i] for cut in both], axis=len(mlp_dims)) for i in range(2)]
    ready = [(*mlp_cut, mlp_dims)] + start([hot], labels[1:])
    sends = gate(cold_sends + [cut[0] for cut in ready])
    cold_sends = sends[:SENDS]
    ready = [(send, cut[1], cut[2]) for send, cut in zip(sends[SENDS:], ready)]
    mlp_part, hot = finish(ready, labels)
    for label in links[1:]:
        hot = halve(hot, label)
    cuts = first_cuts(cold_keep, [flip(send, *core_bit) for send in cold_sends])
    half = D // 2
    parts = []
    for turn in range(len(links)):
        labels = [links[turn], links[-1 - turn]]
        last = turn == len(links) - 1
        if turn == 0:
            labels = labels + [low]
            ready = ordered(cuts + start([hot], labels[2:]))
            *parts, hot = finish(ready, labels)
            parts = unfold(parts, [share, half, COLD_ROWS_DEV])
            ready = ordered(start([mlp_part], [high]), [cut[0] for cut in ready])
            (mlp_part,) = finish(ready, [high])
        elif last:
            ready = start(parts, labels)
            *sends, hot_value = gate([cut[0] for cut in ready] + [hot[0]])
            ready = [(send, cut[1], cut[2]) for send, cut in zip(sends, ready)]
            hot_value = hot_value + flip(hot_value, *high)
            parts = finish(ready, labels)
        else:
            parts = finish(ordered(start(parts, labels)), labels)

    cold_grad = jnp.zeros((narrow, share, D, COLD_ROWS_DEV), jnp.float32)
    moving = jnp.concatenate([parts[0][0], parts[1][0]], axis=1)
    joins = [[low], links[-1:]] + [[]] * (narrow - 4) + [links[-2::-1]]
    for step in range(narrow):
        cold_grad = lax.dynamic_update_index_in_dim(cold_grad, moving, (here - step) % narrow, 0)
        if step == narrow - 1:
            break
        after = [] if step else [mlp_part[0]]
        moving, hot_value = gate([moving, hot_value], after)
        moving = go_round(moving, 1)
        for label in joins[step]:
            hot_value = join(hot_value, label)
    (hot_value,) = gate([hot_value], [moving])
    shared = join(hot_value, core_bit).reshape(-1, LANES)
    cold_grad = jnp.transpose(
        cold_grad.reshape(COLD_TABLES, D, COLD_ROWS_DEV), (0, 2, 1)
    )
    hot_grad = jnp.transpose(shared[:hot_rows].reshape(HOT_TABLES, D, HOT_ROWS), (0, 2, 1))
    small = shared[hot_rows:].reshape(-1)
    n_proj, n_compress = TABLES * RANK, LC_OUT * TABLES
    grad_proj = small[:n_proj].reshape(TABLES, RANK)
    compress_gradient = small[n_proj : n_proj + n_compress].reshape(LC_OUT, TABLES)
    grad_gain = small[n_proj + n_compress : n_proj + n_compress + D]

    done = mlp_part[0]
    own_second, own_first = w_first.shape[1] // devices, TABLES * RANK // devices
    cut = own_second * FM_OUT * D // COLUMNS

    def side_by_side(blocks, rows):
        return jnp.transpose(blocks.reshape(-1, rows, COLUMNS), (1, 0, 2)).reshape(rows, -1)

    grad_second = side_by_side(done[:cut], own_second)
    grad_first = side_by_side(done[cut:], own_first)
    return (grad_first, grad_second, grad_proj, compress_gradient, grad_gain, hot_grad, cold_grad)


def solution(mesh):
    placed = (
        P(("wide", "narrow"), None, None),
        P(("wide", "narrow"), None, None),
        P(),
        P(),
        P(),
        P(),
        P(),
        P(("wide", "narrow"), None),
        P(("wide", "narrow"), None),
        P(("wide", "narrow"), None, None),
    )
    return jax.shard_map(
        local,
        mesh=mesh,
        in_specs=placed,
        out_specs=(
            P(("wide", "narrow"), None),
            P(("wide", "narrow"), None),
            P(),
            P(),
            P(),
            P(),
            P(None, "wide", None),
        ),
        check_vma=False,
    )
```

```python
import functools

import jax
import jax.numpy as jnp
from jax import lax
from jax.experimental import pallas as pl
from jax.experimental.pallas import tpu as pltpu
from jax.sharding import PartitionSpec as P

D = 192
RANK = 16
HOT_TABLES = 16
COLD_TABLES = 16
FM_OUT = 8
LC_OUT = 8
HOT_ROWS = 128
COLD_ROWS_DEV = 256
TABLES = 32
LANES = 128
COLUMNS = 512
ID_ROWS = 8
SENDS = 2
DENSE_COST = 12000000000


NT = (((1,), (1,)), ((), ()))
NN = (((1,), (0,)), ((), ()))
GROUP = 16
OCTET = 8
VMEM = 60 * 1024 * 1024


def mm(a, b, dims=NN):
    return lax.dot_general(a, b, dims, preferred_element_type=jnp.float32)


def iota(shape, dim):
    return lax.broadcasted_iota(jnp.int32, shape, dim)


def ones_where(mask):
    return mask.astype(jnp.float32).astype(jnp.bfloat16)


def eye(size):
    return ones_where(iota((size, size), 0) == iota((size, size), 1))


def same_sample(rows, columns):
    return ones_where(
        lax.rem(iota((rows, columns), 0), GROUP) == lax.rem(iota((rows, columns), 1), GROUP)
    )


def spread_rows(count):
    return ones_where(
        lax.div(iota((count * GROUP, count), 0), GROUP) == iota((count * GROUP, count), 1)
    )


def spread_columns(count):
    return ones_where(
        lax.div(iota((count, count * GROUP), 1), GROUP) == iota((count, count * GROUP), 0)
    )


def expand(matrix):
    rows, columns = matrix.shape
    tall = mm(spread_rows(rows), matrix).astype(jnp.bfloat16)
    full = mm(tall, spread_columns(columns)).astype(jnp.bfloat16)
    return full * same_sample(rows * GROUP, columns * GROUP)


def expand_t(matrix):
    rows, columns = matrix.shape
    tall = mm(spread_rows(columns), matrix, NT).astype(jnp.bfloat16)
    full = mm(tall, spread_columns(rows)).astype(jnp.bfloat16)
    return full * same_sample(columns * GROUP, rows * GROUP)


def pick_rank():
    shape = (RANK * GROUP, OCTET * RANK)
    return ones_where(lax.div(iota(shape, 0), GROUP) == lax.rem(iota(shape, 1), RANK))


def same_table():
    shape = (OCTET * GROUP, OCTET * RANK)
    return ones_where(lax.div(iota(shape, 0), GROUP) == lax.div(iota(shape, 1), RANK))


def mlp_kernel(
    wide,
    core,
    x,
    up_in,
    proj,
    w_first_in,
    w_second_in,
    comp,
    gain,
    keep,
    send,
    xs,
    inner,
    d_pair,
    d_lc,
    grad_gain,
    flat,
    flat_t,
    hidden,
    hidden_t,
    slope,
    lc_out,
    d_fm,
    d_pre,
    w_first,
    w_second,
    up,
    arrived,
):
    step = pl.program_id(0)
    samples = x.shape[2]
    hidden_size = w_first.shape[1]
    groups = samples // GROUP

    @pl.when(step == 0)
    def _():
        first_copy = pltpu.make_async_copy(w_first_in, w_first, arrived.at[0])
        second_copy = pltpu.make_async_copy(w_second_in, w_second, arrived.at[1])
        first_copy.start()
        second_copy.start()
        up_copy = pltpu.make_async_copy(up_in, up, arrived.at[2])
        up_copy.start()
        unit = eye(samples)
        for n in range(TABLES):
            xs[n] = mm(unit, x[n], NT).astype(jnp.bfloat16)
        comp_rows = expand(comp[...])
        for b in range(D // GROUP):
            block = x[:, GROUP * b : GROUP * (b + 1), :].reshape(TABLES * GROUP, samples)
            lc_out[:, GROUP * b : GROUP * (b + 1), :] = mm(comp_rows, block).reshape(
                LC_OUT, GROUP, samples
            )
        proj_t = expand_t(proj[...])
        samples_match = same_sample(TABLES * GROUP, RANK * GROUP).astype(jnp.float32)
        rank_of = pick_rank()
        table_match = same_table().astype(jnp.float32)

        def group(g, carry):
            rows = pl.ds(pl.multiple_of(g * GROUP, GROUP), GROUP)
            xg = xs[:, rows, :].reshape(TABLES * GROUP, D)
            inner_g = mm(proj_t, xg).astype(jnp.bfloat16)
            inner[:, rows, :] = inner_g.reshape(RANK, GROUP, D)
            pair = (mm(xg, inner_g, NT) * samples_match).astype(jnp.bfloat16)
            for j in range(TABLES // OCTET):
                part = pair[OCTET * GROUP * j : OCTET * GROUP * (j + 1)]
                wide_part = mm(part, rank_of) * table_match
                flat[rows, OCTET * RANK * j : OCTET * RANK * (j + 1)] = jnp.sum(
                    wide_part.reshape(OCTET, GROUP, OCTET * RANK), axis=0
                ).astype(jnp.bfloat16)
            return carry

        lax.fori_loop(0, groups, group, 0, unroll=4)
        first_copy.wait()
        second_copy.wait()
        up_copy.wait()
        pairs = flat.shape[1]
        block = 256
        unit_b = eye(block)
        for b in range(pairs // block):
            at = slice(block * b, block * (b + 1))
            flat_t[at] = mm(unit_b, flat[:, at], NT).astype(jnp.bfloat16)
        for b in range(hidden_size // block):
            at = slice(block * b, block * (b + 1))
            pre = mm(flat[...], w_first[:, at])
            sigmoid_v = 1.0 / (1.0 + jnp.exp(-pre))
            slope[:, at] = sigmoid_v * (1.0 + pre * (1.0 - sigmoid_v))
            hidden_b = (pre * sigmoid_v).astype(jnp.bfloat16)
            hidden[:, at] = hidden_b
            hidden_t[at] = mm(unit_b, hidden_b, NT).astype(jnp.bfloat16)
        gain_column = jnp.sum(
            jnp.where(iota((D, D), 0) == iota((D, D), 1), gain[...], 0.0), axis=1, keepdims=True
        )
        scale = 1.0 / D
        gain_sum = jnp.zeros((D, samples), jnp.float32)

        def norm(joined, o, gain_sum):
            mean = jnp.sum(joined, axis=0, keepdims=True) * scale
            centered = joined - mean
            variance = jnp.sum(centered * centered, axis=0, keepdims=True) * scale
            inv_std = lax.rsqrt(variance + 1e-05)
            normed = centered * inv_std
            cotangent = up[o].astype(jnp.float32)
            gain_sum = gain_sum + cotangent * normed
            d_norm = cotangent * gain_column
            mean_d = jnp.sum(d_norm, axis=0, keepdims=True) * scale
            mean_n = jnp.sum(d_norm * normed, axis=0, keepdims=True) * scale
            return (inv_std * (d_norm - mean_d - normed * mean_n)).astype(jnp.bfloat16), gain_sum

        for c in range(FM_OUT // 2):
            at = slice(2 * D * c, 2 * D * (c + 1))
            fm_t = mm(hidden[...], w_second[:, at]).T
            low, gain_sum = norm(fm_t[:D], 2 * c, gain_sum)
            high, gain_sum = norm(fm_t[D:], 2 * c + 1, gain_sum)
            both = jnp.concatenate([low, high], axis=0)
            d_fm[:, at] = mm(unit, both, NT).astype(jnp.bfloat16)
        for o in range(LC_OUT):
            d_joined, gain_sum = norm(lc_out[o], FM_OUT + o, gain_sum)
            d_lc[o] = mm(unit, d_joined, NT).astype(jnp.bfloat16)
        gain_row = jnp.sum(gain_sum, axis=1, keepdims=True)
        grad_gain[...] = jnp.broadcast_to(gain_row, grad_gain.shape)
        for b in range(hidden_size // block):
            at = slice(block * b, block * (b + 1))
            d_pre[:, at] = (mm(d_fm[...], w_second[at], NT) * slope[:, at]).astype(jnp.bfloat16)
        d_pair[...] = mm(d_pre[...], w_first[...], NT).astype(jnp.bfloat16)

    mine = core[0]
    narrow = keep.shape[1]
    second_rows = hidden_t.shape[0] // wide
    first_rows = flat_t.shape[0] // wide
    own_second, own_first = second_rows // narrow, first_rows // narrow
    second_cuts, first_cuts = d_fm.shape[1] // COLUMNS, hidden_size // COLUMNS
    for which, out in ((1 - mine, send), (mine, keep)):
        w = 2 * step + which
        rows = pl.ds(pl.multiple_of(w * second_rows, second_rows), second_rows)
        for c in range(second_cuts):
            part = mm(hidden_t[rows], d_fm[:, COLUMNS * c : COLUMNS * (c + 1)])
            out[0, :, own_second * c : own_second * (c + 1), :] = part.reshape(
                narrow, own_second, COLUMNS
            )
        rows = pl.ds(pl.multiple_of(w * first_rows, first_rows), first_rows)
        for c in range(first_cuts):
            part = mm(flat_t[rows], d_pre[:, COLUMNS * c : COLUMNS * (c + 1)])
            at = own_second * second_cuts + own_first * c
            out[0, :, at : at + own_first, :] = part.reshape(narrow, own_first, COLUMNS)


def whole(shape):
    zeros = (0,) * len(shape)
    return pl.BlockSpec(shape, lambda j, c: zeros, pipeline_mode=pl.Buffered(1))


def mlp(core, x, up, proj, w_first, w_second, comp, gain, wide, narrow):
    samples = x.shape[2]
    pairs, hidden_size = w_first.shape
    outs = w_second.shape[1]
    half = wide // 2
    chunk = (w_first.size + w_second.size) // (wide * narrow * COLUMNS)
    sums = jax.ShapeDtypeStruct((half, narrow, chunk, COLUMNS), jnp.float32)
    rest = [
        jax.ShapeDtypeStruct((TABLES, samples, D), jnp.bfloat16),
        jax.ShapeDtypeStruct((RANK, samples, D), jnp.bfloat16),
        jax.ShapeDtypeStruct((samples, pairs), jnp.bfloat16),
        jax.ShapeDtypeStruct((LC_OUT, samples, D), jnp.bfloat16),
        jax.ShapeDtypeStruct((D, LANES), jnp.float32),
    ]

    def by_step(shape):
        return pl.BlockSpec((1,) + shape.shape[1:], lambda j, c: (j, 0, 0, 0))

    bf16, f32 = jnp.bfloat16, jnp.float32
    return pl.pallas_call(
        functools.partial(mlp_kernel, wide),
        grid_spec=pltpu.PrefetchScalarGridSpec(
            num_scalar_prefetch=1,
            grid=(half,),
            in_specs=[whole(x.shape), pl.BlockSpec(memory_space=pl.ANY), whole(proj.shape)]
            + [pl.BlockSpec(memory_space=pl.ANY)] * 2
            + [whole(a.shape) for a in (comp, gain)],
            out_specs=[by_step(sums)] * 2 + [whole(r.shape) for r in rest],
            scratch_shapes=[
                pltpu.VMEM((samples, pairs), bf16),
                pltpu.VMEM((pairs, samples), bf16),
                pltpu.VMEM((samples, hidden_size), bf16),
                pltpu.VMEM((hidden_size, samples), bf16),
                pltpu.VMEM((samples, hidden_size), f32),
                pltpu.VMEM((LC_OUT, D, samples), f32),
                pltpu.VMEM((samples, outs), bf16),
                pltpu.VMEM((samples, hidden_size), bf16),
                pltpu.VMEM(w_first.shape, bf16),
                pltpu.VMEM(w_second.shape, bf16),
                pltpu.VMEM(up.shape, bf16),
                pltpu.SemaphoreType.DMA((3,)),
            ],
        ),
        out_shape=[sums, sums] + rest,
        compiler_params=pltpu.CompilerParams(vmem_limit_bytes=VMEM),
        cost_estimate=pl.CostEstimate(
            flops=16_000_000_000, bytes_accessed=32_000_000, transcendentals=600_000
        ),
    )(core, x, up, proj, w_first, w_second, comp, gain)


def rows_kernel(
    narrow, here, xs, inner, d_pair, d_lc, proj, comp, hot_ids, cold_ids, *refs
):
    colds, (hot, sums, d_rows, totals) = refs[:narrow], refs[narrow:]
    samples = xs.shape[1]
    share = COLD_TABLES // narrow
    proj_rows, comp_rows = expand(proj[...]), expand_t(comp[...])
    match = same_sample(OCTET * GROUP, RANK * GROUP)
    match_t = same_sample(RANK * GROUP, OCTET * GROUP)
    rank_of, table_match = pick_rank(), same_table()
    totals[...] = jnp.zeros_like(totals)

    def group(g, carry):
        rows = pl.ds(pl.multiple_of(g * GROUP, GROUP), GROUP)
        xg = xs[:, rows, :].reshape(TABLES * GROUP, D)
        inner_g = inner[:, rows, :].reshape(RANK * GROUP, D)
        d_lc_g = d_lc[:, rows, :].reshape(LC_OUT * GROUP, D)
        parts, parts_t = [], []
        for j in range(TABLES // OCTET):
            own = d_pair[rows, OCTET * RANK * j : OCTET * RANK * (j + 1)]
            spread = jnp.concatenate([own] * OCTET, axis=0) * table_match
            parts.append(mm(spread, rank_of, NT).astype(jnp.bfloat16) * match)
            parts_t.append(mm(rank_of, spread, NT).astype(jnp.bfloat16) * match_t)
        d_pairs = jnp.concatenate(parts, axis=0)
        d_pairs_t = jnp.concatenate(parts_t, axis=1)
        d_inner = mm(d_pairs_t, xg).astype(jnp.bfloat16)
        d_embed = mm(d_pairs, inner_g) + mm(proj_rows, d_inner) + mm(comp_rows, d_lc_g)
        d_rows[:, rows, :] = d_embed.astype(jnp.bfloat16).reshape(TABLES, GROUP, D)
        totals[...] += mm(jnp.concatenate([d_inner, d_lc_g], axis=0), xg, NT)
        return carry

    lax.fori_loop(0, samples // GROUP, group, 0, unroll=4)
    unit = eye(D)
    for step in range(narrow):
        target = lax.rem(here[0] + step, narrow)
        for i in range(share):
            colds[step][D * i : D * (i + 1)] = mm(
                unit, d_rows[HOT_TABLES + target * share + i], NT
            )
        for i in range(ID_ROWS):
            colds[step][D * share + i : D * share + i + 1] = cold_ids[
                pl.ds(target * share + min(i, share - 1), 1)
            ]
    for t in range(HOT_TABLES):
        values = mm(unit, d_rows[t], NT).astype(jnp.bfloat16)
        onehot = ones_where(iota((HOT_ROWS, samples), 0) == hot_ids[t : t + 1, :])
        hot[t] = mm(values, onehot, NT)
    sums_shape = totals.shape
    own = lax.rem(iota(sums_shape, 0), GROUP) == lax.rem(iota(sums_shape, 1), GROUP)
    masked = jnp.where(own, totals[...], 0.0)
    folded = jnp.sum(masked.reshape(RANK + LC_OUT, GROUP, sums_shape[1]), axis=1)
    sums[...] = lax.dot_general(
        folded,
        spread_rows(TABLES).astype(jnp.float32),
        NN,
        precision=lax.Precision.HIGHEST,
        preferred_element_type=jnp.float32,
    )


def row_gradients(here, xs, inner, d_pair, d_lc, proj, comp, hot_ids, cold_ids, narrow, part, parts):
    samples = xs.shape[1] // parts
    share = COLD_TABLES // narrow

    def middle(count):
        return pl.BlockSpec((count, samples, D), lambda i: (0, part, 0))

    def last(count):
        return pl.BlockSpec((count, samples), lambda i: (0, part))

    def full(*shape):
        zeros = (0,) * len(shape)
        return pl.BlockSpec(shape, lambda i: zeros)

    shapes = [(share * D + ID_ROWS, samples)] * narrow
    shapes += [(HOT_TABLES, D, HOT_ROWS), (RANK + LC_OUT, TABLES)]
    return pl.pallas_call(
        functools.partial(rows_kernel, narrow),
        grid=(1,),
        in_specs=[
            pl.BlockSpec(memory_space=pltpu.SMEM),
            middle(TABLES),
            middle(RANK),
            pl.BlockSpec((samples, TABLES * RANK), lambda i: (part, 0)),
            middle(LC_OUT),
            full(*proj.shape),
            full(*comp.shape),
            last(HOT_TABLES),
            last(COLD_TABLES),
        ],
        out_specs=[full(*shape) for shape in shapes],
        out_shape=[jax.ShapeDtypeStruct(shape, jnp.float32) for shape in shapes],
        scratch_shapes=[
            pltpu.VMEM((TABLES, samples, D), jnp.bfloat16),
            pltpu.VMEM(((RANK + LC_OUT) * GROUP, TABLES * GROUP), jnp.float32),
        ],
        compiler_params=pltpu.CompilerParams(vmem_limit_bytes=VMEM),
        cost_estimate=pl.CostEstimate(
            flops=1, bytes_accessed=1, transcendentals=0
        ),
    )(here, xs, inner, d_pair, d_lc, proj, comp, hot_ids, cold_ids)


def bits_of(axis):
    return (lax.axis_size(axis) - 1).bit_length()


def flip(value, axis, bit):
    return lax.ppermute(value, axis, [(i, i ^ (1 << bit)) for i in range(lax.axis_size(axis))])


def my_bit(axis, bit):
    return (lax.axis_index(axis) >> bit) & 1


def split(value, dims, label):
    dim = dims.index(label)
    me = my_bit(*label)
    send = lax.dynamic_index_in_dim(value, 1 - me, dim, keepdims=False)
    keep = lax.dynamic_index_in_dim(value, me, dim, keepdims=False)
    return send, keep, dims[:dim] + dims[dim + 1 :]


def join(value, label):
    got = flip(value, *label)
    me = my_bit(*label)
    return jnp.stack([jnp.where(me == 0, value, got), jnp.where(me == 0, got, value)], axis=0)


def nothing(*refs):
    pass


def gate(values, after=()):
    values, after = list(values), list(after)
    return list(
        pl.pallas_call(
        nothing,
        in_specs=[pl.BlockSpec(memory_space=pl.ANY)] * (len(values) + len(after)),
        out_specs=[pl.BlockSpec(memory_space=pl.ANY)] * len(values),
        out_shape=[jax.ShapeDtypeStruct(v.shape, v.dtype) for v in values],
        input_output_aliases={i: i for i in range(len(values))},
    )(*values, *after)
    )


def start(parts, labels):
    return [split(value, dims, label) for (value, dims), label in zip(parts, labels)]


def finish(cuts, labels):
    return [(keep + flip(send, *label), dims) for (send, keep, dims), label in zip(cuts, labels)]


def ordered(cuts, after=()):
    sends = gate([cut[0] for cut in cuts], after)
    return [(send, cut[1], cut[2]) for send, cut in zip(sends, cuts)]


def combine_kernel(cuts, bits, *refs):
    ins, outs = refs[: 8 * cuts], refs[8 * cuts :]
    for i, out in enumerate(outs):
        rows = out.shape[2] // cuts
        for u in range(cuts):
            keep, got = ins[2 * (cuts * i + u)], ins[2 * (cuts * i + u) + 1]
            out[:, :, rows * u : rows * (u + 1), :] = keep[...] + got[...]


def combine(bits, keep, got):
    blocks, n, rows, columns = keep.shape
    half = blocks // 2
    cuts = max(1, len(got) // 2)
    shape = (1, n, rows // (2 * cuts), columns)

    def spec(piece, other, at):
        if piece == 0:
            return pl.BlockSpec(shape, lambda i, b: (2 * i + (b[0] ^ other), 0, at, 0))
        return pl.BlockSpec(shape, lambda i, b: (half * (b[1] ^ other) + i, 0, at, 0))

    specs, operands = [], []
    for piece in (0, 1):
        for other in (1, 0):
            for at in range(piece * cuts, (piece + 1) * cuts):
                specs += [spec(piece, other, at), spec(piece, other, 0 if len(got) > 1 else at)]
                operands += [keep, got[at] if len(got) > 1 else got[0]]
    out = jax.ShapeDtypeStruct((half, n, rows // 2, columns), keep.dtype)
    return pl.pallas_call(
        functools.partial(combine_kernel, cuts),
        grid_spec=pltpu.PrefetchScalarGridSpec(
            num_scalar_prefetch=1,
            grid=(half,),
            in_specs=specs,
            out_specs=[pl.BlockSpec((1, n, rows // 2, columns), lambda i, b: (i, 0, 0, 0))] * 4,
        ),
        out_shape=[out] * 4,
        compiler_params=pltpu.CompilerParams(vmem_limit_bytes=VMEM),
        cost_estimate=pl.CostEstimate(
            flops=keep.size, bytes_accessed=12 * keep.size, transcendentals=0
        ),
    )(bits, *operands)


def add_rows_kernel(rows, parts, core, *refs):
    ids, values, keep, sends = refs[:parts], refs[parts : 2 * parts], refs[2 * parts], refs[2 * parts + 1 :]
    table = pl.program_id(0)
    numbers = jnp.concatenate([r[pl.ds(table, 1)] for r in ids], axis=1).astype(jnp.int32)
    owners, at = lax.div(numbers, rows), lax.rem(numbers, rows)
    values = jnp.concatenate([r[...].astype(jnp.bfloat16) for r in values], axis=1)
    onehot = ones_where(iota((rows, numbers.shape[1]), 0) == at)
    for which, outs in ((1 - core[0], sends), (core[0], [keep])):
        for b in range(keep.shape[0]):
            sums = mm(values * ones_where(owners == 2 * b + which), onehot, NT)
            size = D // len(outs)
            for i, out in enumerate(outs):
                out[b, 0] = sums[size * i : size * (i + 1)]


def add_rows(core, values, tables, blocks, rows):
    samples = values[0].shape[1]
    parts = len(values)
    out = jax.ShapeDtypeStruct((blocks // 2, tables, D, rows), jnp.float32)
    piece = jax.ShapeDtypeStruct((blocks // 2, tables, D // SENDS, rows), jnp.float32)
    return pl.pallas_call(
        functools.partial(add_rows_kernel, rows, parts),
        grid_spec=pltpu.PrefetchScalarGridSpec(
            num_scalar_prefetch=1,
            grid=(tables,),
            in_specs=[
                pl.BlockSpec((ID_ROWS, samples), lambda t, c: (tables * D // ID_ROWS, 0))
            ]
            * parts
            + [pl.BlockSpec((D, samples), lambda t, c: (t, 0))] * parts,
            out_specs=[pl.BlockSpec((blocks // 2, 1, D, rows), lambda t, c: (0, t, 0, 0))]
            + [pl.BlockSpec((blocks // 2, 1, D // SENDS, rows), lambda t, c: (0, t, 0, 0))] * SENDS,
        ),
        out_shape=[out] + [piece] * SENDS,
        compiler_params=pltpu.CompilerParams(vmem_limit_bytes=VMEM),
        cost_estimate=pl.CostEstimate(
            flops=DENSE_COST, bytes_accessed=1, transcendentals=0
        ),
    )(core, *values, *values)


def local(
    embeddings,
    upstream,
    factor_machine_projection,
    w_first,
    w_second,
    compress,
    norm_gain,
    hot_index,
    cold_row,
    cold_owner,
):
    wide, narrow = lax.axis_size("wide"), lax.axis_size("narrow")
    devices = wide * narrow
    wide_bits = [("wide", b) for b in range(bits_of("wide"))]
    narrow_bits = [("narrow", b) for b in range(bits_of("narrow"))]
    core_bit, links = wide_bits[0], wide_bits[1:]
    left_dims = links[::-1] + narrow_bits[::-1]

    sample_count = embeddings.shape[0]
    here = lax.axis_index("narrow")
    x = jnp.transpose(embeddings, (1, 2, 0))
    up = jnp.transpose(upstream, (1, 2, 0))
    core = my_bit("wide", 0).reshape(1)
    mlp_keep, mlp_send, xs, inner, d_pair, d_lc, gain_sum = mlp(
        core,
        x,
        up,
        factor_machine_projection,
        w_first,
        w_second,
        compress,
        norm_gain.reshape(1, D),
        wide,
        narrow,
    )
    cold_ids = (cold_owner[:, :, 0] * COLD_ROWS_DEV + cold_row).T.astype(jnp.float32)

    def rows_of(part, d_pair):
        *values, hot_sums, sums = row_gradients(
            here.reshape(1),
            xs,
            inner,
            d_pair,
            d_lc,
            factor_machine_projection,
            compress,
            hot_index.T,
            cold_ids,
            narrow,
            part,
            2,
        )
        return values, hot_sums, sums

    share = COLD_TABLES // narrow
    low, high = narrow_bits
    link_bits = jnp.stack([my_bit(*links[0]), my_bit(*links[-1])])

    def go_round(value, step):
        return lax.ppermute(value, "narrow", [(i, (i + step) % narrow) for i in range(narrow)])

    def halve(part, label):
        (part,) = finish(start([part], [label]), [label])
        return part

    def first_cuts(keep, got):
        a_send, a_keep, b_send, b_keep = combine(link_bits, keep, got)
        dims = links[::-1]
        return [
            (a_send, a_keep, dims[:-1]),
            (b_send, b_keep, dims[1:]),
        ]

    def unfold(parts, tail):
        return [(value.reshape([2] * len(dims) + tail), dims) for value, dims in parts]

    early, hot_early, sums_early = rows_of(0, d_pair)
    got_early = [go_round(value, step) for step, value in enumerate(early) if step]
    (mlp_got,) = gate([flip(mlp_send, *core_bit)], early[:1])
    chunk = mlp_keep.shape[2]
    cuts = first_cuts(mlp_keep, [mlp_got])
    (d_pair_late,) = gate([d_pair], [cuts[0][0]])
    late, hot_late, sums_late = rows_of(1, d_pair_late)

    sums = sums_early + sums_late
    grad_proj, compress_gradient = sums[:RANK].T, sums[RANK:]
    hot_local = hot_early + hot_late
    hot_rows = hot_local.size // LANES
    small = jnp.concatenate([grad_proj.reshape(-1), compress_gradient.reshape(-1), gain_sum[:, 0]])
    small = jnp.pad(small, (0, -small.size % LANES)).reshape(-1, LANES)
    shared = jnp.concatenate([hot_local.reshape(hot_rows, LANES), small], axis=0)
    shared = jnp.pad(shared, ((0, -shared.shape[0] % (8 * devices)), (0, 0)))
    hot_order = [core_bit] + links + [low]
    hot = (shared.reshape([2] * len(hot_order) + [-1, LANES]), hot_order)

    late_sends = gate(late[1:], got_early)
    got_late = [go_round(value, step + 1) for step, value in enumerate(late_sends)]
    got_values = early[:1] + got_early + late[:1] + got_late
    mlp_parts = unfold(
        finish(cuts, [links[0], links[-1]]), [2] * len(narrow_bits) + [chunk // 2, COLUMNS]
    )
    mlp_parts = [(value, dims + narrow_bits[::-1]) for value, dims in mlp_parts]
    for turn in range(1, len(links)):
        labels = [links[turn], links[-1 - turn]]
        cuts = start(mlp_parts, labels)
        if turn == len(links) - 1:
            (hot_cut,) = start([hot], [core_bit])
            sends = gate([cut[0] for cut in cuts] + [hot_cut[0]], late_sends)
            cuts = [(send, cut[1], cut[2]) for send, cut in zip(sends, cuts)]
            (hot,) = finish([(sends[2], hot_cut[1], hot_cut[2])], [core_bit])
        mlp_parts = finish(cuts, labels)

    cold_keep, *cold_sends = add_rows(core, got_values, share, wide, COLD_ROWS_DEV)
    labels = [low, links[0]]
    both = start(mlp_parts, [low, low])
    mlp_dims = both[0][2]
    mlp_cut = [jnp.concatenate([cut[i] for cut in both], axis=len(mlp_dims)) for i in range(2)]
    ready = [(*mlp_cut, mlp_dims)] + start([hot], labels[1:])
    sends = gate(cold_sends + [cut[0] for cut in ready])
    cold_sends = sends[:SENDS]
    ready = [(send, cut[1], cut[2]) for send, cut in zip(sends[SENDS:], ready)]
    mlp_part, hot = finish(ready, labels)
    for label in links[1:]:
        hot = halve(hot, label)
    cuts = first_cuts(cold_keep, [flip(send, *core_bit) for send in cold_sends])
    half = D // 2
    parts = []
    for turn in range(len(links)):
        labels = [links[turn], links[-1 - turn]]
        last = turn == len(links) - 1
        if turn == 0:
            labels = labels + [low]
            ready = ordered(cuts + start([hot], labels[2:]))
            *parts, hot = finish(ready, labels)
            parts = unfold(parts, [share, half, COLD_ROWS_DEV])
            ready = ordered(start([mlp_part], [high]), [cut[0] for cut in ready])
            (mlp_part,) = finish(ready, [high])
        elif last:
            ready = start(parts, labels)
            *sends, hot_value = gate([cut[0] for cut in ready] + [hot[0]])
            ready = [(send, cut[1], cut[2]) for send, cut in zip(sends, ready)]
            hot_value = hot_value + flip(hot_value, *high)
            parts = finish(ready, labels)
        else:
            parts = finish(ordered(start(parts, labels)), labels)

    cold_grad = jnp.zeros((narrow, share, D, COLD_ROWS_DEV), jnp.float32)
    moving = jnp.concatenate([parts[0][0], parts[1][0]], axis=1)
    joins = [[low], links[-1:]] + [[]] * (narrow - 4) + [links[-2::-1]]
    for step in range(narrow):
        cold_grad = lax.dynamic_update_index_in_dim(cold_grad, moving, (here - step) % narrow, 0)
        if step == narrow - 1:
            break
        after = [] if step else [mlp_part[0]]
        moving, hot_value = gate([moving, hot_value], after)
        moving = go_round(moving, 1)
        for label in joins[step]:
            hot_value = join(hot_value, label)
    (hot_value,) = gate([hot_value], [moving])
    shared = join(hot_value, core_bit).reshape(-1, LANES)
    cold_grad = jnp.transpose(
        cold_grad.reshape(COLD_TABLES, D, COLD_ROWS_DEV), (0, 2, 1)
    )
    hot_grad = jnp.transpose(shared[:hot_rows].reshape(HOT_TABLES, D, HOT_ROWS), (0, 2, 1))
    small = shared[hot_rows:].reshape(-1)
    n_proj, n_compress = TABLES * RANK, LC_OUT * TABLES
    grad_proj = small[:n_proj].reshape(TABLES, RANK)
    compress_gradient = small[n_proj : n_proj + n_compress].reshape(LC_OUT, TABLES)
    grad_gain = small[n_proj + n_compress : n_proj + n_compress + D]

    done = mlp_part[0]
    own_second, own_first = w_first.shape[1] // devices, TABLES * RANK // devices
    cut = own_second * FM_OUT * D // COLUMNS

    def side_by_side(blocks, rows):
        return jnp.transpose(blocks.reshape(-1, rows, COLUMNS), (1, 0, 2)).reshape(rows, -1)

    grad_second = side_by_side(done[:cut], own_second)
    grad_first = side_by_side(done[cut:], own_first)
    return (grad_first, grad_second, grad_proj, compress_gradient, grad_gain, hot_grad, cold_grad)


def solution(mesh):
    placed = (
        P(("wide", "narrow"), None, None),
        P(("wide", "narrow"), None, None),
        P(),
        P(),
        P(),
        P(),
        P(),
        P(("wide", "narrow"), None),
        P(("wide", "narrow"), None),
        P(("wide", "narrow"), None, None),
    )
    return jax.shard_map(
        local,
        mesh=mesh,
        in_specs=placed,
        out_specs=(
            P(("wide", "narrow"), None),
            P(("wide", "narrow"), None),
            P(),
            P(),
            P(),
            P(),
            P(None, "wide", None),
        ),
        check_vma=False,
    )
```
